128 devices in a mesh: row: 8 (over x_lo, z), col: 16 (over y, x_hi, core).
Axes of the slice: x: 4 (x_hi: 2, x_lo: 2; x = x_hi * 2 + x_lo), y: 4, z: 4, core: 2. Of those that a mesh axis runs over, the one named last changes fastest.
Arguments:
- tokens: bfloat16 [1024, 8192], P('col', 'row'), may hold values from -6 to 6
- out_grad: bfloat16 [1024, 8192], P('col', 'row'), may hold values from -6 to 6
- gate_weight: bfloat16 [8192, 14336], P('row', 'col'), may hold values from -0.09375 to 0.09375
- up_weight: bfloat16 [8192, 14336], P('row', 'col'), may hold values from -0.09375 to 0.09375
- down_weight: bfloat16 [14336, 8192], P('col', 'row'), may hold values from -0.0625 to 0.0625
- gate_mask: int32 [64, 112], P('row', 'col'), may hold values 0 or 1
- up_mask: int32 [64, 112], P('row', 'col'), may hold values 0 or 1
- down_mask: int32 [112, 64], P('col', 'row'), may hold values 0 or 1
Outputs:
- output: bfloat16 [1024, 8192], P('col', 'row')
- token_grad: bfloat16 [1024, 8192], P('col', 'row')
- gate_grad: bfloat16 [8192, 14336], P('row', 'col')
- up_grad: bfloat16 [8192, 14336], P('row', 'col')
- down_grad: bfloat16 [14336, 8192], P('col', 'row')
The draws below stay inside these ranges and needn't reach their ends.
All inputs are finite; a program needn't handle non-finite values. No bound on the sum of `gate_mask` or of `up_mask` or of `down_mask` on one device may be relied on, other than what follows from the above.
Results may differ from the reference program's by a relative error of at most 0.03.
Values may be sent and summed in bfloat16 or wider, within the bound.
No kernel may reach another device: no remote copies, remote signals or barrier semaphores. Data moves between devices by JAX's collectives and lax.ppermute only.
A program may use at most 128 MiB of HBM per device.

```python
import jax
import jax.numpy as jnp
from jax import lax

D = 8192
FF = 14336
BLK = 128
TOKENS = 1024
N_ROW = 8


def with_ends(drawn, rng, smallest, high):
    index_at = [jax.random.randint(jax.random.fold_in(rng, axis), (), 0, length) for axis, length in enumerate(drawn.shape)]
    main_axis = drawn.shape.index(max(drawn.shape))
    next_to = index_at[:main_axis] + [(index_at[main_axis] + 1) % drawn.shape[main_axis]] + index_at[main_axis + 1:]
    return drawn.at[tuple(index_at)].set(smallest).at[tuple(next_to)].set(high)


def block_scale(stream_key, extent, cuts, low, high):
    factor_of = 1.0
    for position, blocks in cuts:
        draws = jax.random.uniform(jax.random.fold_in(jax.random.fold_in(stream_key, 6), position), (blocks,), jnp.float32, low / len(cuts), high / len(cuts))
        factor_of = factor_of * jnp.repeat(jnp.exp(draws), extent[position] // blocks).reshape((-1,) + (1,) * (len(extent) - 1 - position))
    return factor_of


def noise(key, extent, scale, bound, pieces=(), dtype=jnp.bfloat16):
    loudness = block_scale(key, extent, pieces, -0.22, 0.18) if pieces else 1.0
    result = jax.random.normal(key, extent, jnp.float32) * scale * loudness
    return jnp.minimum(jnp.maximum(result, -bound), bound).astype(dtype)


def setup_inputs(seed: int = 0) -> dict:
    arg_keys = jax.random.split(jax.random.key(seed), 9)
    tokens = noise(arg_keys[0], (TOKENS, D), 1.0, 6.0, ((0, 16), (1, 8)))
    out_grad = noise(arg_keys[1], (TOKENS, D), 1.0, 6.0, ((0, 16), (1, 8)))
    gate_weight = noise(arg_keys[2], (D, FF), (D // 2) ** -0.5, 0.09375, ((0, 8), (1, 16)))
    up_weight = noise(arg_keys[3], (D, FF), (D // 2) ** -0.5, 0.09375, ((0, 8), (1, 16)))
    down_weight = noise(arg_keys[4], (FF, D), (FF // 2) ** -0.5, 0.0625, ((0, 16), (1, 8)))
    gate_mask = with_ends((jax.random.randint(arg_keys[5], (D // BLK, FF // BLK), 0, 2) < 1).astype(jnp.int32), jax.random.fold_in(arg_keys[5], 1), 0, 1)
    up_mask = with_ends((jax.random.randint(arg_keys[6], (D // BLK, FF // BLK), 0, 2) < 1).astype(jnp.int32), jax.random.fold_in(arg_keys[6], 1), 0, 1)
    down_mask = with_ends((jax.random.randint(arg_keys[7], (FF // BLK, D // BLK), 0, 2) < 1).astype(jnp.int32), jax.random.fold_in(arg_keys[7], 1), 0, 1)
    return {"tokens": tokens, "out_grad": out_grad, "gate_weight": gate_weight, "up_weight": up_weight, "down_weight": down_weight, "gate_mask": gate_mask, "up_mask": up_mask, "down_mask": down_mask}


def widen(weight, keep_blocks):
    block_rows, block_cols = keep_blocks.shape
    block_size = weight.shape[0] // block_rows
    spread = jnp.broadcast_to(keep_blocks[:, None, :, None], (block_rows, block_size, block_cols, block_size))
    return weight * spread.reshape(weight.shape).astype(jnp.bfloat16)


def reference(tokens, out_grad, gate_weight, up_weight, down_weight, gate_mask, up_mask, down_mask):
    gate_masked = widen(gate_weight, gate_mask)
    up_masked = widen(up_weight, up_mask)
    down_masked = widen(down_weight, down_mask)
    piece = D // N_ROW
    hidden_width = gate_masked.shape[1]
    totals = jnp.zeros((tokens.shape[0], 3 * hidden_width), jnp.float32)
    for block_index in range(N_ROW):
        first = block_index * piece
        rows_x = tokens[:, first:first + piece]
        rows_g = out_grad[:, first:first + piece]
        term = jnp.concatenate([
            jnp.dot(rows_x, gate_masked[first:first + piece], preferred_element_type=jnp.float32),
            jnp.dot(rows_x, up_masked[first:first + piece], preferred_element_type=jnp.float32),
            jnp.dot(rows_g, down_masked[:, first:first + piece].T, preferred_element_type=jnp.float32)], axis=1)
        rounded = lax.optimization_barrier(term.astype(jnp.bfloat16))
        totals = totals + rounded.astype(jnp.float32)
    gate = totals[:, :hidden_width]
    up_part = totals[:, hidden_width:2 * hidden_width]
    hidden_grad = totals[:, 2 * hidden_width:]
    sigmoid_gate = jax.nn.sigmoid(gate)
    activated = gate * sigmoid_gate
    hidden = (activated * up_part).astype(jnp.bfloat16)
    gate_delta = (hidden_grad * up_part * sigmoid_gate * (1.0 + gate * (1.0 - sigmoid_gate))).astype(jnp.bfloat16)
    up_delta = (hidden_grad * activated).astype(jnp.bfloat16)
    output = jnp.dot(hidden, down_masked, preferred_element_type=jnp.float32).astype(jnp.bfloat16)
    token_grad = (jnp.dot(gate_delta, gate_masked.T, preferred_element_type=jnp.float32)
                  + jnp.dot(up_delta, up_masked.T, preferred_element_type=jnp.float32)).astype(jnp.bfloat16)
    down_grad = widen(jnp.dot(hidden.T, out_grad, preferred_element_type=jnp.float32).astype(jnp.bfloat16), down_mask)
    gate_grad = widen(jnp.dot(tokens.T, gate_delta, preferred_element_type=jnp.float32).astype(jnp.bfloat16), gate_mask)
    up_grad = widen(jnp.dot(tokens.T, up_delta, preferred_element_type=jnp.float32).astype(jnp.bfloat16), up_mask)
    return (output, token_grad, gate_grad, up_grad, down_grad)
```

```python
import functools

import jax
import jax.numpy as jnp
from jax import lax
from jax.experimental import pallas as pl
from jax.experimental.pallas import tpu as pltpu
from jax.sharding import PartitionSpec as P

BLK = 128
CHUNKS = (32, 32)
PEERS = tuple((dy, dx) for dy in range(4) for dx in range(2))
SEND_UP = ((2, 0, 0), (2, 0, 1), (1, 1, 0), (1, 1, 1))
SEND_DOWN = ((2, 1, 0), (2, 1, 1), (3, 0, 0), (3, 0, 1))
NEXT_UP = ((1, 0, 0), (1, 0, 1))
NEXT_DOWN = ((3, 1, 0), (3, 1, 1))
OWN = ((0, 0, 0), (0, 0, 1), (0, 1, 0), (0, 1, 1))
GATHERED = tuple((dz, half, dx) for dz in (0, 1, 3, 2) for half in range(2) for dx in range(2))
VMEM_LIMIT = 56 * 1024 * 1024


def move(array, dy=0, dxh=0, dcore=0, dxl=0, dz=0):
    pairs = []
    for device in range(128):
        row, col = divmod(device, 16)
        x_lo, z = divmod(row, 4)
        y, x_hi, core = col // 4, col // 2 % 2, col % 2
        to_row = (x_lo + dxl) % 2 * 4 + (z + dz) % 4
        to_col = ((y + dy) % 4 * 2 + (x_hi + dxh) % 2) * 2 + (core + dcore) % 2
        pairs.append((device, to_row * 16 + to_col))
    return lax.ppermute(array, ("row", "col"), pairs)


def slot(piece):
    row = lax.axis_index("row")
    dz, _, dx = piece
    return lax.rem(lax.rem(row, 4) + dz, 4) * 2 + lax.rem(row // 4 + dx, 2)


def nn(left, right):
    return lax.dot_general(
        left, right, (((1,), (0,)), ((), ())), preferred_element_type=jnp.float32
    )


def nt(left, right):
    return lax.dot_general(
        left, right, (((1,), (1,)), ((), ())), preferred_element_type=jnp.float32
    )


def tn(left, right):
    return lax.dot_general(
        left, right, (((0,), (0,)), ((), ())), preferred_element_type=jnp.float32
    )


def params():
    return pltpu.CompilerParams(vmem_limit_bytes=VMEM_LIMIT)


VMEM = pl.BlockSpec(memory_space=pltpu.VMEM)
ANY = pl.BlockSpec(memory_space=pl.ANY)
SMEM = pl.BlockSpec(memory_space=pltpu.SMEM)


def mask_kernel(gate, up, down, gate_mask, up_mask, down_mask, both, down_out):
    rows, width = gate.shape

    def keep(weight, mask, i, j, out, column):
        rows_at = pl.ds(i * BLK, BLK)
        block = weight[rows_at, j * BLK : (j + 1) * BLK]
        out[rows_at, column : column + BLK] = block * mask[i, j].astype(jnp.bfloat16)

    def gate_up(i, carry):
        for j in range(width // BLK):
            keep(gate, gate_mask, i, j, both, j * BLK)
            keep(up, up_mask, i, j, both, width + j * BLK)
        return carry

    def down_rows(i, carry):
        for j in range(rows // BLK):
            keep(down, down_mask, i, j, down_out, j * BLK)
        return carry

    lax.fori_loop(0, rows // BLK, gate_up, 0)
    lax.fori_loop(0, width // BLK, down_rows, 0)


def mask_weights(gate, up, down, gate_mask, up_mask, down_mask):
    rows, width = gate.shape
    return pl.pallas_call(
        mask_kernel,
        in_specs=[VMEM] * 3 + [SMEM] * 3,
        out_specs=[VMEM] * 2,
        out_shape=[
            jax.ShapeDtypeStruct((rows, 2 * width), jnp.bfloat16),
            jax.ShapeDtypeStruct((width, rows), jnp.bfloat16),
        ],
        compiler_params=params(),
        name="mask_weights",
    )(gate, up, down, gate_mask, up_mask, down_mask)


def tiles(size, step=256):
    return [(at, min(step, size - at)) for at in range(0, size, step)]


def forward_kernel(groups, own, other, both, down, *rest):
    outs, (held, sems) = rest[: len(groups)], rest[len(groups) :]
    pieces = [piece for group in groups for piece in group]
    copies = []
    for at, piece in enumerate(pieces):
        source = (own, other)[piece[1]]
        copy = pltpu.make_async_copy(source.at[slot(piece)], held.at[at], sems.at[at])
        copy.start()
        copies.append(copy)
    for copy in copies:
        copy.wait()
    count, _, rows, depth = held.shape
    tokens = held[:, 0].reshape(count * rows, depth)
    grads = held[:, 1].reshape(count * rows, depth)

    def put(part, column):
        width = part.shape[1]
        part = part.astype(jnp.bfloat16).reshape(count, rows, width)
        at = 0
        for out, group in zip(outs, groups):
            out[:, :, column : column + width] = part[at : at + len(group)]
            at += len(group)

    for column, width in tiles(both.shape[1]):
        put(nn(tokens, both[:, column : column + width]), column)
    for column, width in tiles(down.shape[0]):
        put(nt(grads, down[column : column + width, :]), both.shape[1] + column)


def forward(groups, own, other, both, down):
    rows, depth = own.shape[2:]
    count = sum(len(group) for group in groups)
    total = both.shape[1] + down.shape[0]
    flops = 2 * count * rows * depth * total
    return pl.pallas_call(
        functools.partial(forward_kernel, groups),
        in_specs=[ANY, ANY, VMEM, VMEM],
        out_specs=[VMEM] * len(groups),
        out_shape=[
            jax.ShapeDtypeStruct((len(group), rows, total), jnp.bfloat16) for group in groups
        ],
        scratch_shapes=[
            pltpu.VMEM((count, 2, rows, depth), jnp.bfloat16),
            pltpu.SemaphoreType.DMA((count,)),
        ],
        compiler_params=params(),
        cost_estimate=pl.CostEstimate(
            flops=flops, bytes_accessed=8 * 1024 * 1024, transcendentals=0
        ),
        name="forward",
    )(own, other, both, down)


def gathered_at(piece, arrays):
    own, up, down, far_first, far_second = arrays
    dz, half, dx = piece
    if dz == 2:
        return (far_first, far_second)[half], dx
    return {0: own, 1: up, 3: down}[dz], half * 2 + dx


def backward_kernel(half, *refs):
    arrays, (both, down, out, held, sems) = refs[:5], refs[5:]
    copies = []
    for at, piece in enumerate([piece for piece in GATHERED if piece[1] == half]):
        source, index = gathered_at(piece, arrays)
        copy = pltpu.make_async_copy(source.at[index], held.at[slot(piece)], sems.at[at])
        copy.start()
        copies.append(copy)
    for copy in copies:
        copy.wait()
    count, rows, total = held.shape
    width, depth = down.shape
    hidden = held[:, :, :width].reshape(count * rows, width)
    deltas = held[:, :, width:].reshape(count * rows, total - width)
    for column, size in tiles(depth):
        part = nn(hidden, down[:, column : column + size])
        out[:, :, column : column + size] = part.astype(jnp.bfloat16).reshape(count, rows, size)
    for column, size in tiles(depth):
        part = nt(deltas, both[column : column + size, :])
        at = depth + column
        out[:, :, at : at + size] = part.astype(jnp.bfloat16).reshape(count, rows, size)


def backward(half, arrays, both, down):
    rows, total = arrays[0].shape[1:]
    depth = down.shape[1]
    flops = 2 * 8 * rows * depth * total
    return pl.pallas_call(
        functools.partial(backward_kernel, half),
        in_specs=[ANY] * 5 + [VMEM, VMEM],
        out_specs=VMEM,
        out_shape=jax.ShapeDtypeStruct((8, rows, 2 * depth), jnp.bfloat16),
        scratch_shapes=[
            pltpu.VMEM((8, rows, total), jnp.bfloat16),
            pltpu.SemaphoreType.DMA((8,)),
        ],
        compiler_params=params(),
        cost_estimate=pl.CostEstimate(
            flops=flops, bytes_accessed=8 * 1024 * 1024, transcendentals=0
        ),
        name="backward",
    )(*arrays, both, down)


def weight_grad_kernel(chunks, *refs):
    inputs = refs[: 7 * len(chunks)]
    gate_mask, up_mask, down_mask, gate_grad, up_grad, down_grad = refs[7 * len(chunks) :][:6]
    tokens, grads, values, sems = refs[7 * len(chunks) + 6 :]
    copies = []
    first = 0
    for which, rows in enumerate(chunks):
        own, other, *arrays = inputs[7 * which : 7 * which + 7]
        for at, piece in enumerate(GATHERED):
            rows_at = pl.ds(first + at * rows, rows)
            source = (own, other)[piece[1]].at[slot(piece)]
            held, index = gathered_at(piece, arrays)
            for kind, (start, end) in enumerate(
                (
                    (source.at[0], tokens.at[rows_at]),
                    (source.at[1], grads.at[rows_at]),
                    (held.at[index], values.at[rows_at]),
                )
            ):
                copy = pltpu.make_async_copy(start, end, sems.at[which, kind, at])
                copy.start()
                copies.append(copy)
        first += 16 * rows
    for copy in copies:
        copy.wait()
    width, depth = down_grad.shape

    def store(part, mask, row, out):
        for j in range(part.shape[1] // BLK):
            for i in range(part.shape[0] // BLK):
                block = part[i * BLK : (i + 1) * BLK, j * BLK : (j + 1) * BLK]
                keep = mask[row // BLK + i, j].astype(jnp.bfloat16)
                out[row + i * BLK : row + (i + 1) * BLK, j * BLK : (j + 1) * BLK] = (
                    block.astype(jnp.bfloat16) * keep
                )

    for row, size in tiles(depth):
        left = tokens[:, row : row + size]
        store(tn(left, values[:, width : 2 * width]), gate_mask, row, gate_grad)
        store(tn(left, values[:, 2 * width :]), up_mask, row, up_grad)
    for row, size in tiles(width):
        store(tn(values[:, row : row + size], grads[...]), down_mask, row, down_grad)


def weight_grads(chunks, inputs, gate_mask, up_mask, down_mask):
    depth = inputs[0].shape[-1]
    total = inputs[2].shape[-1]
    width = total // 3
    count = 16 * sum(chunks)
    return pl.pallas_call(
        functools.partial(weight_grad_kernel, chunks),
        in_specs=[ANY] * len(inputs) + [SMEM] * 3,
        out_specs=[VMEM] * 3,
        out_shape=[
            jax.ShapeDtypeStruct((depth, width), jnp.bfloat16),
            jax.ShapeDtypeStruct((depth, width), jnp.bfloat16),
            jax.ShapeDtypeStruct((width, depth), jnp.bfloat16),
        ],
        scratch_shapes=[
            pltpu.VMEM((count, depth), jnp.bfloat16),
            pltpu.VMEM((count, depth), jnp.bfloat16),
            pltpu.VMEM((count, total), jnp.bfloat16),
            pltpu.SemaphoreType.DMA((len(chunks), 3, 16)),
        ],
        compiler_params=params(),
        cost_estimate=pl.CostEstimate(
            flops=2 * count * depth * total, bytes_accessed=15 * 1024 * 1024, transcendentals=0
        ),
        name="weight_grads",
    )(*inputs, gate_mask, up_mask, down_mask)


def wide(array):
    return array.astype(jnp.float32)


def elementwise(totals):
    width = totals.shape[-1] // 3
    gate = totals[..., :width]
    up_part = totals[..., width : 2 * width]
    hidden_grad = totals[..., 2 * width :]
    sigmoid_gate = jax.nn.sigmoid(gate)
    activated = gate * sigmoid_gate
    hidden = activated * up_part
    gate_delta = hidden_grad * up_part * sigmoid_gate * (1.0 + gate * (1.0 - sigmoid_gate))
    up_delta = hidden_grad * activated
    return jnp.concatenate([hidden, gate_delta, up_delta], axis=-1).astype(jnp.bfloat16)


def col_gather(part):
    pieces = [part] + [move(part, dy=-dy, dxh=dx) for dy, dx in PEERS[1:]]
    own = jnp.stack(pieces)
    return own, move(own, dcore=1)


def row_sum(own, other, both, down):
    send_up, send_down = forward((SEND_UP, SEND_DOWN), own, other, both, down)
    from_down = move(send_up, dz=1)
    from_up = move(send_down, dz=-1)
    next_up, next_down, kept = forward((NEXT_UP, NEXT_DOWN, OWN), own, other, both, down)
    late_down = move(next_up + from_down[:2], dz=1)
    late_up = move(next_down + from_up[:2], dz=-1)
    sums = jnp.concatenate(
        [
            wide(kept[:2]) + wide(late_down) + wide(from_up[2:]),
            wide(kept[2:]) + wide(late_up) + wide(from_down[2:]),
        ]
    ).astype(jnp.bfloat16)
    partner = move(sums, dxl=1)
    swapped = jnp.concatenate([partner[1:2], partner[0:1], partner[3:4], partner[2:3]])
    return wide(sums) + wide(swapped)


def row_gather(values):
    from_down = move(values, dz=1)
    from_up = move(values, dz=-1)
    far_first = move(from_down[:2], dz=1)
    far_second = move(from_up[2:], dz=-1)
    return (values, from_up, from_down, far_first, far_second)


def col_sum(arrays, both, down):
    for_other = backward(1, arrays, both, down)
    received = move(for_other, dcore=1)
    for_own = backward(0, arrays, both, down)
    chip = (wide(for_own) + wide(received)).astype(jnp.bfloat16)
    total = wide(chip[0])
    for at, (dy, dx) in enumerate(PEERS[1:], 1):
        total = total + wide(move(chip[at], dy=dy, dxh=dx))
    return total.astype(jnp.bfloat16)


def shards(tokens, out_grad, gate_weight, up_weight, down_weight, gate_mask, up_mask, down_mask):
    depth = tokens.shape[1]
    starts = [sum(CHUNKS[:i]) for i in range(len(CHUNKS))]
    gathered = [
        col_gather(jnp.stack([tokens[at : at + rows], out_grad[at : at + rows]]))
        for at, rows in zip(starts, CHUNKS)
    ]
    both, down = mask_weights(gate_weight, up_weight, down_weight, gate_mask, up_mask, down_mask)
    values = [row_gather(elementwise(row_sum(*pair, both, down))) for pair in gathered]
    results = [col_sum(arrays, both, down) for arrays in values]
    inputs = [item for pair, arrays in zip(gathered, values) for item in (*pair, *arrays)]
    gate_grad, up_grad, down_grad = weight_grads(CHUNKS, inputs, gate_mask, up_mask, down_mask)
    result = jnp.concatenate(results)
    return (result[:, :depth], result[:, depth:], gate_grad, up_grad, down_grad)


def solution(mesh):
    in_specs = (
        P("col", "row"),
        P("col", "row"),
        P("row", "col"),
        P("row", "col"),
        P("col", "row"),
        P("row", "col"),
        P("row", "col"),
        P("col", "row"),
    )
    out_specs = (
        P("col", "row"),
        P("col", "row"),
        P("row", "col"),
        P("row", "col"),
        P("col", "row"),
    )
    return jax.shard_map(shards, mesh=mesh, in_specs=in_specs, out_specs=out_specs, check_vma=False)
```

```python
import functools

import jax
import jax.numpy as jnp
from jax import lax
from jax.experimental import pallas as pl
from jax.experimental.pallas import tpu as pltpu
from jax.sharding import PartitionSpec as P

BLK = 128
CHUNKS = (32, 32)
PEERS = tuple((dy, dx) for dy in range(4) for dx in range(2))
SEND_UP = ((2, 0, 0), (2, 0, 1), (1, 1, 0), (1, 1, 1))
SEND_DOWN = ((2, 1, 0), (2, 1, 1), (3, 0, 0), (3, 0, 1))
NEXT_UP = ((1, 0, 0), (1, 0, 1))
NEXT_DOWN = ((3, 1, 0), (3, 1, 1))
OWN = ((0, 0, 0), (0, 0, 1), (0, 1, 0), (0, 1, 1))
GROUPS = (SEND_UP, SEND_DOWN, NEXT_UP, NEXT_DOWN, OWN)
GATHERED = tuple((dz, half, dx) for dz in (0, 1, 3, 2) for half in range(2) for dx in range(2))
VMEM_LIMIT = 56 * 1024 * 1024


def move(array, dy=0, dxh=0, dcore=0, dxl=0, dz=0):
    pairs = []
    for device in range(128):
        row, col = divmod(device, 16)
        x_lo, z = divmod(row, 4)
        y, x_hi, core = col // 4, col // 2 % 2, col % 2
        to_row = (x_lo + dxl) % 2 * 4 + (z + dz) % 4
        to_col = ((y + dy) % 4 * 2 + (x_hi + dxh) % 2) * 2 + (core + dcore) % 2
        pairs.append((device, to_row * 16 + to_col))
    return lax.ppermute(array, ("row", "col"), pairs)


def slot(piece):
    row = lax.axis_index("row")
    dz, _, dx = piece
    return lax.rem(lax.rem(row, 4) + dz, 4) * 2 + lax.rem(row // 4 + dx, 2)


def nn(left, right):
    return lax.dot_general(
        left, right, (((1,), (0,)), ((), ())), preferred_element_type=jnp.float32
    )


def nt(left, right):
    return lax.dot_general(
        left, right, (((1,), (1,)), ((), ())), preferred_element_type=jnp.float32
    )


def tn(left, right):
    return lax.dot_general(
        left, right, (((0,), (0,)), ((), ())), preferred_element_type=jnp.float32
    )


def params():
    return pltpu.CompilerParams(vmem_limit_bytes=VMEM_LIMIT)


VMEM = pl.BlockSpec(memory_space=pltpu.VMEM)
ANY = pl.BlockSpec(memory_space=pl.ANY)
SMEM = pl.BlockSpec(memory_space=pltpu.SMEM)


def mask_kernel(gate, up, down, gate_mask, up_mask, down_mask, out):
    step = pl.program_id(0)
    width = gate.shape[1]
    down_t = down[...].T
    for j in range(width // BLK):
        at = pl.ds(j * BLK, BLK)
        out[:, at] = gate[:, at] * gate_mask[step, j].astype(jnp.bfloat16)
        to = pl.ds(width + j * BLK, BLK)
        out[:, to] = up[:, at] * up_mask[step, j].astype(jnp.bfloat16)
        to = pl.ds(2 * width + j * BLK, BLK)
        out[:, to] = down_t[:, j * BLK : (j + 1) * BLK] * down_mask[j, step].astype(jnp.bfloat16)


def mask_weights(gate, up, down, gate_mask, up_mask, down_mask):
    depth, width = gate.shape
    return pl.pallas_call(
        mask_kernel,
        grid=(depth // BLK,),
        in_specs=[
            pl.BlockSpec((BLK, width), lambda i: (i, 0)),
            pl.BlockSpec((BLK, width), lambda i: (i, 0)),
            pl.BlockSpec((width, BLK), lambda i: (0, i)),
            SMEM,
            SMEM,
            SMEM,
        ],
        out_specs=pl.BlockSpec((BLK, 3 * width), lambda i: (i, 0)),
        out_shape=jax.ShapeDtypeStruct((depth, 3 * width), jnp.bfloat16),
        compiler_params=params(),
        cost_estimate=pl.CostEstimate(
            flops=3 * depth * width, bytes_accessed=12 * depth * width, transcendentals=0
        ),
        name="mask_weights",
    )(gate, up, down, gate_mask, up_mask, down_mask)


def tiles(size, step=256):
    return [(at, min(step, size - at)) for at in range(0, size, step)]


def forward_kernel(groups, own, other, weights, *rest):
    outs = rest[: len(groups)]
    tokens, grads, sems = rest[len(groups) :]
    pieces = [piece for group in groups for piece in group]
    rows = own.shape[2]
    step = pl.program_id(0)
    copies = []
    for at, piece in enumerate(pieces):
        source = (own, other)[piece[1]].at[slot(piece)]
        to = pl.ds(at * rows, rows)
        for kind, target in enumerate((tokens, grads)):
            copy = pltpu.make_async_copy(source.at[kind], target.at[to], sems.at[at, kind])
            copies.append(copy)

    @pl.when(step == 0)
    def _():
        for copy in copies:
            copy.start()
        for copy in copies:
            copy.wait()

    def put(left):
        part = nn(left, weights[...]).astype(jnp.bfloat16)
        first = 0
        for out, group in zip(outs, groups):
            size = len(group) * rows
            out[...] = part[first : first + size]
            first += size

    @pl.when(step < 2)
    def _():
        put(tokens[...])

    @pl.when(step == 2)
    def _():
        put(grads[...])


def forward(groups, own, other, weights):
    rows, depth = own.shape[2:]
    count = sum(len(group) for group in groups)
    total = weights.shape[1]
    width = total // 3
    flops = 2 * count * rows * depth * total
    outs = pl.pallas_call(
        functools.partial(forward_kernel, groups),
        grid=(3,),
        in_specs=[ANY, ANY, pl.BlockSpec((depth, width), lambda j: (0, j))],
        out_specs=[pl.BlockSpec((len(group) * rows, width), lambda j: (0, j)) for group in groups],
        out_shape=[
            jax.ShapeDtypeStruct((len(group) * rows, total), jnp.bfloat16) for group in groups
        ],
        scratch_shapes=[
            pltpu.VMEM((count * rows, depth), jnp.bfloat16),
            pltpu.VMEM((count * rows, depth), jnp.bfloat16),
            pltpu.SemaphoreType.DMA((count, 2)),
        ],
        compiler_params=params(),
        cost_estimate=pl.CostEstimate(
            flops=flops, bytes_accessed=10 * 1024 * 1024, transcendentals=0
        ),
        name="forward",
    )(own, other, weights)
    return [out.reshape(len(group), rows, total) for out, group in zip(outs, groups)]


def gathered_at(piece, arrays):
    own, up, down, far_first, far_second = arrays
    dz, half, dx = piece
    if dz == 2:
        return (far_first, far_second)[half], dx
    return {0: own, 1: up, 3: down}[dz], half * 2 + dx


def backward_kernel(*refs):
    arrays, weights, outs = refs[:5], refs[5], refs[6:8]
    held, total_ref, sems = refs[8:]
    rows = arrays[0].shape[1]
    step = pl.program_id(0)
    copies = []
    for at, piece in enumerate(GATHERED):
        source, index = gathered_at(piece, arrays)
        to = pl.ds(pl.multiple_of(((1 - piece[1]) * 8 + slot(piece)) * rows, rows), rows)
        copies.append(pltpu.make_async_copy(source.at[index], held.at[to], sems.at[at]))

    @pl.when(step == 0)
    def _():
        for copy in copies:
            copy.start()
        for copy in copies:
            copy.wait()

    width = weights.shape[1]

    def term(at):
        return nt(held[:, at * width : (at + 1) * width], weights[...])

    def put(part):
        part = part.astype(jnp.bfloat16)
        half = part.shape[0] // 2
        outs[0][...] = part[:half]
        outs[1][...] = part[half:]

    @pl.when(step == 0)
    def _():
        put(term(2))

    @pl.when(step == 1)
    def _():
        total_ref[...] = term(0)

    @pl.when(step == 2)
    def _():
        put(total_ref[...] + term(1))


def backward(arrays, weights):
    rows, total = arrays[0].shape[1:]
    depth = weights.shape[0]
    flops = 2 * 16 * rows * depth * total
    outs = pl.pallas_call(
        backward_kernel,
        grid=(3,),
        in_specs=[ANY] * 5
        + [pl.BlockSpec((depth, total // 3), lambda j: (0, lax.rem(j + 2, 3)))],
        out_specs=[pl.BlockSpec((8 * rows, depth), lambda j: (0, (j + 1) // 2))] * 2,
        out_shape=[jax.ShapeDtypeStruct((8 * rows, 2 * depth), jnp.bfloat16)] * 2,
        scratch_shapes=[
            pltpu.VMEM((16 * rows, total), jnp.bfloat16),
            pltpu.VMEM((16 * rows, depth), jnp.float32),
            pltpu.SemaphoreType.DMA((16,)),
        ],
        compiler_params=params(),
        cost_estimate=pl.CostEstimate(
            flops=flops, bytes_accessed=10 * 1024 * 1024, transcendentals=0
        ),
        name="backward",
    )(*arrays, weights)
    return [out.reshape(8, rows, 2 * depth) for out in outs]


def weight_grad_kernel(chunks, *refs):
    inputs = refs[: 7 * len(chunks)]
    gate_mask, up_mask, down_mask, gate_grad, up_grad, down_grad = refs[7 * len(chunks) :][:6]
    tokens, grads, values, sems = refs[7 * len(chunks) + 6 :]
    copies = []
    first = 0
    for which, rows in enumerate(chunks):
        own, other, *arrays = inputs[7 * which : 7 * which + 7]
        for at, piece in enumerate(GATHERED):
            rows_at = pl.ds(first + at * rows, rows)
            source = (own, other)[piece[1]].at[slot(piece)]
            held, index = gathered_at(piece, arrays)
            for kind, (start, end) in enumerate(
                (
                    (source.at[0], tokens.at[rows_at]),
                    (source.at[1], grads.at[rows_at]),
                    (held.at[index], values.at[rows_at]),
                )
            ):
                copy = pltpu.make_async_copy(start, end, sems.at[which, kind, at])
                copy.start()
                copies.append(copy)
        first += 16 * rows
    for copy in copies:
        copy.wait()
    width, depth = down_grad.shape

    def store(part, mask, row, out):
        for j in range(part.shape[1] // BLK):
            for i in range(part.shape[0] // BLK):
                block = part[i * BLK : (i + 1) * BLK, j * BLK : (j + 1) * BLK]
                keep = mask[row // BLK + i, j].astype(jnp.bfloat16)
                out[row + i * BLK : row + (i + 1) * BLK, j * BLK : (j + 1) * BLK] = (
                    block.astype(jnp.bfloat16) * keep
                )

    for row, size in tiles(depth):
        left = tokens[:, row : row + size]
        store(tn(left, values[:, :width]), gate_mask, row, gate_grad)
        store(tn(left, values[:, width : 2 * width]), up_mask, row, up_grad)
    for row, size in tiles(width):
        at = 2 * width + row
        store(tn(values[:, at : at + size], grads[...]), down_mask, row, down_grad)


def weight_grads(chunks, inputs, gate_mask, up_mask, down_mask):
    depth = inputs[0].shape[-1]
    total = inputs[2].shape[-1]
    width = total // 3
    count = 16 * sum(chunks)
    return pl.pallas_call(
        functools.partial(weight_grad_kernel, chunks),
        in_specs=[ANY] * len(inputs) + [SMEM] * 3,
        out_specs=[VMEM] * 3,
        out_shape=[
            jax.ShapeDtypeStruct((depth, width), jnp.bfloat16),
            jax.ShapeDtypeStruct((depth, width), jnp.bfloat16),
            jax.ShapeDtypeStruct((width, depth), jnp.bfloat16),
        ],
        scratch_shapes=[
            pltpu.VMEM((count, depth), jnp.bfloat16),
            pltpu.VMEM((count, depth), jnp.bfloat16),
            pltpu.VMEM((count, total), jnp.bfloat16),
            pltpu.SemaphoreType.DMA((len(chunks), 3, 16)),
        ],
        compiler_params=params(),
        cost_estimate=pl.CostEstimate(
            flops=2 * count * depth * total, bytes_accessed=15 * 1024 * 1024, transcendentals=0
        ),
        name="weight_grads",
    )(*inputs, gate_mask, up_mask, down_mask)


def wide(array):
    return array.astype(jnp.float32)


def elementwise(totals):
    width = totals.shape[-1] // 3
    gate = totals[..., :width]
    up_part = totals[..., width : 2 * width]
    hidden_grad = totals[..., 2 * width :]
    sigmoid_gate = jax.nn.sigmoid(gate)
    activated = gate * sigmoid_gate
    hidden = activated * up_part
    gate_delta = hidden_grad * up_part * sigmoid_gate * (1.0 + gate * (1.0 - sigmoid_gate))
    up_delta = hidden_grad * activated
    return jnp.concatenate([gate_delta, up_delta, hidden], axis=-1).astype(jnp.bfloat16)


def after(value, *others):
    return lax.optimization_barrier((value, others))[0]


def row_sums(kept, late_down, late_up, from_down, from_up):
    return jnp.concatenate(
        [
            wide(kept[:2]) + wide(late_down) + wide(from_up[2:]),
            wide(kept[2:]) + wide(late_up) + wide(from_down[2:]),
        ]
    ).astype(jnp.bfloat16)


def gather_direct(part):
    return jnp.stack([part] + [move(part, dy=-dy, dxh=dx) for dy, dx in PEERS[1:]])


def gather_pair(part):
    return jnp.stack([part, move(part, dxh=1)])


def gather_pairs(pair):
    return jnp.concatenate([pair] + [move(pair, dy=-dy) for dy in range(1, 4)])


def swap_sums(sums):
    partner = move(sums, dxl=1)
    swapped = jnp.concatenate([partner[1:2], partner[0:1], partner[3:4], partner[2:3]])
    return wide(sums) + wide(swapped)


def chip_sum(for_own, received):
    return (wide(for_own) + wide(received)).astype(jnp.bfloat16)


def scatter_direct(chip):
    total = wide(chip[0])
    for at, (dy, dx) in enumerate(PEERS[1:], 1):
        total = total + wide(move(chip[at], dy=dy, dxh=dx))
    return total.astype(jnp.bfloat16)


def scatter_pairs(chip):
    total = wide(chip[:2])
    for dy in range(1, 4):
        total = total + wide(move(chip[2 * dy : 2 * dy + 2], dy=dy))
    return total.astype(jnp.bfloat16)


def scatter_pair(pair):
    return (wide(pair[0]) + wide(move(pair[1], dxh=1))).astype(jnp.bfloat16)


def shards(tokens, out_grad, gate_weight, up_weight, down_weight, gate_mask, up_mask, down_mask):
    depth = tokens.shape[1]
    cut = CHUNKS[0]
    part_a = jnp.stack([tokens[:cut], out_grad[:cut]])
    part_b = jnp.stack([tokens[cut:], out_grad[cut:]])
    weights = mask_weights(gate_weight, up_weight, down_weight, gate_mask, up_mask, down_mask)

    own_a = gather_direct(part_a)
    own_a, weights = lax.optimization_barrier((own_a, weights))
    other_a = move(own_a, dcore=1)
    pair_b = gather_pair(after(part_b, own_a))

    up_a, down_a, next_up_a, next_down_a, kept_a = forward(GROUPS, own_a, other_a, weights)
    from_down_a = move(up_a, dz=1)
    from_up_a = move(down_a, dz=-1)
    own_b = gather_pairs(after(pair_b, up_a))
    next_up_a = next_up_a + from_down_a[:2]
    next_down_a = next_down_a + from_up_a[:2]
    late_down_a = move(next_up_a, dz=1)
    late_up_a = move(next_down_a, dz=-1)

    own_b = after(own_b, next_up_a, next_down_a)
    other_b = move(own_b, dcore=1)
    up_b, down_b, next_up_b, next_down_b, kept_b = forward(GROUPS, own_b, other_b, weights)
    from_down_b = move(up_b, dz=1)
    from_up_b = move(down_b, dz=-1)

    sums_a = row_sums(kept_a, late_down_a, late_up_a, from_down_a, from_up_a)
    sums_a = after(sums_a, up_b)
    total_a = swap_sums(sums_a)
    next_up_b = next_up_b + after(from_down_b, sums_a)[:2]
    next_down_b = next_down_b + after(from_up_b, sums_a)[:2]
    late_down_b = move(next_up_b, dz=1)
    late_up_b = move(next_down_b, dz=-1)

    values_a = elementwise(after(total_a, next_up_b, next_down_b))
    near_a = (move(values_a, dz=-1), move(values_a, dz=1))
    sums_b = row_sums(kept_b, late_down_b, late_up_b, from_down_b, from_up_b)
    sums_b = after(sums_b, values_a)
    total_b = swap_sums(sums_b)
    far_a = (move(near_a[1][:2], dz=1), move(near_a[0][2:], dz=-1))
    arrays_a = (values_a, *near_a, *far_a)

    values_b = elementwise(total_b)
    near_b = (move(values_b, dz=-1), move(values_b, dz=1))
    arrays_a = after(arrays_a, values_b)
    for_other_a, for_own_a = backward(arrays_a, weights)
    received_a = move(for_other_a, dcore=1)
    far_b = (
        move(after(near_b[1], for_other_a)[:2], dz=1),
        move(after(near_b[0], for_other_a)[2:], dz=-1),
    )
    arrays_b = (values_b, *near_b, *far_b)
    chip_a = chip_sum(for_own_a, received_a)
    pair_a = scatter_pairs(chip_a)

    arrays_b = after(arrays_b, chip_a)
    for_other_b, for_own_b = backward(arrays_b, weights)
    received_b = move(for_other_b, dcore=1)
    result_a = scatter_pair(after(pair_a, for_other_b))
    chip_b = after(chip_sum(for_own_b, received_b), pair_a)
    result_b = scatter_direct(chip_b)

    inputs = [own_a, other_a, *arrays_a, own_b, other_b, *arrays_b]
    inputs = after(inputs, chip_b)
    gate_grad, up_grad, down_grad = weight_grads(CHUNKS, inputs, gate_mask, up_mask, down_mask)
    result = jnp.concatenate([result_a, result_b])
    return (result[:, :depth], result[:, depth:], gate_grad, up_grad, down_grad)


def solution(mesh):
    in_specs = (
        P("col", "row"),
        P("col", "row"),
        P("row", "col"),
        P("row", "col"),
        P("col", "row"),
        P("row", "col"),
        P("row", "col"),
        P("col", "row"),
    )
    out_specs = (
        P("col", "row"),
        P("col", "row"),
        P("row", "col"),
        P("row", "col"),
        P("col", "row"),
    )
    return jax.shard_map(shards, mesh=mesh, in_specs=in_specs, out_specs=out_specs, check_vma=False)
```

```python
import functools

import jax
import jax.numpy as jnp
from jax import lax
from jax.experimental import pallas as pl
from jax.experimental.pallas import tpu as pltpu
from jax.sharding import PartitionSpec as P

BLK = 128
CHUNKS = ((32, True, True), (32, True, True))
SEND_UP = ((2, 0), (1, 1))
SEND_DOWN = ((2, 1), (3, 0))
NEXT_UP = ((1, 0),)
NEXT_DOWN = ((3, 1),)
OWN = ((0, 0), (0, 1))
GROUPS = (SEND_UP, SEND_DOWN, NEXT_UP, NEXT_DOWN, OWN)
GATHERED = tuple((dz, half) for dz in (0, 1, 3, 2) for half in range(2))
VMEM_LIMIT = 24 * 1024 * 1024


def move(array, dy=0, dxh=0, dcore=0, dxl=0, dz=0):
    pairs = []
    for device in range(128):
        row, col = divmod(device, 16)
        x_lo, z = divmod(row, 4)
        y, x_hi, core = col // 4, col // 2 % 2, col % 2
        to_row = (x_lo + dxl) % 2 * 4 + (z + dz) % 4
        to_col = ((y + dy) % 4 * 2 + (x_hi + dxh) % 2) * 2 + (core + dcore) % 2
        pairs.append((device, to_row * 16 + to_col))
    return lax.ppermute(array, ("row", "col"), pairs)


def nn(left, right):
    return lax.dot_general(
        left, right, (((1,), (0,)), ((), ())), preferred_element_type=jnp.float32
    )


def nt(left, right):
    return lax.dot_general(
        left, right, (((1,), (1,)), ((), ())), preferred_element_type=jnp.float32
    )


def tn(left, right):
    return lax.dot_general(
        left, right, (((0,), (0,)), ((), ())), preferred_element_type=jnp.float32
    )


def params():
    return pltpu.CompilerParams(vmem_limit_bytes=VMEM_LIMIT)


def cheap():
    return pl.CostEstimate(flops=1024, bytes_accessed=1024, transcendentals=0)


VMEM = pl.BlockSpec(memory_space=pltpu.VMEM)
ANY = pl.BlockSpec(memory_space=pl.ANY)
SMEM = pl.BlockSpec(memory_space=pltpu.SMEM)


def owner(dz):
    return lax.rem(lax.axis_index("row") + dz, 4)


def token_copies(gathered, pieces, held, first, sems):
    rows = held_rows = None
    copies = []
    if len(gathered) == 2:
        rows = gathered[0].shape[2]
        for at, (dz, half) in enumerate(pieces):
            to = held.at[:, pl.ds(first + at * rows, rows)]
            copies.append((gathered[half].at[owner(dz)], to))
    else:
        rows = gathered[0].shape[2]
        for at, (dz, half) in enumerate(pieces):
            for sub in range(2):
                to = held.at[:, pl.ds(first + (2 * at + sub) * rows, rows)]
                copies.append((gathered[0].at[owner(dz) * 4 + half * 2 + sub], to))
    return [
        pltpu.make_async_copy(source, to, sems.at[at]) for at, (source, to) in enumerate(copies)
    ]


def gathered_at(piece, arrays, rows):
    own, up, down, far_first, far_second = arrays
    dz, half = piece
    if dz == 2:
        return (far_first, far_second)[half]
    return {0: own, 1: up, 3: down}[dz].at[pl.ds(half * rows, rows)]


def mask_kernel(gate, up, down, gate_mask, up_mask, down_mask, out):
    step = pl.program_id(0)
    width = gate.shape[1]
    down_t = down[...].T
    for j in range(width // BLK):
        at = pl.ds(j * BLK, BLK)
        out[:, at] = gate[:, at] * gate_mask[step, j].astype(jnp.bfloat16)
        to = pl.ds(width + j * BLK, BLK)
        out[:, to] = up[:, at] * up_mask[step, j].astype(jnp.bfloat16)
        to = pl.ds(2 * width + j * BLK, BLK)
        out[:, to] = down_t[:, j * BLK : (j + 1) * BLK] * down_mask[j, step].astype(jnp.bfloat16)


def mask_weights(gate, up, down, gate_mask, up_mask, down_mask):
    depth, width = gate.shape
    return pl.pallas_call(
        mask_kernel,
        grid=(depth // BLK,),
        in_specs=[
            pl.BlockSpec((BLK, width), lambda i: (i, 0)),
            pl.BlockSpec((BLK, width), lambda i: (i, 0)),
            pl.BlockSpec((width, BLK), lambda i: (0, i)),
            SMEM,
            SMEM,
            SMEM,
        ],
        out_specs=pl.BlockSpec((BLK, 3 * width), lambda i: (i, 0)),
        out_shape=jax.ShapeDtypeStruct((depth, 3 * width), jnp.bfloat16),
        compiler_params=params(),
        cost_estimate=pl.CostEstimate(
            flops=3 * depth * width, bytes_accessed=12 * depth * width, transcendentals=0
        ),
        name="mask_weights",
    )(gate, up, down, gate_mask, up_mask, down_mask)


def weight_copies(source, target, sems, order):
    width = target.shape[1] // 3
    depth = target.shape[0] // 2
    copies = []
    for at in order:
        columns = pl.ds(at * width, width)
        copies.append(
            [
                pltpu.make_async_copy(
                    source.at[pl.ds(part * depth, depth), columns],
                    target.at[pl.ds(part * depth, depth), columns],
                    sems.at[at, part],
                )
                for part in range(2)
            ]
        )
    return copies


def start(copies):
    for copy in copies:
        copy.start()


def wait(copies):
    for copy in copies:
        copy.wait()


def forward_kernel(count, *refs):
    gathered, weights, outs = refs[:count], refs[count], refs[count + 1 : count + 6]
    held, held_weights, sems, weight_sems = refs[count + 6 :]
    pieces = [piece for group in GROUPS for piece in group]
    copies = token_copies(gathered, pieces, held, 0, sems)
    loads = weight_copies(weights, held_weights, weight_sems, range(3))
    start(loads[0])
    start(copies)
    start(loads[1])
    start(loads[2])
    wait(copies)
    width = weights.shape[1] // 3
    rows = held.shape[1] // 8
    for at in range(3):
        wait(loads[at])
        columns = slice(at * width, (at + 1) * width)
        part = nn(held[at // 2], held_weights[:, columns]).astype(jnp.bfloat16)
        first = 0
        for out, group in zip(outs, GROUPS):
            size = len(group) * rows
            out[:, columns] = part[first : first + size]
            first += size


def forward(gathered, weights):
    depth, total = weights.shape
    count = len(gathered)
    rows = gathered[0].shape[2] * count // 2 if count == 2 else gathered[0].shape[2] * 2
    return pl.pallas_call(
        functools.partial(forward_kernel, count),
        in_specs=[ANY] * (count + 1),
        out_specs=[VMEM] * len(GROUPS),
        out_shape=[
            jax.ShapeDtypeStruct((len(group) * rows, total), jnp.bfloat16) for group in GROUPS
        ],
        scratch_shapes=[
            pltpu.VMEM((2, 8 * rows, depth), jnp.bfloat16),
            pltpu.VMEM((depth, total), jnp.bfloat16),
            pltpu.SemaphoreType.DMA((16,)),
            pltpu.SemaphoreType.DMA((3, 2)),
        ],
        compiler_params=params(),
        cost_estimate=cheap(),
        name="forward",
    )(*gathered, weights)


def place(piece, sub, gather_hops, scatter_hops):
    dz, half = piece
    col = lax.axis_index("col")
    y_me, x_me, core_me = col // 4, lax.rem(col // 2, 2), lax.rem(col, 2)
    if gather_hops:
        y, x, core = owner(dz), sub, half
        if scatter_hops:
            return ((1 - core) * 4 + y) * 2 + x
        return (lax.rem(y + y_me, 4) * 2 + lax.rem(x + x_me, 2)) * 2 + lax.rem(core + core_me, 2)
    y, x, core = owner(dz), half, sub
    if not scatter_hops:
        return (y * 2 + x) * 2 + core
    other = lax.rem(core + core_me, 2)
    return ((1 - other) * 4 + lax.rem(y - y_me + 4, 4)) * 2 + lax.rem(x + x_me, 2)


def backward_kernel(gather_hops, scatter_hops, *refs):
    arrays, weights = refs[:5], refs[5]
    outs, (held, held_weights, sems, weight_sems) = refs[6:-4], refs[-4:]
    rows = arrays[3].shape[0]
    copies = []
    together = gather_hops == scatter_hops
    for piece in GATHERED:
        source = gathered_at(piece, arrays, rows)
        size = rows if together else rows // 2
        for sub in range(1 if together else 2):
            at = place(piece, sub, gather_hops, scatter_hops)
            to = pl.ds(pl.multiple_of(at * (rows // 2), rows // 2), size)
            copies.append(
                pltpu.make_async_copy(
                    source.at[pl.ds(sub * size, size)], held.at[to], sems.at[len(copies)]
                )
            )
    loads = weight_copies(weights, held_weights, weight_sems, (2, 0, 1))
    start(loads[0])
    start(copies)
    start(loads[1])
    start(loads[2])
    wait(copies)
    depth = held_weights.shape[0]
    width = held_weights.shape[1] // 3

    def term(at):
        columns = slice(at * width, (at + 1) * width)
        return nt(held[:, columns], held_weights[:, columns])

    def put(part, column):
        part = part.astype(jnp.bfloat16)
        size = part.shape[0] // len(outs)
        for at, out in enumerate(outs):
            out[:, column : column + depth] = part[at * size : (at + 1) * size]

    wait(loads[0])
    put(term(2), 0)
    wait(loads[1])
    wait(loads[2])
    columns = slice(0, 2 * width)
    put(nt(held[:, columns], held_weights[:, columns]), depth)


def backward(arrays, weights, gather_hops, scatter_hops):
    rows = arrays[3].shape[0]
    depth, total = weights.shape
    count = 2 if scatter_hops else 1
    return pl.pallas_call(
        functools.partial(backward_kernel, gather_hops, scatter_hops),
        in_specs=[ANY] * 6,
        out_specs=[VMEM] * count,
        out_shape=[jax.ShapeDtypeStruct((8 * rows // count, 2 * depth), jnp.bfloat16)] * count,
        scratch_shapes=[
            pltpu.VMEM((8 * rows, total), jnp.bfloat16),
            pltpu.VMEM((depth, total), jnp.bfloat16),
            pltpu.SemaphoreType.DMA((16,)),
            pltpu.SemaphoreType.DMA((3, 2)),
        ],
        compiler_params=params(),
        cost_estimate=cheap(),
        name="backward",
    )(*arrays, weights)


def weight_grad_kernel(counts, *refs):
    number = sum(counts) + 5 * len(counts)
    gate_mask, up_mask, down_mask, gate_grad, up_grad, down_grad = refs[number : number + 6]
    tokens, values, sems, value_sems = refs[number + 6 :]
    first = at = 0
    copies = []
    for which, count in enumerate(counts):
        gathered, arrays = refs[at : at + count], refs[at + count : at + count + 5]
        at += count + 5
        rows = arrays[3].shape[0]
        copies += token_copies(gathered, GATHERED, tokens, first, sems.at[which])
        for number, piece in enumerate(GATHERED):
            copies.append(
                pltpu.make_async_copy(
                    gathered_at(piece, arrays, rows),
                    values.at[pl.ds(first + number * rows, rows)],
                    value_sems.at[which, number],
                )
            )
        first += 8 * rows
    start(copies)
    wait(copies)
    width, depth = down_grad.shape

    def store(part, mask, row, out):
        for j in range(part.shape[1] // BLK):
            for i in range(part.shape[0] // BLK):
                block = part[i * BLK : (i + 1) * BLK, j * BLK : (j + 1) * BLK]
                keep = mask[row // BLK + i, j].astype(jnp.bfloat16)
                out[row + i * BLK : row + (i + 1) * BLK, j * BLK : (j + 1) * BLK] = (
                    block.astype(jnp.bfloat16) * keep
                )

    for row in range(0, depth, 256):
        left = tokens[0, :, row : row + 256]
        store(tn(left, values[:, :width]), gate_mask, row, gate_grad)
        store(tn(left, values[:, width : 2 * width]), up_mask, row, up_grad)
    for row in range(0, width, 256):
        size = min(256, width - row)
        left = values[:, 2 * width + row : 2 * width + row + size]
        store(tn(left, tokens[1]), down_mask, row, down_grad)


def weight_grads(chunks, gate_mask, up_mask, down_mask):
    depth = chunks[0][0][0].shape[-1]
    total = chunks[0][1][0].shape[-1]
    width = total // 3
    counts = tuple(len(gathered) for gathered, _ in chunks)
    count = sum(8 * arrays[3].shape[0] for _, arrays in chunks)
    inputs = [item for gathered, arrays in chunks for item in (*gathered, *arrays)]
    return pl.pallas_call(
        functools.partial(weight_grad_kernel, counts),
        in_specs=[ANY] * len(inputs) + [SMEM] * 3,
        out_specs=[VMEM] * 3,
        out_shape=[
            jax.ShapeDtypeStruct((depth, width), jnp.bfloat16),
            jax.ShapeDtypeStruct((depth, width), jnp.bfloat16),
            jax.ShapeDtypeStruct((width, depth), jnp.bfloat16),
        ],
        scratch_shapes=[
            pltpu.VMEM((2, count, depth), jnp.bfloat16),
            pltpu.VMEM((count, total), jnp.bfloat16),
            pltpu.SemaphoreType.DMA((len(chunks), 16)),
            pltpu.SemaphoreType.DMA((len(chunks), 8)),
        ],
        compiler_params=params(),
        cost_estimate=cheap(),
        name="weight_grads",
    )(*inputs, gate_mask, up_mask, down_mask)


def wide(array):
    return array.astype(jnp.float32)


def elementwise(totals):
    width = totals.shape[-1] // 3
    gate = totals[..., :width]
    up_part = totals[..., width : 2 * width]
    hidden_grad = totals[..., 2 * width :]
    sigmoid_gate = jax.nn.sigmoid(gate)
    activated = gate * sigmoid_gate
    hidden = activated * up_part
    gate_delta = hidden_grad * up_part * sigmoid_gate * (1.0 + gate * (1.0 - sigmoid_gate))
    up_delta = hidden_grad * activated
    return jnp.concatenate([gate_delta, up_delta, hidden], axis=-1).astype(jnp.bfloat16)


def after(value, *others):
    return lax.optimization_barrier((value, others))[0]


def chip_sum(for_own, received):
    return (wide(for_own) + wide(received)).astype(jnp.bfloat16)


def gather_pair(part):
    return jnp.concatenate([part, move(part, dxh=1)], axis=1)


def scatter_pairs(chip):
    rows = chip.shape[0] // 4
    total = wide(chip[:rows])
    for dy in range(1, 4):
        total = total + wide(move(chip[dy * rows : (dy + 1) * rows], dy=dy))
    return total.astype(jnp.bfloat16)


def scatter_pair(pair):
    rows = pair.shape[0] // 2
    return (wide(pair[:rows]) + wide(move(pair[rows:], dxh=1))).astype(jnp.bfloat16)


class Chunk:
    def __init__(self, part, gather_hops, scatter_hops):
        self.part, self.hops = part, (gather_hops, scatter_hops)

    def gather_near(self):
        self.pair = gather_pair(self.part)

    def gather_far(self, *others):
        self.pair = after(self.pair, *others)
        self.pairs = [self.pair] + [move(self.pair, dy=-dy) for dy in range(1, 4)]
        return self.pair

    def gather_core(self, *others):
        own = jnp.stack(after(self.pairs, *others))
        self.gathered = (own, move(own, dcore=1))
        return own

    def gather(self):
        self.gathered = (lax.all_gather(self.part, "col", axis=0),)

    def forward(self, weights):
        outs = forward(self.gathered, weights)
        self.late_up, self.late_down, self.kept = outs[2:]
        self.from_down = move(outs[0], dz=1)
        self.from_up = move(outs[1], dz=-1)
        return outs[0]

    def relay(self, *others):
        down, up = after((self.from_down, self.from_up), *others)
        rows = down.shape[0] // 2
        send_up = self.late_up + down[:rows]
        send_down = self.late_down + up[:rows]
        self.last_down = move(send_up, dz=1)
        self.last_up = move(send_down, dz=-1)
        self.direct = (up[rows:], down[rows:])
        return send_up, send_down

    def swap(self, *others):
        last_down, last_up = after((self.last_down, self.last_up), *others)
        rows = last_down.shape[0]
        self.sums = jnp.concatenate(
            [
                wide(self.kept[:rows]) + wide(last_down) + wide(self.direct[0]),
                wide(self.kept[rows:]) + wide(last_up) + wide(self.direct[1]),
            ]
        ).astype(jnp.bfloat16)
        self.partner = move(self.sums, dxl=1)
        return self.sums

    def spread(self, *others):
        partner = after(self.partner, *others)
        self.values = elementwise(wide(self.sums) + wide(partner))
        self.near = (move(self.values, dz=-1), move(self.values, dz=1))
        return self.values

    def far(self, *others):
        up, down = after(self.near, *others)
        rows = up.shape[0] // 2
        sent = down[:rows], up[rows:]
        self.arrays = (self.values, up, down, move(sent[0], dz=1), move(sent[1], dz=-1))
        return sent

    def backward(self, weights, *others):
        self.arrays = after(self.arrays, *others)
        outs = backward(self.arrays, weights, *self.hops)
        if self.hops[1]:
            self.for_own = outs[1]
            self.received = move(outs[0], dcore=1)
        else:
            self.result = lax.psum_scatter(outs[0], "col", scatter_dimension=0, tiled=True)
        return outs[0]

    def scatter(self, *others):
        if self.hops[1]:
            received = after(self.received, *others)
            chip = chip_sum(self.for_own, received)
            self.result = scatter_pair(scatter_pairs(chip))
            return chip
        return None


def shards(tokens, out_grad, gate_weight, up_weight, down_weight, gate_mask, up_mask, down_mask):
    depth = tokens.shape[1]
    chunks = []
    first = 0
    for rows, gather_hops, scatter_hops in CHUNKS:
        part = jnp.stack([tokens[first : first + rows], out_grad[first : first + rows]])
        chunks.append(Chunk(part, gather_hops, scatter_hops))
        first += rows
    a, b = chunks
    weights = mask_weights(gate_weight, up_weight, down_weight, gate_mask, up_mask, down_mask)
    a.gather_near()
    b.gather_near()
    a.pair, b.pair, weights = lax.optimization_barrier((a.pair, b.pair, weights))
    a.gather_far()
    own_a = a.gather_core()
    b.gather_far(own_a)
    up_a = a.forward(weights)
    own_b = b.gather_core(up_a)
    up_b = b.forward(weights)
    relay_a = a.relay(up_b)
    swap_a = a.swap(relay_a)
    relay_b = b.relay(swap_a)
    spread_a = a.spread(relay_b)
    swap_b = b.swap(spread_a)
    far_a = a.far(swap_b)
    spread_b = b.spread(far_a)
    back_a = a.backward(weights, spread_b)
    far_b = b.far(back_a)
    chip_a = a.scatter(far_b)
    back_b = b.backward(weights, chip_a)
    chip_b = b.scatter()
    inputs = after([(chunk.gathered, chunk.arrays) for chunk in chunks], chip_b)
    gate_grad, up_grad, down_grad = weight_grads(inputs, gate_mask, up_mask, down_mask)
    result = jnp.concatenate([chunk.result for chunk in chunks])
    return (result[:, :depth], result[:, depth:], gate_grad, up_grad, down_grad)


def solution(mesh):
    in_specs = (
        P("col", "row"),
        P("col", "row"),
        P("row", "col"),
        P("row", "col"),
        P("col", "row"),
        P("row", "col"),
        P("row", "col"),
        P("col", "row"),
    )
    out_specs = (
        P("col", "row"),
        P("col", "row"),
        P("row", "col"),
        P("row", "col"),
        P("col", "row"),
    )
    return jax.shard_map(shards, mesh=mesh, in_specs=in_specs, out_specs=out_specs, check_vma=False)
```

```python
import functools

import jax
import jax.numpy as jnp
from jax import lax
from jax.experimental import pallas as pl
from jax.experimental.pallas import tpu as pltpu
from jax.sharding import PartitionSpec as P

BLK = 128
CHUNKS = (32, 32)
GATHERS = ((0,), (1,))
ORDER = (
    "forward 0",
    "core 1",
    "relay 0",
    "forward 1",
    "swap 0",
    "relay 1",
    "spread 0",
    "swap 1",
    "far 0",
    "spread 1",
    "backward 0",
    "far 1",
    "send 0",
    "chip 0",
    "backward 1",
    "send 1",
    "chip 1",
    "grads",
    "last 0",
    "last 1",
)
SEND_UP = ((2, 0), (1, 1))
SEND_DOWN = ((2, 1), (3, 0))
NEXT_UP = ((1, 0),)
NEXT_DOWN = ((3, 1),)
OWN = ((0, 0), (0, 1))
GROUPS = (SEND_UP, SEND_DOWN, NEXT_UP, NEXT_DOWN, OWN)
GATHERED = tuple((dz, half) for dz in (0, 1, 3, 2) for half in range(2))
VMEM_LIMIT = 24 * 1024 * 1024


def move(array, dy=0, dxh=0, dcore=0, dxl=0, dz=0):
    pairs = []
    for device in range(128):
        row, col = divmod(device, 16)
        x_lo, z = divmod(row, 4)
        y, x_hi, core = col // 4, col // 2 % 2, col % 2
        to_row = (x_lo + dxl) % 2 * 4 + (z + dz) % 4
        to_col = ((y + dy) % 4 * 2 + (x_hi + dxh) % 2) * 2 + (core + dcore) % 2
        pairs.append((device, to_row * 16 + to_col))
    return lax.ppermute(array, ("row", "col"), pairs)


def nn(left, right):
    return lax.dot_general(
        left, right, (((1,), (0,)), ((), ())), preferred_element_type=jnp.float32
    )


def nt(left, right):
    return lax.dot_general(
        left, right, (((1,), (1,)), ((), ())), preferred_element_type=jnp.float32
    )


def tn(left, right):
    return lax.dot_general(
        left, right, (((0,), (0,)), ((), ())), preferred_element_type=jnp.float32
    )


def params():
    return pltpu.CompilerParams(vmem_limit_bytes=VMEM_LIMIT)


def cheap():
    return pl.CostEstimate(flops=1024, bytes_accessed=1024, transcendentals=0)


VMEM = pl.BlockSpec(memory_space=pltpu.VMEM)
ANY = pl.BlockSpec(memory_space=pl.ANY)
SMEM = pl.BlockSpec(memory_space=pltpu.SMEM)


def owner(dz):
    return lax.rem(lax.axis_index("row") + dz, 4)


def token_copies(gathered, offset, rows, pieces, held, first, sems):
    copies = []
    for at, (dz, half) in enumerate(pieces):
        source = gathered[half].at[owner(dz), :, pl.ds(offset, rows)]
        to = held.at[:, pl.ds(first + at * rows, rows)]
        copies.append(pltpu.make_async_copy(source, to, sems.at[at]))
    return copies


def gathered_at(piece, arrays, rows):
    own, up, down, far_first, far_second = arrays
    dz, half = piece
    if dz == 2:
        return (far_first, far_second)[half]
    return {0: own, 1: up, 3: down}[dz].at[pl.ds(half * rows, rows)]


def mask_kernel(gate, up, down, gate_mask, up_mask, down_mask, out):
    step = pl.program_id(0)
    width = gate.shape[1]
    down_t = down[...].T
    for j in range(width // BLK):
        at = pl.ds(j * BLK, BLK)
        out[:, at] = gate[:, at] * gate_mask[step, j].astype(jnp.bfloat16)
        to = pl.ds(width + j * BLK, BLK)
        out[:, to] = up[:, at] * up_mask[step, j].astype(jnp.bfloat16)
        to = pl.ds(2 * width + j * BLK, BLK)
        out[:, to] = down_t[:, j * BLK : (j + 1) * BLK] * down_mask[j, step].astype(jnp.bfloat16)


def mask_weights(gate, up, down, gate_mask, up_mask, down_mask):
    depth, width = gate.shape
    return pl.pallas_call(
        mask_kernel,
        grid=(depth // BLK,),
        in_specs=[
            pl.BlockSpec((BLK, width), lambda i: (i, 0)),
            pl.BlockSpec((BLK, width), lambda i: (i, 0)),
            pl.BlockSpec((width, BLK), lambda i: (0, i)),
            SMEM,
            SMEM,
            SMEM,
        ],
        out_specs=pl.BlockSpec((BLK, 3 * width), lambda i: (i, 0)),
        out_shape=jax.ShapeDtypeStruct((depth, 3 * width), jnp.bfloat16),
        compiler_params=params(),
        cost_estimate=pl.CostEstimate(
            flops=3 * depth * width, bytes_accessed=12 * depth * width, transcendentals=0
        ),
        name="mask_weights",
    )(gate, up, down, gate_mask, up_mask, down_mask)


def weight_copies(source, target, sems, order):
    width = target.shape[1] // 3
    depth = target.shape[0] // 2
    copies = []
    for at in order:
        columns = pl.ds(at * width, width)
        copies.append(
            [
                pltpu.make_async_copy(
                    source.at[pl.ds(part * depth, depth), columns],
                    target.at[pl.ds(part * depth, depth), columns],
                    sems.at[at, part],
                )
                for part in range(2)
            ]
        )
    return copies


def start(copies):
    for copy in copies:
        copy.start()


def wait(copies):
    for copy in copies:
        copy.wait()


def forward_kernel(offset, rows, *refs):
    gathered, weights, outs = refs[:2], refs[2], refs[3:8]
    held, held_weights, sems, weight_sems = refs[8:]
    pieces = [piece for group in GROUPS for piece in group]
    copies = token_copies(gathered, offset, rows, pieces, held, 0, sems)
    loads = weight_copies(weights, held_weights, weight_sems, range(3))
    start(loads[0])
    start(copies)
    start(loads[1])
    start(loads[2])
    wait(copies)
    width = weights.shape[1] // 3
    for at in range(3):
        wait(loads[at])
        columns = slice(at * width, (at + 1) * width)
        part = nn(held[at // 2], held_weights[:, columns]).astype(jnp.bfloat16)
        first = 0
        for out, group in zip(outs, GROUPS):
            size = len(group) * rows
            out[:, columns] = part[first : first + size]
            first += size


def forward(gathered, offset, rows, weights):
    depth, total = weights.shape
    return pl.pallas_call(
        functools.partial(forward_kernel, offset, rows),
        in_specs=[ANY] * 3,
        out_specs=[VMEM] * len(GROUPS),
        out_shape=[
            jax.ShapeDtypeStruct((len(group) * rows, total), jnp.bfloat16) for group in GROUPS
        ],
        scratch_shapes=[
            pltpu.VMEM((2, 8 * rows, depth), jnp.bfloat16),
            pltpu.VMEM((depth, total), jnp.bfloat16),
            pltpu.SemaphoreType.DMA((8,)),
            pltpu.SemaphoreType.DMA((3, 2)),
        ],
        compiler_params=params(),
        cost_estimate=cheap(),
        name="forward",
    )(*gathered, weights)


def backward_kernel(*refs):
    arrays, weights = refs[:5], refs[5]
    outs, (held, held_weights, sems, weight_sems) = refs[6:8], refs[8:]
    rows = arrays[3].shape[0]
    copies = []
    for at, (dz, half) in enumerate(GATHERED):
        source = gathered_at((dz, half), arrays, rows)
        to = pl.ds(pl.multiple_of(((1 - half) * 4 + owner(dz)) * rows, rows), rows)
        copies.append(pltpu.make_async_copy(source, held.at[to], sems.at[at]))
    loads = weight_copies(weights, held_weights, weight_sems, (2, 0, 1))
    start(loads[0])
    start(copies)
    start(loads[1])
    start(loads[2])
    wait(copies)
    depth = held_weights.shape[0]
    width = held_weights.shape[1] // 3

    def term(at):
        columns = slice(at * width, (at + 1) * width)
        return nt(held[:, columns], held_weights[:, columns])

    def put(part, column):
        part = part.astype(jnp.bfloat16)
        size = part.shape[0] // len(outs)
        for at, out in enumerate(outs):
            out[:, column : column + depth] = part[at * size : (at + 1) * size]

    wait(loads[0])
    put(term(2), 0)
    wait(loads[1])
    wait(loads[2])
    columns = slice(0, 2 * width)
    put(nt(held[:, columns], held_weights[:, columns]), depth)


def backward(arrays, weights):
    rows = arrays[3].shape[0]
    depth, total = weights.shape
    return pl.pallas_call(
        backward_kernel,
        in_specs=[ANY] * 6,
        out_specs=[VMEM] * 2,
        out_shape=[jax.ShapeDtypeStruct((4 * rows, 2 * depth), jnp.bfloat16)] * 2,
        scratch_shapes=[
            pltpu.VMEM((8 * rows, total), jnp.bfloat16),
            pltpu.VMEM((depth, total), jnp.bfloat16),
            pltpu.SemaphoreType.DMA((8,)),
            pltpu.SemaphoreType.DMA((3, 2)),
        ],
        compiler_params=params(),
        cost_estimate=pl.CostEstimate(
            flops=16 * rows * depth * total, bytes_accessed=8 * depth * total, transcendentals=0
        ),
        name="backward",
    )(*arrays, weights)


def weight_grad_kernel(offsets, *refs):
    number = 7 * len(offsets)
    gate_mask, up_mask, down_mask, gate_grad, up_grad, down_grad = refs[number : number + 6]
    tokens, values, sems, value_sems = refs[number + 6 :]
    first = 0
    copies = []
    for which, offset in enumerate(offsets):
        gathered, arrays = refs[7 * which : 7 * which + 2], refs[7 * which + 2 : 7 * which + 7]
        rows = arrays[3].shape[0]
        copies += token_copies(gathered, offset, rows, GATHERED, tokens, first, sems.at[which])
        for at, piece in enumerate(GATHERED):
            copies.append(
                pltpu.make_async_copy(
                    gathered_at(piece, arrays, rows),
                    values.at[pl.ds(first + at * rows, rows)],
                    value_sems.at[which, at],
                )
            )
        first += 8 * rows
    start(copies)
    wait(copies)
    width, depth = down_grad.shape

    def store(part, mask, row, out):
        for j in range(part.shape[1] // BLK):
            for i in range(part.shape[0] // BLK):
                block = part[i * BLK : (i + 1) * BLK, j * BLK : (j + 1) * BLK]
                keep = mask[row // BLK + i, j].astype(jnp.bfloat16)
                out[row + i * BLK : row + (i + 1) * BLK, j * BLK : (j + 1) * BLK] = (
                    block.astype(jnp.bfloat16) * keep
                )

    for row in range(0, depth, 256):
        left = tokens[0, :, row : row + 256]
        store(tn(left, values[:, :width]), gate_mask, row, gate_grad)
        store(tn(left, values[:, width : 2 * width]), up_mask, row, up_grad)
    for row in range(0, width, 256):
        size = min(256, width - row)
        left = values[:, 2 * width + row : 2 * width + row + size]
        store(tn(left, tokens[1]), down_mask, row, down_grad)


def weight_grads(offsets, chunks, gate_mask, up_mask, down_mask):
    depth = chunks[0][0][0].shape[-1]
    total = chunks[0][1][0].shape[-1]
    width = total // 3
    count = sum(8 * arrays[3].shape[0] for _, arrays in chunks)
    inputs = [item for gathered, arrays in chunks for item in (*gathered, *arrays)]
    return pl.pallas_call(
        functools.partial(weight_grad_kernel, offsets),
        in_specs=[ANY] * len(inputs) + [SMEM] * 3,
        out_specs=[VMEM] * 3,
        out_shape=[
            jax.ShapeDtypeStruct((depth, width), jnp.bfloat16),
            jax.ShapeDtypeStruct((depth, width), jnp.bfloat16),
            jax.ShapeDtypeStruct((width, depth), jnp.bfloat16),
        ],
        scratch_shapes=[
            pltpu.VMEM((2, count, depth), jnp.bfloat16),
            pltpu.VMEM((count, total), jnp.bfloat16),
            pltpu.SemaphoreType.DMA((len(chunks), 8)),
            pltpu.SemaphoreType.DMA((len(chunks), 8)),
        ],
        compiler_params=params(),
        cost_estimate=pl.CostEstimate(
            flops=2 * count * depth * total, bytes_accessed=16 * depth * total, transcendentals=0
        ),
        name="weight_grads",
    )(*inputs, gate_mask, up_mask, down_mask)


def wide(array):
    return array.astype(jnp.float32)


def elementwise(totals):
    width = totals.shape[-1] // 3
    gate = totals[..., :width]
    up_part = totals[..., width : 2 * width]
    hidden_grad = totals[..., 2 * width :]
    sigmoid_gate = jax.nn.sigmoid(gate)
    activated = gate * sigmoid_gate
    hidden = activated * up_part
    gate_delta = hidden_grad * up_part * sigmoid_gate * (1.0 + gate * (1.0 - sigmoid_gate))
    up_delta = hidden_grad * activated
    return jnp.concatenate([gate_delta, up_delta, hidden], axis=-1).astype(jnp.bfloat16)


def after(value, *others):
    return lax.optimization_barrier((value, others))[0]


def chip_sum(for_own, received):
    return (wide(for_own) + wide(received)).astype(jnp.bfloat16)


class Gather:
    def __init__(self, pair):
        self.pair = pair

    def far(self, *others):
        self.pair = after(self.pair, *others)
        self.pairs = [self.pair] + [move(self.pair, dy=-dy) for dy in range(1, 4)]

    def core(self, *others):
        own = jnp.stack(after(self.pairs, *others))
        self.arrays = (own, move(own, dcore=1))
        return own


class Chunk:
    def __init__(self, gather, offset, rows, weights):
        self.source, self.offset, self.rows = gather, offset, 2 * rows
        self.weights = weights

    def forward(self, *others):
        self.gathered = self.source.arrays
        gathered = after(self.gathered, *others)
        outs = forward(gathered, self.offset, self.rows, self.weights)
        self.late_up, self.late_down, self.kept = outs[2:]
        self.from_down = move(outs[0], dz=1)
        self.from_up = move(outs[1], dz=-1)
        return outs[0]

    def relay(self, *others):
        down, up = after((self.from_down, self.from_up), *others)
        rows = self.rows
        send_up = self.late_up + down[:rows]
        send_down = self.late_down + up[:rows]
        self.last_down = move(send_up, dz=1)
        self.last_up = move(send_down, dz=-1)
        self.direct = (up[rows:], down[rows:])
        return send_up, send_down

    def swap(self, *others):
        last_down, last_up = after((self.last_down, self.last_up), *others)
        rows = self.rows
        self.sums = jnp.concatenate(
            [
                wide(self.kept[:rows]) + wide(last_down) + wide(self.direct[0]),
                wide(self.kept[rows:]) + wide(last_up) + wide(self.direct[1]),
            ]
        ).astype(jnp.bfloat16)
        self.partner = move(self.sums, dxl=1)
        return self.sums

    def spread(self, *others):
        partner = after(self.partner, *others)
        self.values = elementwise(wide(self.sums) + wide(partner))
        self.near = (move(self.values, dz=-1), move(self.values, dz=1))
        return self.values

    def far(self, *others):
        up, down = after(self.near, *others)
        sent = down[: self.rows], up[self.rows :]
        self.arrays = (self.values, up, down, move(sent[0], dz=1), move(sent[1], dz=-1))
        return sent

    def backward(self, *others):
        self.arrays = after(self.arrays, *others)
        self.for_other, self.for_own = backward(self.arrays, self.weights)
        return self.for_other

    def send(self, *others):
        for_other = after(self.for_other, *others)
        self.received = move(for_other, dcore=1)
        return for_other

    def chip(self, *others):
        received = after(self.received, *others)
        chip = (wide(self.for_own) + wide(received)).astype(jnp.bfloat16)
        rows = self.rows
        self.parts = [chip[:rows]] + [
            move(chip[dy * rows : (dy + 1) * rows], dy=dy) for dy in range(1, 4)
        ]
        return chip

    def last(self, *others):
        total = sum(wide(part) for part in after(self.parts, *others)).astype(jnp.bfloat16)
        half = self.rows // 2
        self.result = wide(total[:half]) + wide(move(total[half:], dxh=1))
        return total


def shards(tokens, out_grad, gate_weight, up_weight, down_weight, gate_mask, up_mask, down_mask):
    depth = tokens.shape[1]
    starts = [sum(CHUNKS[:i]) for i in range(len(CHUNKS))]
    part = jnp.stack([tokens, out_grad])
    received = move(part, dxh=1)
    weights = mask_weights(gate_weight, up_weight, down_weight, gate_mask, up_mask, down_mask)
    gathers, chunks = [], []
    for group in GATHERS:
        slices = [slice(starts[i], starts[i] + CHUNKS[i]) for i in group]
        gather = Gather(
            jnp.concatenate([half[:, at] for at in slices for half in (part, received)], axis=1)
        )
        gathers.append(gather)
        for i in group:
            offset = 2 * (starts[i] - starts[group[0]])
            chunks.append(Chunk(gather, offset, CHUNKS[i], weights))
    gathers[0].far()
    before = gathers[0].core()
    gathers[1].far(before)
    for step in ORDER:
        name, _, which = step.partition(" ")
        if name == "core":
            before = gathers[int(which)].core(before)
        elif name == "grads":
            inputs = after([(chunk.gathered, chunk.arrays) for chunk in chunks], before)
            offsets = tuple(chunk.offset for chunk in chunks)
            grads = weight_grads(offsets, inputs, gate_mask, up_mask, down_mask)
            before = grads[0]
        else:
            before = getattr(chunks[int(which)], name)(before)
    result = jnp.concatenate([chunk.result for chunk in chunks]).astype(jnp.bfloat16)
    return (result[:, :depth], result[:, depth:], *grads)


def solution(mesh):
    in_specs = (
        P("col", "row"),
        P("col", "row"),
        P("row", "col"),
        P("row", "col"),
        P("col", "row"),
        P("row", "col"),
        P("row", "col"),
        P("col", "row"),
    )
    out_specs = (
        P("col", "row"),
        P("col", "row"),
        P("row", "col"),
        P("row", "col"),
        P("col", "row"),
    )
    return jax.shard_map(shards, mesh=mesh, in_specs=in_specs, out_specs=out_specs, check_vma=False)
```

```python
import functools

import jax
import jax.numpy as jnp
from jax import lax
from jax.experimental import pallas as pl
from jax.experimental.pallas import tpu as pltpu
from jax.sharding import PartitionSpec as P

BLK = 128
CHUNKS = (32, 32)
GATHERS = ((0,), (1,))
ORDER = (
    "forward 0",
    "core 1",
    "forward 1",
    "relay 0",
    "swap 0",
    "relay 1",
    "spread 0",
    "swap 1",
    "far 0",
    "spread 1",
    "backward 0",
    "far 1",
    "send 0",
    "chip 0",
    "backward 1",
    "send 1",
    "last 0",
    "chip 1",
    "grads",
    "last 1",
)
SEND_UP = ((2, 0), (1, 1))
SEND_DOWN = ((2, 1), (3, 0))
NEXT_UP = ((1, 0),)
NEXT_DOWN = ((3, 1),)
OWN = ((0, 0), (0, 1))
GROUPS = (SEND_UP, SEND_DOWN, NEXT_UP, NEXT_DOWN, OWN)
GATHERED = tuple((dz, half) for dz in (0, 1, 3, 2) for half in range(2))
VMEM_LIMIT = 24 * 1024 * 1024


def move(array, dy=0, dxh=0, dcore=0, dxl=0, dz=0):
    pairs = []
    for device in range(128):
        row, col = divmod(device, 16)
        x_lo, z = divmod(row, 4)
        y, x_hi, core = col // 4, col // 2 % 2, col % 2
        to_row = (x_lo + dxl) % 2 * 4 + (z + dz) % 4
        to_col = ((y + dy) % 4 * 2 + (x_hi + dxh) % 2) * 2 + (core + dcore) % 2
        pairs.append((device, to_row * 16 + to_col))
    return lax.ppermute(array, ("row", "col"), pairs)


def nn(left, right):
    return lax.dot_general(
        left, right, (((1,), (0,)), ((), ())), preferred_element_type=jnp.float32
    )


def nt(left, right):
    return lax.dot_general(
        left, right, (((1,), (1,)), ((), ())), preferred_element_type=jnp.float32
    )


def tn(left, right):
    return lax.dot_general(
        left, right, (((0,), (0,)), ((), ())), preferred_element_type=jnp.float32
    )


def params():
    return pltpu.CompilerParams(vmem_limit_bytes=VMEM_LIMIT)


def cheap():
    return pl.CostEstimate(flops=1024, bytes_accessed=1024, transcendentals=0)


VMEM = pl.BlockSpec(memory_space=pltpu.VMEM)
ANY = pl.BlockSpec(memory_space=pl.ANY)
SMEM = pl.BlockSpec(memory_space=pltpu.SMEM)


def owner(dz):
    return lax.rem(lax.axis_index("row") + dz, 4)


def token_copies(gathered, offset, rows, pieces, held, first, sems):
    copies = []
    for at, (dz, half) in enumerate(pieces):
        to = pl.ds(first + at * rows, rows)
        for kind in range(2):
            source = gathered[2 * half + kind].at[owner(dz), pl.ds(offset, rows)]
            copies.append(pltpu.make_async_copy(source, held.at[kind, to], sems.at[kind, at]))
    return copies


def gathered_at(piece, arrays, rows):
    own, up, down, far_first, far_second = arrays
    dz, half = piece
    if dz == 2:
        return (far_first, far_second)[half]
    return {0: own, 1: up, 3: down}[dz].at[pl.ds(half * rows, rows)]


def mask_kernel(gate, up, down, gate_mask, up_mask, down_mask, out):
    step = pl.program_id(0)
    width = gate.shape[1]
    down_t = down[...].T
    for j in range(width // BLK):
        at = pl.ds(j * BLK, BLK)
        out[:, at] = gate[:, at] * gate_mask[step, j].astype(jnp.bfloat16)
        to = pl.ds(width + j * BLK, BLK)
        out[:, to] = up[:, at] * up_mask[step, j].astype(jnp.bfloat16)
        to = pl.ds(2 * width + j * BLK, BLK)
        out[:, to] = down_t[:, j * BLK : (j + 1) * BLK] * down_mask[j, step].astype(jnp.bfloat16)


def mask_weights(gate, up, down, gate_mask, up_mask, down_mask):
    depth, width = gate.shape
    return pl.pallas_call(
        mask_kernel,
        grid=(depth // BLK,),
        in_specs=[
            pl.BlockSpec((BLK, width), lambda i: (i, 0)),
            pl.BlockSpec((BLK, width), lambda i: (i, 0)),
            pl.BlockSpec((width, BLK), lambda i: (0, i)),
            SMEM,
            SMEM,
            SMEM,
        ],
        out_specs=pl.BlockSpec((BLK, 3 * width), lambda i: (i, 0)),
        out_shape=jax.ShapeDtypeStruct((depth, 3 * width), jnp.bfloat16),
        compiler_params=params(),
        cost_estimate=pl.CostEstimate(
            flops=3 * depth * width, bytes_accessed=12 * depth * width, transcendentals=0
        ),
        name="mask_weights",
    )(gate, up, down, gate_mask, up_mask, down_mask)


def weight_copies(source, target, sems, order):
    width = target.shape[1] // 3
    depth = target.shape[0] // 2
    copies = []
    for at in order:
        columns = pl.ds(at * width, width)
        copies.append(
            [
                pltpu.make_async_copy(
                    source.at[pl.ds(part * depth, depth), columns],
                    target.at[pl.ds(part * depth, depth), columns],
                    sems.at[at, part],
                )
                for part in range(2)
            ]
        )
    return copies


def start(copies):
    for copy in copies:
        copy.start()


def wait(copies):
    for copy in copies:
        copy.wait()


def forward_kernel(offset, rows, *refs):
    gathered, weights, outs = refs[:4], refs[4], refs[5:10]
    held, held_weights, sems, weight_sems = refs[10:]
    pieces = [piece for group in GROUPS for piece in group]
    copies = token_copies(gathered, offset, rows, pieces, held, 0, sems)
    loads = weight_copies(weights, held_weights, weight_sems, range(3))
    start(loads[0])
    start(copies)
    start(loads[1])
    start(loads[2])
    wait(copies)
    width = weights.shape[1] // 3
    for at in range(3):
        wait(loads[at])
        columns = slice(at * width, (at + 1) * width)
        part = nn(held[at // 2], held_weights[:, columns]).astype(jnp.bfloat16)
        first = 0
        for out, group in zip(outs, GROUPS):
            size = len(group) * rows
            out[:, columns] = part[first : first + size]
            first += size


def forward(gathered, offset, rows, weights):
    depth, total = weights.shape
    return pl.pallas_call(
        functools.partial(forward_kernel, offset, rows),
        in_specs=[ANY] * 5,
        out_specs=[VMEM] * len(GROUPS),
        out_shape=[
            jax.ShapeDtypeStruct((len(group) * rows, total), jnp.bfloat16) for group in GROUPS
        ],
        scratch_shapes=[
            pltpu.VMEM((2, 8 * rows, depth), jnp.bfloat16),
            pltpu.VMEM((depth, total), jnp.bfloat16),
            pltpu.SemaphoreType.DMA((2, 8)),
            pltpu.SemaphoreType.DMA((3, 2)),
        ],
        compiler_params=params(),
        cost_estimate=cheap(),
        name="forward",
    )(*gathered, weights)


def backward_kernel(*refs):
    arrays, weights = refs[:5], refs[5]
    outs, (held, held_weights, sems, weight_sems) = refs[6:8], refs[8:]
    rows = arrays[3].shape[0]
    copies = []
    for at, (dz, half) in enumerate(GATHERED):
        source = gathered_at((dz, half), arrays, rows)
        to = pl.ds(pl.multiple_of(((1 - half) * 4 + owner(dz)) * rows, rows), rows)
        copies.append(pltpu.make_async_copy(source, held.at[to], sems.at[at]))
    loads = weight_copies(weights, held_weights, weight_sems, (2, 0, 1))
    start(loads[0])
    start(copies)
    start(loads[1])
    start(loads[2])
    wait(copies)
    depth = held_weights.shape[0]
    width = held_weights.shape[1] // 3

    def term(at):
        columns = slice(at * width, (at + 1) * width)
        return nt(held[:, columns], held_weights[:, columns])

    def put(part, column):
        part = part.astype(jnp.bfloat16)
        size = part.shape[0] // len(outs)
        for at, out in enumerate(outs):
            out[:, column : column + depth] = part[at * size : (at + 1) * size]

    wait(loads[0])
    put(term(2), 0)
    wait(loads[1])
    wait(loads[2])
    columns = slice(0, 2 * width)
    put(nt(held[:, columns], held_weights[:, columns]), depth)


def backward(arrays, weights):
    rows = arrays[3].shape[0]
    depth, total = weights.shape
    return pl.pallas_call(
        backward_kernel,
        in_specs=[ANY] * 6,
        out_specs=[VMEM] * 2,
        out_shape=[jax.ShapeDtypeStruct((4 * rows, 2 * depth), jnp.bfloat16)] * 2,
        scratch_shapes=[
            pltpu.VMEM((8 * rows, total), jnp.bfloat16),
            pltpu.VMEM((depth, total), jnp.bfloat16),
            pltpu.SemaphoreType.DMA((8,)),
            pltpu.SemaphoreType.DMA((3, 2)),
        ],
        compiler_params=params(),
        cost_estimate=pl.CostEstimate(
            flops=16 * rows * depth * total, bytes_accessed=8 * depth * total, transcendentals=0
        ),
        name="backward",
    )(*arrays, weights)


def weight_grad_kernel(offsets, *refs):
    number = 9 * len(offsets)
    gate_mask, up_mask, down_mask, gate_grad, up_grad, down_grad = refs[number : number + 6]
    tokens, values, sems, value_sems = refs[number + 6 :]
    first = 0
    copies = []
    for which, offset in enumerate(offsets):
        gathered, arrays = refs[9 * which : 9 * which + 4], refs[9 * which + 4 : 9 * which + 9]
        rows = arrays[3].shape[0]
        copies += token_copies(gathered, offset, rows, GATHERED, tokens, first, sems.at[which])
        for at, piece in enumerate(GATHERED):
            copies.append(
                pltpu.make_async_copy(
                    gathered_at(piece, arrays, rows),
                    values.at[pl.ds(first + at * rows, rows)],
                    value_sems.at[which, at],
                )
            )
        first += 8 * rows
    start(copies)
    wait(copies)
    width, depth = down_grad.shape

    def store(part, mask, row, out):
        for j in range(part.shape[1] // BLK):
            for i in range(part.shape[0] // BLK):
                block = part[i * BLK : (i + 1) * BLK, j * BLK : (j + 1) * BLK]
                keep = mask[row // BLK + i, j].astype(jnp.bfloat16)
                out[row + i * BLK : row + (i + 1) * BLK, j * BLK : (j + 1) * BLK] = (
                    block.astype(jnp.bfloat16) * keep
                )

    for row in range(0, depth, 256):
        left = tokens[0, :, row : row + 256]
        store(tn(left, values[:, :width]), gate_mask, row, gate_grad)
        store(tn(left, values[:, width : 2 * width]), up_mask, row, up_grad)
    for row in range(0, width, 256):
        size = min(256, width - row)
        left = values[:, 2 * width + row : 2 * width + row + size]
        store(tn(left, tokens[1]), down_mask, row, down_grad)


def weight_grads(offsets, chunks, gate_mask, up_mask, down_mask):
    depth = chunks[0][0][0].shape[-1]
    total = chunks[0][1][0].shape[-1]
    width = total // 3
    count = sum(8 * arrays[3].shape[0] for _, arrays in chunks)
    inputs = [item for gathered, arrays in chunks for item in (*gathered, *arrays)]
    return pl.pallas_call(
        functools.partial(weight_grad_kernel, offsets),
        in_specs=[ANY] * len(inputs) + [SMEM] * 3,
        out_specs=[VMEM] * 3,
        out_shape=[
            jax.ShapeDtypeStruct((depth, width), jnp.bfloat16),
            jax.ShapeDtypeStruct((depth, width), jnp.bfloat16),
            jax.ShapeDtypeStruct((width, depth), jnp.bfloat16),
        ],
        scratch_shapes=[
            pltpu.VMEM((2, count, depth), jnp.bfloat16),
            pltpu.VMEM((count, total), jnp.bfloat16),
            pltpu.SemaphoreType.DMA((len(chunks), 2, 8)),
            pltpu.SemaphoreType.DMA((len(chunks), 8)),
        ],
        compiler_params=params(),
        cost_estimate=pl.CostEstimate(
            flops=2 * count * depth * total, bytes_accessed=16 * depth * total, transcendentals=0
        ),
        name="weight_grads",
    )(*inputs, gate_mask, up_mask, down_mask)


def wide(array):
    return array.astype(jnp.float32)


def elementwise(totals):
    width = totals.shape[-1] // 3
    gate = totals[..., :width]
    up_part = totals[..., width : 2 * width]
    hidden_grad = totals[..., 2 * width :]
    sigmoid_gate = jax.nn.sigmoid(gate)
    activated = gate * sigmoid_gate
    hidden = activated * up_part
    gate_delta = hidden_grad * up_part * sigmoid_gate * (1.0 + gate * (1.0 - sigmoid_gate))
    up_delta = hidden_grad * activated
    return jnp.concatenate([gate_delta, up_delta, hidden], axis=-1).astype(jnp.bfloat16)


def after(value, *others):
    return lax.optimization_barrier((value, others))[0]


def chip_sum(for_own, received):
    return (wide(for_own) + wide(received)).astype(jnp.bfloat16)


class Gather:
    def __init__(self, pair):
        self.pair = pair

    def far(self, *others):
        self.pair = after(self.pair, *others)
        self.pairs = [self.pair] + [move(self.pair, dy=-dy) for dy in range(1, 4)]

    def core(self, *others):
        pairs = after(self.pairs, *others)
        own = [jnp.stack([pair[kind] for pair in pairs]) for kind in range(2)]
        self.arrays = (*own, *[move(array, dcore=1) for array in own])
        return own


class Chunk:
    def __init__(self, gather, offset, rows, weights):
        self.source, self.offset, self.rows = gather, offset, 2 * rows
        self.weights = weights

    def forward(self, *others):
        self.gathered = self.source.arrays
        gathered = after(self.gathered, *others)
        outs = forward(gathered, self.offset, self.rows, self.weights)
        self.late_up, self.late_down, self.kept = outs[2:]
        self.from_down = move(outs[0], dz=1)
        self.from_up = move(outs[1], dz=-1)
        return outs[0]

    def relay(self, *others):
        down, up = after((self.from_down, self.from_up), *others)
        rows = self.rows
        send_up = self.late_up + down[:rows]
        send_down = self.late_down + up[:rows]
        self.last_down = move(send_up, dz=1)
        self.last_up = move(send_down, dz=-1)
        self.direct = (up[rows:], down[rows:])
        return send_up, send_down

    def swap(self, *others):
        last_down, last_up = after((self.last_down, self.last_up), *others)
        rows = self.rows
        self.sums = jnp.concatenate(
            [
                wide(self.kept[:rows]) + wide(last_down) + wide(self.direct[0]),
                wide(self.kept[rows:]) + wide(last_up) + wide(self.direct[1]),
            ]
        ).astype(jnp.bfloat16)
        self.partner = move(self.sums, dxl=1)
        return self.sums

    def spread(self, *others):
        partner = after(self.partner, *others)
        self.values = elementwise(wide(self.sums) + wide(partner))
        self.near = (move(self.values, dz=-1), move(self.values, dz=1))
        return self.values

    def far(self, *others):
        up, down = after(self.near, *others)
        sent = down[: self.rows], up[self.rows :]
        self.arrays = (self.values, up, down, move(sent[0], dz=1), move(sent[1], dz=-1))
        return sent

    def backward(self, *others):
        self.arrays = after(self.arrays, *others)
        self.for_other, self.for_own = backward(self.arrays, self.weights)
        return self.for_other

    def send(self, *others):
        for_other = after(self.for_other, *others)
        self.received = move(for_other, dcore=1)
        return for_other

    def chip(self, *others):
        received = after(self.received, *others)
        chip = (wide(self.for_own) + wide(received)).astype(jnp.bfloat16)
        rows = self.rows
        self.parts = [chip[:rows]] + [
            move(chip[dy * rows : (dy + 1) * rows], dy=dy) for dy in range(1, 4)
        ]
        return chip

    def last(self, *others):
        total = sum(wide(part) for part in after(self.parts, *others)).astype(jnp.bfloat16)
        half = self.rows // 2
        self.result = wide(total[:half]) + wide(move(total[half:], dxh=1))
        return total


def shards(tokens, out_grad, gate_weight, up_weight, down_weight, gate_mask, up_mask, down_mask):
    depth = tokens.shape[1]
    starts = [sum(CHUNKS[:i]) for i in range(len(CHUNKS))]
    part = jnp.stack([tokens, out_grad])
    received = move(part, dxh=1)
    weights = mask_weights(gate_weight, up_weight, down_weight, gate_mask, up_mask, down_mask)
    gathers, chunks = [], []
    for group in GATHERS:
        slices = [slice(starts[i], starts[i] + CHUNKS[i]) for i in group]
        gather = Gather(
            jnp.concatenate([half[:, at] for at in slices for half in (part, received)], axis=1)
        )
        gathers.append(gather)
        for i in group:
            offset = 2 * (starts[i] - starts[group[0]])
            chunks.append(Chunk(gather, offset, CHUNKS[i], weights))
    gathers[0].far()
    before = gathers[0].core()
    gathers[1].far(before)
    for step in ORDER:
        name, _, which = step.partition(" ")
        if name == "core":
            before = gathers[int(which)].core(before)
        elif name == "grads":
            inputs = after([(chunk.gathered, chunk.arrays) for chunk in chunks], before)
            offsets = tuple(chunk.offset for chunk in chunks)
            grads = weight_grads(offsets, inputs, gate_mask, up_mask, down_mask)
            before = grads[0]
        else:
            before = getattr(chunks[int(which)], name)(before)
    result = jnp.concatenate([chunk.result for chunk in chunks]).astype(jnp.bfloat16)
    return (result[:, :depth], result[:, depth:], *grads)


def solution(mesh):
    in_specs = (
        P("col", "row"),
        P("col", "row"),
        P("row", "col"),
        P("row", "col"),
        P("col", "row"),
        P("row", "col"),
        P("row", "col"),
        P("col", "row"),
    )
    out_specs = (
        P("col", "row"),
        P("col", "row"),
        P("row", "col"),
        P("row", "col"),
        P("col", "row"),
    )
    return jax.shard_map(shards, mesh=mesh, in_specs=in_specs, out_specs=out_specs, check_vma=False)
```

```python
import functools

import jax
import jax.numpy as jnp
from jax import lax
from jax.experimental import pallas as pl
from jax.experimental.pallas import tpu as pltpu
from jax.sharding import PartitionSpec as P

BLK = 128
CHUNKS = (32, 32)
GATHERS = ((0,), (1,))
ORDER = (
    "forward 0",
    "core 1",
    "forward 1",
    "relay 0",
    "swap 0",
    "relay 1",
    "spread 0",
    "swap 1",
    "far 0",
    "spread 1",
    "backward 0",
    "far 1",
    "send 0",
    "chip 0",
    "backward 1",
    "last 0",
    "send 1",
    "chip 1",
    "grads",
    "last 1",
)
SEND_UP = ((2, 0), (1, 1))
SEND_DOWN = ((2, 1), (3, 0))
NEXT_UP = ((1, 0),)
NEXT_DOWN = ((3, 1),)
OWN = ((0, 0), (0, 1))
GROUPS = (SEND_UP, SEND_DOWN, NEXT_UP, NEXT_DOWN, OWN)
GATHERED = tuple((dz, half) for dz in (0, 1, 3, 2) for half in range(2))
VMEM_LIMIT = 24 * 1024 * 1024


def move(array, dy=0, dxh=0, dcore=0, dxl=0, dz=0):
    pairs = []
    for device in range(128):
        row, col = divmod(device, 16)
        x_lo, z = divmod(row, 4)
        y, x_hi, core = col // 4, col // 2 % 2, col % 2
        to_row = (x_lo + dxl) % 2 * 4 + (z + dz) % 4
        to_col = ((y + dy) % 4 * 2 + (x_hi + dxh) % 2) * 2 + (core + dcore) % 2
        pairs.append((device, to_row * 16 + to_col))
    return lax.ppermute(array, ("row", "col"), pairs)


def nn(left, right):
    return lax.dot_general(
        left, right, (((1,), (0,)), ((), ())), preferred_element_type=jnp.float32
    )


def nt(left, right):
    return lax.dot_general(
        left, right, (((1,), (1,)), ((), ())), preferred_element_type=jnp.float32
    )


def tn(left, right):
    return lax.dot_general(
        left, right, (((0,), (0,)), ((), ())), preferred_element_type=jnp.float32
    )


def params():
    return pltpu.CompilerParams(vmem_limit_bytes=VMEM_LIMIT)


def cheap():
    return pl.CostEstimate(flops=1024, bytes_accessed=1024, transcendentals=0)


VMEM = pl.BlockSpec(memory_space=pltpu.VMEM)
SMEM = pl.BlockSpec(memory_space=pltpu.SMEM)


def owner(dz):
    return lax.rem(lax.axis_index("row") + dz, 4)


def tokens_of(kind, gathered, offset, rows, columns):
    return [
        gathered[2 * half + kind][owner(dz), offset : offset + rows, columns]
        for dz, half in GATHERED
    ]


def values_of(arrays, columns):
    own, up, down, far_first, far_second = arrays
    return [array[:, columns] for array in (own, up, down, far_first, far_second)]


def mask_kernel(gate, up, down, gate_mask, up_mask, down_mask, out):
    step = pl.program_id(0)
    width = gate.shape[1]
    down_t = down[...].T
    for j in range(width // BLK):
        at = pl.ds(j * BLK, BLK)
        out[:, at] = gate[:, at] * gate_mask[step, j].astype(jnp.bfloat16)
        to = pl.ds(width + j * BLK, BLK)
        out[:, to] = up[:, at] * up_mask[step, j].astype(jnp.bfloat16)
        to = pl.ds(2 * width + j * BLK, BLK)
        out[:, to] = down_t[:, j * BLK : (j + 1) * BLK] * down_mask[j, step].astype(jnp.bfloat16)


def mask_weights(gate, up, down, gate_mask, up_mask, down_mask):
    depth, width = gate.shape
    return pl.pallas_call(
        mask_kernel,
        grid=(depth // BLK,),
        in_specs=[
            pl.BlockSpec((BLK, width), lambda i: (i, 0)),
            pl.BlockSpec((BLK, width), lambda i: (i, 0)),
            pl.BlockSpec((width, BLK), lambda i: (0, i)),
            SMEM,
            SMEM,
            SMEM,
        ],
        out_specs=pl.BlockSpec((BLK, 3 * width), lambda i: (i, 0)),
        out_shape=jax.ShapeDtypeStruct((depth, 3 * width), jnp.bfloat16),
        compiler_params=params(),
        cost_estimate=pl.CostEstimate(
            flops=3 * depth * width, bytes_accessed=12 * depth * width, transcendentals=0
        ),
        name="mask_weights",
    )(gate, up, down, gate_mask, up_mask, down_mask)


def forward_kernel(offset, rows, *refs):
    gathered, weights, outs = refs[:4], refs[4], refs[5:]
    width = weights.shape[1] // 3
    every = slice(None)
    for at in range(3):
        columns = slice(at * width, (at + 1) * width)
        left = jnp.concatenate(tokens_of(at // 2, gathered, offset, rows, every))
        part = nn(left, weights[:, columns]).astype(jnp.bfloat16)
        for number, piece in enumerate(GATHERED):
            for out, group in zip(outs, GROUPS):
                if piece in group:
                    first = group.index(piece) * rows
                    out[first : first + rows, columns] = part[number * rows : (number + 1) * rows]


def forward(gathered, offset, rows, weights):
    total = weights.shape[1]
    return pl.pallas_call(
        functools.partial(forward_kernel, offset, rows),
        in_specs=[VMEM] * 5,
        out_specs=[VMEM] * len(GROUPS),
        out_shape=[
            jax.ShapeDtypeStruct((len(group) * rows, total), jnp.bfloat16) for group in GROUPS
        ],
        compiler_params=params(),
        cost_estimate=cheap(),
        name="forward",
    )(*gathered, weights)


def backward_kernel(*refs):
    arrays, weights, for_other, for_own = refs[:5], *refs[5:]
    depth, total = weights.shape
    width = total // 3
    rows = for_own.shape[1]
    for columns, to in ((slice(2 * width, total), 0), (slice(0, 2 * width), depth)):
        left = jnp.concatenate(values_of(arrays, columns))
        part = nt(left, weights[:, columns]).astype(jnp.bfloat16)
        for at, (dz, half) in enumerate(GATHERED):
            out = (for_own, for_other)[half]
            out[owner(dz), :, to : to + depth] = part[at * rows : (at + 1) * rows]


def backward(arrays, weights):
    rows = arrays[3].shape[0]
    depth, total = weights.shape
    outs = pl.pallas_call(
        backward_kernel,
        in_specs=[VMEM] * 6,
        out_specs=[VMEM] * 2,
        out_shape=[jax.ShapeDtypeStruct((4, rows, 2 * depth), jnp.bfloat16)] * 2,
        compiler_params=params(),
        cost_estimate=pl.CostEstimate(
            flops=16 * rows * depth * total, bytes_accessed=8 * depth * total, transcendentals=0
        ),
        name="backward",
    )(*arrays, weights)
    return [out.reshape(4 * rows, 2 * depth) for out in outs]


def weight_grad_kernel(offsets, *refs):
    number = 9 * len(offsets)
    gate_mask, up_mask, down_mask, gate_grad, up_grad, down_grad = refs[number:]
    width, depth = down_grad.shape
    every = slice(None)

    def tokens(kind, columns):
        parts = []
        for which, offset in enumerate(offsets):
            chunk = refs[9 * which : 9 * which + 9]
            parts += tokens_of(kind, chunk[:4], offset, chunk[7].shape[0], columns)
        return jnp.concatenate(parts)

    def values(columns):
        parts = []
        for which in range(len(offsets)):
            parts += values_of(refs[9 * which + 4 : 9 * which + 9], columns)
        return jnp.concatenate(parts)

    def store(part, mask, row, out):
        for j in range(part.shape[1] // BLK):
            for i in range(part.shape[0] // BLK):
                block = part[i * BLK : (i + 1) * BLK, j * BLK : (j + 1) * BLK]
                keep = mask[row // BLK + i, j].astype(jnp.bfloat16)
                out[row + i * BLK : row + (i + 1) * BLK, j * BLK : (j + 1) * BLK] = (
                    block.astype(jnp.bfloat16) * keep
                )

    for row in range(0, depth, 256):
        left = tokens(0, slice(row, row + 256))
        store(tn(left, values(slice(0, width))), gate_mask, row, gate_grad)
        store(tn(left, values(slice(width, 2 * width))), up_mask, row, up_grad)
    for row in range(0, width, 256):
        size = min(256, width - row)
        left = values(slice(2 * width + row, 2 * width + row + size))
        store(tn(left, tokens(1, every)), down_mask, row, down_grad)


def weight_grads(offsets, chunks, gate_mask, up_mask, down_mask):
    depth = chunks[0][0][0].shape[-1]
    total = chunks[0][1][0].shape[-1]
    width = total // 3
    count = sum(8 * arrays[3].shape[0] for _, arrays in chunks)
    inputs = [item for gathered, arrays in chunks for item in (*gathered, *arrays)]
    return pl.pallas_call(
        functools.partial(weight_grad_kernel, offsets),
        in_specs=[VMEM] * len(inputs) + [SMEM] * 3,
        out_specs=[VMEM] * 3,
        out_shape=[
            jax.ShapeDtypeStruct((depth, width), jnp.bfloat16),
            jax.ShapeDtypeStruct((depth, width), jnp.bfloat16),
            jax.ShapeDtypeStruct((width, depth), jnp.bfloat16),
        ],
        compiler_params=params(),
        cost_estimate=pl.CostEstimate(
            flops=2 * count * depth * total, bytes_accessed=16 * depth * total, transcendentals=0
        ),
        name="weight_grads",
    )(*inputs, gate_mask, up_mask, down_mask)


def wide(array):
    return array.astype(jnp.float32)


def elementwise(totals):
    width = totals.shape[-1] // 3
    gate = totals[..., :width]
    up_part = totals[..., width : 2 * width]
    hidden_grad = totals[..., 2 * width :]
    sigmoid_gate = jax.nn.sigmoid(gate)
    activated = gate * sigmoid_gate
    hidden = activated * up_part
    gate_delta = hidden_grad * up_part * sigmoid_gate * (1.0 + gate * (1.0 - sigmoid_gate))
    up_delta = hidden_grad * activated
    return jnp.concatenate([gate_delta, up_delta, hidden], axis=-1).astype(jnp.bfloat16)


def after(value, *others):
    return lax.optimization_barrier((value, others))[0]


def chip_sum(for_own, received):
    return (wide(for_own) + wide(received)).astype(jnp.bfloat16)


class Gather:
    def __init__(self, pair):
        self.pair = pair

    def far(self, *others):
        self.pair = after(self.pair, *others)
        self.pairs = [self.pair] + [move(self.pair, dy=-dy) for dy in range(1, 4)]

    def core(self, *others):
        pairs = after(self.pairs, *others)
        own = [jnp.stack([pair[kind] for pair in pairs]) for kind in range(2)]
        self.arrays = (*own, *[move(array, dcore=1) for array in own])
        return own


class Chunk:
    def __init__(self, gather, offset, rows, weights):
        self.source, self.offset, self.rows = gather, offset, 2 * rows
        self.weights = weights

    def forward(self, *others):
        self.gathered = self.source.arrays
        gathered = after(self.gathered, *others)
        outs = forward(gathered, self.offset, self.rows, self.weights)
        self.late_up, self.late_down, self.kept = outs[2:]
        self.from_down = move(outs[0], dz=1)
        self.from_up = move(outs[1], dz=-1)
        return outs[0]

    def relay(self, *others):
        down, up = after((self.from_down, self.from_up), *others)
        rows = self.rows
        send_up = self.late_up + down[:rows]
        send_down = self.late_down + up[:rows]
        self.last_down = move(send_up, dz=1)
        self.last_up = move(send_down, dz=-1)
        self.direct = (up[rows:], down[rows:])
        return send_up, send_down

    def swap(self, *others):
        last_down, last_up = after((self.last_down, self.last_up), *others)
        rows = self.rows
        self.sums = jnp.concatenate(
            [
                wide(self.kept[:rows]) + wide(last_down) + wide(self.direct[0]),
                wide(self.kept[rows:]) + wide(last_up) + wide(self.direct[1]),
            ]
        ).astype(jnp.bfloat16)
        self.partner = move(self.sums, dxl=1)
        return self.sums

    def spread(self, *others):
        partner = after(self.partner, *others)
        self.values = elementwise(wide(self.sums) + wide(partner))
        self.near = (move(self.values, dz=-1), move(self.values, dz=1))
        return self.values

    def far(self, *others):
        up, down = after(self.near, *others)
        sent = down[: self.rows], up[self.rows :]
        self.arrays = (self.values, up, down, move(sent[0], dz=1), move(sent[1], dz=-1))
        return sent

    def backward(self, *others):
        self.arrays = after(self.arrays, *others)
        self.for_other, self.for_own = backward(self.arrays, self.weights)
        return self.for_other

    def send(self, *others):
        for_other = after(self.for_other, *others)
        self.received = move(for_other, dcore=1)
        return for_other

    def chip(self, *others):
        received = after(self.received, *others)
        chip = (wide(self.for_own) + wide(received)).astype(jnp.bfloat16)
        rows = self.rows
        self.parts = [chip[:rows]] + [
            move(chip[dy * rows : (dy + 1) * rows], dy=dy) for dy in range(1, 4)
        ]
        return chip

    def last(self, *others):
        total = sum(wide(part) for part in after(self.parts, *others)).astype(jnp.bfloat16)
        half = self.rows // 2
        self.result = wide(total[:half]) + wide(move(total[half:], dxh=1))
        return total


def shards(tokens, out_grad, gate_weight, up_weight, down_weight, gate_mask, up_mask, down_mask):
    depth = tokens.shape[1]
    starts = [sum(CHUNKS[:i]) for i in range(len(CHUNKS))]
    part = jnp.stack([tokens, out_grad])
    received = move(part, dxh=1)
    weights = mask_weights(gate_weight, up_weight, down_weight, gate_mask, up_mask, down_mask)
    gathers, chunks = [], []
    for group in GATHERS:
        slices = [slice(starts[i], starts[i] + CHUNKS[i]) for i in group]
        gather = Gather(
            jnp.concatenate([half[:, at] for at in slices for half in (part, received)], axis=1)
        )
        gathers.append(gather)
        for i in group:
            offset = 2 * (starts[i] - starts[group[0]])
            chunks.append(Chunk(gather, offset, CHUNKS[i], weights))
    gathers[0].far()
    before = gathers[0].core(weights)
    gathers[1].far(before)
    for step in ORDER:
        name, _, which = step.partition(" ")
        if name == "core":
            before = gathers[int(which)].core(before)
        elif name == "grads":
            inputs = after([(chunk.gathered, chunk.arrays) for chunk in chunks], before)
            offsets = tuple(chunk.offset for chunk in chunks)
            grads = weight_grads(offsets, inputs, gate_mask, up_mask, down_mask)
            before = grads[0]
        else:
            before = getattr(chunks[int(which)], name)(before)
    result = jnp.concatenate([chunk.result for chunk in chunks]).astype(jnp.bfloat16)
    return (result[:, :depth], result[:, depth:], *grads)


def solution(mesh):
    in_specs = (
        P("col", "row"),
        P("col", "row"),
        P("row", "col"),
        P("row", "col"),
        P("col", "row"),
        P("row", "col"),
        P("row", "col"),
        P("col", "row"),
    )
    out_specs = (
        P("col", "row"),
        P("col", "row"),
        P("row", "col"),
        P("row", "col"),
        P("col", "row"),
    )
    return jax.shard_map(shards, mesh=mesh, in_specs=in_specs, out_specs=out_specs, check_vma=False)
```

```python
import functools

import jax
import jax.numpy as jnp
from jax import lax
from jax.experimental import pallas as pl
from jax.experimental.pallas import tpu as pltpu
from jax.sharding import PartitionSpec as P

BLK = 128
CHUNKS = (32, 32)
GATHERS = ((0,), (1,))
ORDER = (
    "forward 0",
    "relay 0",
    "core 1",
    "forward 1",
    "swap 0",
    "relay 1",
    "spread 0",
    "swap 1",
    "far 0",
    "spread 1",
    "backward 0",
    "send 0",
    "chip 0",
    "far 1",
    "backward 1",
    "last 0",
    "send 1",
    "chip 1",
    "grads",
    "last 1",
)
SEND_UP = ((2, 0), (1, 1))
SEND_DOWN = ((2, 1), (3, 0))
NEXT_UP = ((1, 0),)
NEXT_DOWN = ((3, 1),)
OWN = ((0, 0), (0, 1))
GROUPS = (SEND_UP, SEND_DOWN, NEXT_UP, NEXT_DOWN, OWN)
GATHERED = tuple((dz, half) for dz in (0, 1, 3, 2) for half in range(2))
VMEM_LIMIT = 24 * 1024 * 1024


def move(array, dy=0, dxh=0, dcore=0, dxl=0, dz=0):
    pairs = []
    for device in range(128):
        row, col = divmod(device, 16)
        x_lo, z = divmod(row, 4)
        y, x_hi, core = col // 4, col // 2 % 2, col % 2
        to_row = (x_lo + dxl) % 2 * 4 + (z + dz) % 4
        to_col = ((y + dy) % 4 * 2 + (x_hi + dxh) % 2) * 2 + (core + dcore) % 2
        pairs.append((device, to_row * 16 + to_col))
    return lax.ppermute(array, ("row", "col"), pairs)


def nn(left, right):
    return lax.dot_general(
        left, right, (((1,), (0,)), ((), ())), preferred_element_type=jnp.float32
    )


def nt(left, right):
    return lax.dot_general(
        left, right, (((1,), (1,)), ((), ())), preferred_element_type=jnp.float32
    )


def tn(left, right):
    return lax.dot_general(
        left, right, (((0,), (0,)), ((), ())), preferred_element_type=jnp.float32
    )


def params():
    return pltpu.CompilerParams(vmem_limit_bytes=VMEM_LIMIT)


def cheap():
    return pl.CostEstimate(flops=1024, bytes_accessed=1024, transcendentals=0)


VMEM = pl.BlockSpec(memory_space=pltpu.VMEM)
SMEM = pl.BlockSpec(memory_space=pltpu.SMEM)


def owner(dz):
    return lax.rem(lax.axis_index("row") + dz, 4)


def tokens_of(kind, gathered, offset, rows, columns):
    return [
        gathered[2 * half + kind][owner(dz), offset : offset + rows, columns]
        for dz, half in GATHERED
    ]


def values_of(arrays, columns):
    own, up, down, far_first, far_second = arrays
    return [array[:, columns] for array in (own, up, down, far_first, far_second)]


def mask_kernel(gate, up, down, gate_mask, up_mask, down_mask, out):
    step = pl.program_id(0)
    width = gate.shape[1]
    down_t = down[...].T
    for j in range(width // BLK):
        at = pl.ds(j * BLK, BLK)
        out[:, at] = gate[:, at] * gate_mask[step, j].astype(jnp.bfloat16)
        to = pl.ds(width + j * BLK, BLK)
        out[:, to] = up[:, at] * up_mask[step, j].astype(jnp.bfloat16)
        to = pl.ds(2 * width + j * BLK, BLK)
        out[:, to] = down_t[:, j * BLK : (j + 1) * BLK] * down_mask[j, step].astype(jnp.bfloat16)


def mask_weights(gate, up, down, gate_mask, up_mask, down_mask):
    depth, width = gate.shape
    return pl.pallas_call(
        mask_kernel,
        grid=(depth // BLK,),
        in_specs=[
            pl.BlockSpec((BLK, width), lambda i: (i, 0)),
            pl.BlockSpec((BLK, width), lambda i: (i, 0)),
            pl.BlockSpec((width, BLK), lambda i: (0, i)),
            SMEM,
            SMEM,
            SMEM,
        ],
        out_specs=pl.BlockSpec((BLK, 3 * width), lambda i: (i, 0)),
        out_shape=jax.ShapeDtypeStruct((depth, 3 * width), jnp.bfloat16),
        compiler_params=params(),
        cost_estimate=pl.CostEstimate(
            flops=3 * depth * width, bytes_accessed=12 * depth * width, transcendentals=0
        ),
        name="mask_weights",
    )(gate, up, down, gate_mask, up_mask, down_mask)


def forward_kernel(offset, rows, *refs):
    gathered, weights, outs = refs[:4], refs[4], refs[5:]
    width = weights.shape[1] // 3
    every = slice(None)
    for at in range(3):
        columns = slice(at * width, (at + 1) * width)
        left = jnp.concatenate(tokens_of(at // 2, gathered, offset, rows, every))
        part = nn(left, weights[:, columns]).astype(jnp.bfloat16)
        for number, piece in enumerate(GATHERED):
            for out, group in zip(outs, GROUPS):
                if piece in group:
                    first = group.index(piece) * rows
                    out[first : first + rows, columns] = part[number * rows : (number + 1) * rows]


def forward(gathered, offset, rows, weights):
    total = weights.shape[1]
    return pl.pallas_call(
        functools.partial(forward_kernel, offset, rows),
        in_specs=[VMEM] * 5,
        out_specs=[VMEM] * len(GROUPS),
        out_shape=[
            jax.ShapeDtypeStruct((len(group) * rows, total), jnp.bfloat16) for group in GROUPS
        ],
        compiler_params=params(),
        cost_estimate=cheap(),
        name="forward",
    )(*gathered, weights)


def backward_kernel(*refs):
    arrays, weights, for_other, for_own = refs[:5], *refs[5:]
    depth, total = weights.shape
    width = total // 3
    rows = for_own.shape[1]
    for columns, to in ((slice(2 * width, total), 0), (slice(0, 2 * width), depth)):
        left = jnp.concatenate(values_of(arrays, columns))
        part = nt(left, weights[:, columns]).astype(jnp.bfloat16)
        for at, (dz, half) in enumerate(GATHERED):
            out = (for_own, for_other)[half]
            out[owner(dz), :, to : to + depth] = part[at * rows : (at + 1) * rows]


def backward(arrays, weights):
    rows = arrays[3].shape[0]
    depth, total = weights.shape
    outs = pl.pallas_call(
        backward_kernel,
        in_specs=[VMEM] * 6,
        out_specs=[VMEM] * 2,
        out_shape=[jax.ShapeDtypeStruct((4, rows, 2 * depth), jnp.bfloat16)] * 2,
        compiler_params=params(),
        cost_estimate=pl.CostEstimate(
            flops=16 * rows * depth * total, bytes_accessed=8 * depth * total, transcendentals=0
        ),
        name="backward",
    )(*arrays, weights)
    return [out.reshape(4 * rows, 2 * depth) for out in outs]


def weight_grad_kernel(offsets, *refs):
    number = 9 * len(offsets)
    gate_mask, up_mask, down_mask, gate_grad, up_grad, down_grad = refs[number:]
    width, depth = down_grad.shape
    every = slice(None)

    def tokens(kind, columns):
        parts = []
        for which, offset in enumerate(offsets):
            chunk = refs[9 * which : 9 * which + 9]
            parts += tokens_of(kind, chunk[:4], offset, chunk[7].shape[0], columns)
        return jnp.concatenate(parts)

    def values(columns):
        parts = []
        for which in range(len(offsets)):
            parts += values_of(refs[9 * which + 4 : 9 * which + 9], columns)
        return jnp.concatenate(parts)

    def store(part, mask, row, out):
        for j in range(part.shape[1] // BLK):
            for i in range(part.shape[0] // BLK):
                block = part[i * BLK : (i + 1) * BLK, j * BLK : (j + 1) * BLK]
                keep = mask[row // BLK + i, j].astype(jnp.bfloat16)
                out[row + i * BLK : row + (i + 1) * BLK, j * BLK : (j + 1) * BLK] = (
                    block.astype(jnp.bfloat16) * keep
                )

    for row in range(0, depth, 256):
        left = tokens(0, slice(row, row + 256))
        store(tn(left, values(slice(0, width))), gate_mask, row, gate_grad)
        store(tn(left, values(slice(width, 2 * width))), up_mask, row, up_grad)
    for row in range(0, width, 256):
        size = min(256, width - row)
        left = values(slice(2 * width + row, 2 * width + row + size))
        store(tn(left, tokens(1, every)), down_mask, row, down_grad)


def weight_grads(offsets, chunks, gate_mask, up_mask, down_mask):
    depth = chunks[0][0][0].shape[-1]
    total = chunks[0][1][0].shape[-1]
    width = total // 3
    count = sum(8 * arrays[3].shape[0] for _, arrays in chunks)
    inputs = [item for gathered, arrays in chunks for item in (*gathered, *arrays)]
    return pl.pallas_call(
        functools.partial(weight_grad_kernel, offsets),
        in_specs=[VMEM] * len(inputs) + [SMEM] * 3,
        out_specs=[VMEM] * 3,
        out_shape=[
            jax.ShapeDtypeStruct((depth, width), jnp.bfloat16),
            jax.ShapeDtypeStruct((depth, width), jnp.bfloat16),
            jax.ShapeDtypeStruct((width, depth), jnp.bfloat16),
        ],
        compiler_params=params(),
        cost_estimate=pl.CostEstimate(
            flops=2 * count * depth * total, bytes_accessed=16 * depth * total, transcendentals=0
        ),
        name="weight_grads",
    )(*inputs, gate_mask, up_mask, down_mask)


def wide(array):
    return array.astype(jnp.float32)


def elementwise(totals):
    width = totals.shape[-1] // 3
    gate = totals[..., :width]
    up_part = totals[..., width : 2 * width]
    hidden_grad = totals[..., 2 * width :]
    sigmoid_gate = jax.nn.sigmoid(gate)
    activated = gate * sigmoid_gate
    hidden = activated * up_part
    gate_delta = hidden_grad * up_part * sigmoid_gate * (1.0 + gate * (1.0 - sigmoid_gate))
    up_delta = hidden_grad * activated
    return jnp.concatenate([gate_delta, up_delta, hidden], axis=-1).astype(jnp.bfloat16)


def after(value, *others):
    return lax.optimization_barrier((value, others))[0]


def chip_sum(for_own, received):
    return (wide(for_own) + wide(received)).astype(jnp.bfloat16)


class Gather:
    def __init__(self, pair):
        self.pair = pair

    def far(self, *others):
        self.pair = after(self.pair, *others)
        self.pairs = [self.pair] + [move(self.pair, dy=-dy) for dy in range(1, 4)]

    def core(self, *others):
        pairs = after(self.pairs, *others)
        own = [jnp.stack([pair[kind] for pair in pairs]) for kind in range(2)]
        self.arrays = (*own, *[move(array, dcore=1) for array in own])
        return own


class Chunk:
    def __init__(self, gather, offset, rows, weights):
        self.source, self.offset, self.rows = gather, offset, 2 * rows
        self.weights = weights

    def forward(self, *others):
        self.gathered = self.source.arrays
        gathered = after(self.gathered, *others)
        outs = forward(gathered, self.offset, self.rows, self.weights)
        self.late_up, self.late_down, self.kept = outs[2:]
        self.from_down = move(outs[0], dz=1)
        self.from_up = move(outs[1], dz=-1)
        return outs[0]

    def relay(self, *others):
        down, up = after((self.from_down, self.from_up), *others)
        rows = self.rows
        send_up = self.late_up + down[:rows]
        send_down = self.late_down + up[:rows]
        self.last_down = move(send_up, dz=1)
        self.last_up = move(send_down, dz=-1)
        self.direct = (up[rows:], down[rows:])
        return send_up, send_down

    def swap(self, *others):
        last_down, last_up = after((self.last_down, self.last_up), *others)
        rows = self.rows
        self.sums = jnp.concatenate(
            [
                wide(self.kept[:rows]) + wide(last_down) + wide(self.direct[0]),
                wide(self.kept[rows:]) + wide(last_up) + wide(self.direct[1]),
            ]
        ).astype(jnp.bfloat16)
        self.partner = move(self.sums, dxl=1)
        return self.sums

    def spread(self, *others):
        partner = after(self.partner, *others)
        self.values = elementwise(wide(self.sums) + wide(partner))
        self.near = (move(self.values, dz=-1), move(self.values, dz=1))
        return self.values

    def far(self, *others):
        up, down = after(self.near, *others)
        sent = down[: self.rows], up[self.rows :]
        self.arrays = (self.values, up, down, move(sent[0], dz=1), move(sent[1], dz=-1))
        return sent

    def backward(self, *others):
        self.arrays = after(self.arrays, *others)
        self.for_other, self.for_own = backward(self.arrays, self.weights)
        return self.for_other

    def send(self, *others):
        for_other = after(self.for_other, *others)
        self.received = move(for_other, dcore=1)
        return for_other

    def chip(self, *others):
        received = after(self.received, *others)
        chip = (wide(self.for_own) + wide(received)).astype(jnp.bfloat16)
        rows = self.rows
        self.parts = [chip[:rows]] + [
            move(chip[dy * rows : (dy + 1) * rows], dy=dy) for dy in range(1, 4)
        ]
        return chip

    def last(self, *others):
        total = sum(wide(part) for part in after(self.parts, *others)).astype(jnp.bfloat16)
        half = self.rows // 2
        self.result = wide(total[:half]) + wide(move(total[half:], dxh=1))
        return total


def shards(tokens, out_grad, gate_weight, up_weight, down_weight, gate_mask, up_mask, down_mask):
    depth = tokens.shape[1]
    starts = [sum(CHUNKS[:i]) for i in range(len(CHUNKS))]
    part = jnp.stack([tokens, out_grad])
    received = move(part, dxh=1)
    weights = mask_weights(gate_weight, up_weight, down_weight, gate_mask, up_mask, down_mask)
    gathers, chunks = [], []
    for group in GATHERS:
        slices = [slice(starts[i], starts[i] + CHUNKS[i]) for i in group]
        gather = Gather(
            jnp.concatenate([half[:, at] for at in slices for half in (part, received)], axis=1)
        )
        gathers.append(gather)
        for i in group:
            offset = 2 * (starts[i] - starts[group[0]])
            chunks.append(Chunk(gather, offset, CHUNKS[i], weights))
    gathers[0].far()
    before = gathers[0].core(weights)
    gathers[1].far(before)
    for step in ORDER:
        name, _, which = step.partition(" ")
        if name == "core":
            before = gathers[int(which)].core(before)
        elif name == "grads":
            inputs = after([(chunk.gathered, chunk.arrays) for chunk in chunks], before)
            offsets = tuple(chunk.offset for chunk in chunks)
            grads = weight_grads(offsets, inputs, gate_mask, up_mask, down_mask)
            before = grads[0]
        else:
            before = getattr(chunks[int(which)], name)(before)
    result = jnp.concatenate([chunk.result for chunk in chunks]).astype(jnp.bfloat16)
    return (result[:, :depth], result[:, depth:], *grads)


def solution(mesh):
    in_specs = (
        P("col", "row"),
        P("col", "row"),
        P("row", "col"),
        P("row", "col"),
        P("col", "row"),
        P("row", "col"),
        P("row", "col"),
        P("col", "row"),
    )
    out_specs = (
        P("col", "row"),
        P("col", "row"),
        P("row", "col"),
        P("row", "col"),
        P("col", "row"),
    )
    return jax.shard_map(shards, mesh=mesh, in_specs=in_specs, out_specs=out_specs, check_vma=False)
```

```python
import functools

import jax
import jax.numpy as jnp
from jax import lax
from jax.experimental import pallas as pl
from jax.experimental.pallas import tpu as pltpu
from jax.sharding import PartitionSpec as P

BLK = 128
CHUNKS = (32, 32)
GATHERS = ((0,), (1,))
ORDER = (
    "forward 0",
    "relay 0",
    "core 1",
    "forward 1",
    "swap 0",
    "relay 1",
    "spread 0",
    "swap 1",
    "far 0",
    "spread 1",
    "backward 0",
    "send 0",
    "far 1",
    "chip 0",
    "backward 1",
    "last 0",
    "send 1",
    "chip 1",
    "grads",
    "last 1",
)
SEND_UP = ((2, 0), (1, 1))
SEND_DOWN = ((2, 1), (3, 0))
NEXT_UP = ((1, 0),)
NEXT_DOWN = ((3, 1),)
OWN = ((0, 0), (0, 1))
GROUPS = (SEND_UP, SEND_DOWN, NEXT_UP, NEXT_DOWN, OWN)
GATHERED = tuple((dz, half) for dz in (0, 1, 3, 2) for half in range(2))
VMEM_LIMIT = 24 * 1024 * 1024


def move(array, dy=0, dxh=0, dcore=0, dxl=0, dz=0):
    pairs = []
    for device in range(128):
        row, col = divmod(device, 16)
        x_lo, z = divmod(row, 4)
        y, x_hi, core = col // 4, col // 2 % 2, col % 2
        to_row = (x_lo + dxl) % 2 * 4 + (z + dz) % 4
        to_col = ((y + dy) % 4 * 2 + (x_hi + dxh) % 2) * 2 + (core + dcore) % 2
        pairs.append((device, to_row * 16 + to_col))
    return lax.ppermute(array, ("row", "col"), pairs)


def nn(left, right):
    return lax.dot_general(
        left, right, (((1,), (0,)), ((), ())), preferred_element_type=jnp.float32
    )


def nt(left, right):
    return lax.dot_general(
        left, right, (((1,), (1,)), ((), ())), preferred_element_type=jnp.float32
    )


def tn(left, right):
    return lax.dot_general(
        left, right, (((0,), (0,)), ((), ())), preferred_element_type=jnp.float32
    )


def params():
    return pltpu.CompilerParams(vmem_limit_bytes=VMEM_LIMIT)


def cheap():
    return pl.CostEstimate(flops=1024, bytes_accessed=1024, transcendentals=0)


VMEM = pl.BlockSpec(memory_space=pltpu.VMEM)
SMEM = pl.BlockSpec(memory_space=pltpu.SMEM)


def owner(dz):
    return lax.rem(lax.axis_index("row") + dz, 4)


def tokens_of(kind, gathered, offset, rows, columns):
    return [
        gathered[2 * half + kind][owner(dz), offset : offset + rows, columns]
        for dz, half in GATHERED
    ]


def values_of(arrays, columns):
    own, up, down, far_first, far_second = arrays
    return [array[:, columns] for array in (own, up, down, far_first, far_second)]


def mask_kernel(gate, up, down, gate_mask, up_mask, down_mask, out):
    step = pl.program_id(0)
    width = gate.shape[1]
    down_t = down[...].T
    for j in range(width // BLK):
        at = pl.ds(j * BLK, BLK)
        out[:, at] = gate[:, at] * gate_mask[step, j].astype(jnp.bfloat16)
        to = pl.ds(width + j * BLK, BLK)
        out[:, to] = up[:, at] * up_mask[step, j].astype(jnp.bfloat16)
        to = pl.ds(2 * width + j * BLK, BLK)
        out[:, to] = down_t[:, j * BLK : (j + 1) * BLK] * down_mask[j, step].astype(jnp.bfloat16)


def mask_weights(gate, up, down, gate_mask, up_mask, down_mask):
    depth, width = gate.shape
    return pl.pallas_call(
        mask_kernel,
        grid=(depth // BLK,),
        in_specs=[
            pl.BlockSpec((BLK, width), lambda i: (i, 0)),
            pl.BlockSpec((BLK, width), lambda i: (i, 0)),
            pl.BlockSpec((width, BLK), lambda i: (0, i)),
            SMEM,
            SMEM,
            SMEM,
        ],
        out_specs=pl.BlockSpec((BLK, 3 * width), lambda i: (i, 0)),
        out_shape=jax.ShapeDtypeStruct((depth, 3 * width), jnp.bfloat16),
        compiler_params=params(),
        cost_estimate=pl.CostEstimate(
            flops=3 * depth * width, bytes_accessed=12 * depth * width, transcendentals=0
        ),
        name="mask_weights",
    )(gate, up, down, gate_mask, up_mask, down_mask)


def forward_kernel(offset, rows, *refs):
    gathered, weights, outs = refs[:4], refs[4], refs[5:]
    width = weights.shape[1] // 3
    every = slice(None)
    for at in range(3):
        columns = slice(at * width, (at + 1) * width)
        left = jnp.concatenate(tokens_of(at // 2, gathered, offset, rows, every))
        part = nn(left, weights[:, columns]).astype(jnp.bfloat16)
        for number, piece in enumerate(GATHERED):
            for out, group in zip(outs, GROUPS):
                if piece in group:
                    first = group.index(piece) * rows
                    out[first : first + rows, columns] = part[number * rows : (number + 1) * rows]


def forward(gathered, offset, rows, weights):
    total = weights.shape[1]
    return pl.pallas_call(
        functools.partial(forward_kernel, offset, rows),
        in_specs=[VMEM] * 5,
        out_specs=[VMEM] * len(GROUPS),
        out_shape=[
            jax.ShapeDtypeStruct((len(group) * rows, total), jnp.bfloat16) for group in GROUPS
        ],
        compiler_params=params(),
        cost_estimate=cheap(),
        name="forward",
    )(*gathered, weights)


def backward_kernel(*refs):
    arrays, weights, outs = refs[:5], refs[5], refs[6:]
    total = weights.shape[1]
    width = total // 3
    rows = arrays[3].shape[0]
    for which, columns in enumerate((slice(2 * width, total), slice(0, 2 * width))):
        left = jnp.concatenate(values_of(arrays, columns))
        part = nt(left, weights[:, columns]).astype(jnp.bfloat16)
        for at, (dz, half) in enumerate(GATHERED):
            outs[2 * half + which][owner(dz)] = part[at * rows : (at + 1) * rows]


def backward(arrays, weights):
    rows = arrays[3].shape[0]
    depth, total = weights.shape
    outs = pl.pallas_call(
        backward_kernel,
        in_specs=[VMEM] * 6,
        out_specs=[VMEM] * 4,
        out_shape=[jax.ShapeDtypeStruct((4, rows, depth), jnp.bfloat16)] * 4,
        compiler_params=params(),
        cost_estimate=pl.CostEstimate(
            flops=16 * rows * depth * total, bytes_accessed=8 * depth * total, transcendentals=0
        ),
        name="backward",
    )(*arrays, weights)
    outs = [out.reshape(4 * rows, depth) for out in outs]
    return outs[2:], outs[:2]


def weight_grad_kernel(offsets, *refs):
    number = 9 * len(offsets)
    gate_mask, up_mask, down_mask, gate_grad, up_grad, down_grad = refs[number:]
    width, depth = down_grad.shape
    every = slice(None)

    def tokens(kind, columns):
        parts = []
        for which, offset in enumerate(offsets):
            chunk = refs[9 * which : 9 * which + 9]
            parts += tokens_of(kind, chunk[:4], offset, chunk[7].shape[0], columns)
        return jnp.concatenate(parts)

    def values(columns):
        parts = []
        for which in range(len(offsets)):
            parts += values_of(refs[9 * which + 4 : 9 * which + 9], columns)
        return jnp.concatenate(parts)

    def store(part, mask, row, out):
        for j in range(part.shape[1] // BLK):
            for i in range(part.shape[0] // BLK):
                block = part[i * BLK : (i + 1) * BLK, j * BLK : (j + 1) * BLK]
                keep = mask[row // BLK + i, j].astype(jnp.bfloat16)
                out[row + i * BLK : row + (i + 1) * BLK, j * BLK : (j + 1) * BLK] = (
                    block.astype(jnp.bfloat16) * keep
                )

    for row in range(0, depth, 256):
        left = tokens(0, slice(row, row + 256))
        store(tn(left, values(slice(0, width))), gate_mask, row, gate_grad)
        store(tn(left, values(slice(width, 2 * width))), up_mask, row, up_grad)
    for row in range(0, width, 256):
        size = min(256, width - row)
        left = values(slice(2 * width + row, 2 * width + row + size))
        store(tn(left, tokens(1, every)), down_mask, row, down_grad)


def weight_grads(offsets, chunks, gate_mask, up_mask, down_mask):
    depth = chunks[0][0][0].shape[-1]
    total = chunks[0][1][0].shape[-1]
    width = total // 3
    count = sum(8 * arrays[3].shape[0] for _, arrays in chunks)
    inputs = [item for gathered, arrays in chunks for item in (*gathered, *arrays)]
    return pl.pallas_call(
        functools.partial(weight_grad_kernel, offsets),
        in_specs=[VMEM] * len(inputs) + [SMEM] * 3,
        out_specs=[VMEM] * 3,
        out_shape=[
            jax.ShapeDtypeStruct((depth, width), jnp.bfloat16),
            jax.ShapeDtypeStruct((depth, width), jnp.bfloat16),
            jax.ShapeDtypeStruct((width, depth), jnp.bfloat16),
        ],
        compiler_params=params(),
        cost_estimate=pl.CostEstimate(
            flops=2 * count * depth * total, bytes_accessed=16 * depth * total, transcendentals=0
        ),
        name="weight_grads",
    )(*inputs, gate_mask, up_mask, down_mask)


def wide(array):
    return array.astype(jnp.float32)


def elementwise(totals):
    width = totals.shape[-1] // 3
    gate = totals[..., :width]
    up_part = totals[..., width : 2 * width]
    hidden_grad = totals[..., 2 * width :]
    sigmoid_gate = jax.nn.sigmoid(gate)
    activated = gate * sigmoid_gate
    hidden = activated * up_part
    gate_delta = hidden_grad * up_part * sigmoid_gate * (1.0 + gate * (1.0 - sigmoid_gate))
    up_delta = hidden_grad * activated
    return jnp.concatenate([gate_delta, up_delta, hidden], axis=-1).astype(jnp.bfloat16)


def after(value, *others):
    return lax.optimization_barrier((value, others))[0]


def chip_sum(for_own, received):
    return (wide(for_own) + wide(received)).astype(jnp.bfloat16)


class Gather:
    def __init__(self, pair):
        self.pair = pair

    def far(self, *others):
        self.pair = after(self.pair, *others)
        self.pairs = [self.pair] + [move(self.pair, dy=-dy) for dy in range(1, 4)]

    def core(self, *others):
        pairs = after(self.pairs, *others)
        own = [jnp.stack([pair[kind] for pair in pairs]) for kind in range(2)]
        self.arrays = (*own, *[move(array, dcore=1) for array in own])
        return own


class Chunk:
    def __init__(self, gather, offset, rows, weights):
        self.source, self.offset, self.rows = gather, offset, 2 * rows
        self.weights = weights

    def forward(self, *others):
        self.gathered = self.source.arrays
        gathered = after(self.gathered, *others)
        outs = forward(gathered, self.offset, self.rows, self.weights)
        self.late_up, self.late_down, self.kept = outs[2:]
        self.from_down = move(outs[0], dz=1)
        self.from_up = move(outs[1], dz=-1)
        return outs[0]

    def relay(self, *others):
        down, up = after((self.from_down, self.from_up), *others)
        rows = self.rows
        send_up = self.late_up + down[:rows]
        send_down = self.late_down + up[:rows]
        self.last_down = move(send_up, dz=1)
        self.last_up = move(send_down, dz=-1)
        self.direct = (up[rows:], down[rows:])
        return send_up, send_down

    def swap(self, *others):
        last_down, last_up = after((self.last_down, self.last_up), *others)
        rows = self.rows
        self.sums = jnp.concatenate(
            [
                wide(self.kept[:rows]) + wide(last_down) + wide(self.direct[0]),
                wide(self.kept[rows:]) + wide(last_up) + wide(self.direct[1]),
            ]
        ).astype(jnp.bfloat16)
        self.partner = move(self.sums, dxl=1)
        return self.sums

    def spread(self, *others):
        partner = after(self.partner, *others)
        self.values = elementwise(wide(self.sums) + wide(partner))
        self.near = (move(self.values, dz=-1), move(self.values, dz=1))
        return self.values

    def far(self, *others):
        up, down = after(self.near, *others)
        sent = down[: self.rows], up[self.rows :]
        self.arrays = (self.values, up, down, move(sent[0], dz=1), move(sent[1], dz=-1))
        return sent

    def backward(self, *others):
        self.arrays = after(self.arrays, *others)
        self.for_other, self.for_own = backward(self.arrays, self.weights)
        return self.for_other

    def send(self, *others):
        for_other = after(self.for_other, *others)
        self.received = [move(part, dcore=1) for part in for_other]
        return for_other

    def chip(self, *others):
        received = after(self.received, *others)
        chip = jnp.concatenate(
            [wide(mine) + wide(theirs) for mine, theirs in zip(self.for_own, received)], axis=1
        ).astype(jnp.bfloat16)
        rows = self.rows
        self.parts = [chip[:rows]] + [
            move(chip[dy * rows : (dy + 1) * rows], dy=dy) for dy in range(1, 4)
        ]
        return chip

    def last(self, *others):
        total = sum(wide(part) for part in after(self.parts, *others)).astype(jnp.bfloat16)
        half = self.rows // 2
        self.result = wide(total[:half]) + wide(move(total[half:], dxh=1))
        return total


def shards(tokens, out_grad, gate_weight, up_weight, down_weight, gate_mask, up_mask, down_mask):
    depth = tokens.shape[1]
    starts = [sum(CHUNKS[:i]) for i in range(len(CHUNKS))]
    weights = mask_weights(gate_weight, up_weight, down_weight, gate_mask, up_mask, down_mask)
    gathers, chunks = [], []
    for group in GATHERS:
        first, last = starts[group[0]], starts[group[-1]] + CHUNKS[group[-1]]
        part = jnp.stack([tokens[first:last], out_grad[first:last]])
        received = move(part, dxh=1)
        slices = [slice(starts[i] - first, starts[i] - first + CHUNKS[i]) for i in group]
        gather = Gather(
            jnp.concatenate([half[:, at] for at in slices for half in (part, received)], axis=1)
        )
        gathers.append(gather)
        for i in group:
            chunks.append(Chunk(gather, 2 * (starts[i] - first), CHUNKS[i], weights))
    gathers[0].far()
    before = gathers[0].core(weights, *[gather.pair for gather in gathers[1:]])
    gathers[1].far(before)
    for step in ORDER:
        name, _, which = step.partition(" ")
        if name == "core":
            before = gathers[int(which)].core(before)
        elif name == "grads":
            inputs = after([(chunk.gathered, chunk.arrays) for chunk in chunks], before)
            offsets = tuple(chunk.offset for chunk in chunks)
            grads = weight_grads(offsets, inputs, gate_mask, up_mask, down_mask)
            before = grads[0]
        else:
            before = getattr(chunks[int(which)], name)(before)
    result = jnp.concatenate([chunk.result for chunk in chunks]).astype(jnp.bfloat16)
    return (result[:, :depth], result[:, depth:], *grads)


def solution(mesh):
    in_specs = (
        P("col", "row"),
        P("col", "row"),
        P("row", "col"),
        P("row", "col"),
        P("col", "row"),
        P("row", "col"),
        P("row", "col"),
        P("col", "row"),
    )
    out_specs = (
        P("col", "row"),
        P("col", "row"),
        P("row", "col"),
        P("row", "col"),
        P("col", "row"),
    )
    return jax.shard_map(shards, mesh=mesh, in_specs=in_specs, out_specs=out_specs, check_vma=False)
```

```python
import functools

import jax
import jax.numpy as jnp
from jax import lax
from jax.experimental import pallas as pl
from jax.experimental.pallas import tpu as pltpu
from jax.sharding import PartitionSpec as P

BLK = 128
CHUNKS = (32, 32)
GATHERS = ((0,), (1,))
ORDER = (
    "forward 0",
    "relay 0",
    "core 1",
    "forward 1",
    "swap 0",
    "relay 1",
    "spread 0",
    "swap 1",
    "far 0",
    "spread 1",
    "backward 0",
    "send 0",
    "far 1",
    "chip 0",
    "backward 1",
    "last 0",
    "send 1",
    "chip 1",
    "grads",
    "last 1",
)
SEND_UP = ((2, 0), (1, 1))
SEND_DOWN = ((2, 1), (3, 0))
NEXT_UP = ((1, 0),)
NEXT_DOWN = ((3, 1),)
OWN = ((0, 0), (0, 1))
GROUPS = (SEND_UP, SEND_DOWN, NEXT_UP, NEXT_DOWN, OWN)
GATHERED = tuple((dz, half) for dz in (0, 1, 3, 2) for half in range(2))
VMEM_LIMIT = 24 * 1024 * 1024


def move(array, dy=0, dxh=0, dcore=0, dxl=0, dz=0):
    pairs = []
    for device in range(128):
        row, col = divmod(device, 16)
        x_lo, z = divmod(row, 4)
        y, x_hi, core = col // 4, col // 2 % 2, col % 2
        to_row = (x_lo + dxl) % 2 * 4 + (z + dz * (1 - 2 * core)) % 4
        to_col = ((y + dy) % 4 * 2 + (x_hi + dxh) % 2) * 2 + (core + dcore) % 2
        pairs.append((device, to_row * 16 + to_col))
    return lax.ppermute(array, ("row", "col"), pairs)


def nn(left, right):
    return lax.dot_general(
        left, right, (((1,), (0,)), ((), ())), preferred_element_type=jnp.float32
    )


def nt(left, right):
    return lax.dot_general(
        left, right, (((1,), (1,)), ((), ())), preferred_element_type=jnp.float32
    )


def tn(left, right):
    return lax.dot_general(
        left, right, (((0,), (0,)), ((), ())), preferred_element_type=jnp.float32
    )


def params():
    return pltpu.CompilerParams(vmem_limit_bytes=VMEM_LIMIT)


def cheap():
    return pl.CostEstimate(flops=1024, bytes_accessed=1024, transcendentals=0)


VMEM = pl.BlockSpec(memory_space=pltpu.VMEM)
SMEM = pl.BlockSpec(memory_space=pltpu.SMEM)


def owner(dz):
    z = lax.rem(lax.axis_index("row"), 4)
    odd = lax.rem(lax.axis_index("col"), 2)
    return lax.rem(z + dz + odd * ((4 - 2 * dz) % 4), 4)


def tokens_of(kind, gathered, offset, rows, columns):
    return [
        gathered[2 * half + kind][owner(dz), offset : offset + rows, columns]
        for dz, half in GATHERED
    ]


def values_of(arrays, columns):
    own, up, down, far_first, far_second = arrays
    return [array[:, columns] for array in (own, up, down, far_first, far_second)]


def mask_kernel(gate, up, down, gate_mask, up_mask, down_mask, out):
    step = pl.program_id(0)
    width = gate.shape[1]
    down_t = down[...].T
    for j in range(width // BLK):
        at = pl.ds(j * BLK, BLK)
        out[:, at] = gate[:, at] * gate_mask[step, j].astype(jnp.bfloat16)
        to = pl.ds(width + j * BLK, BLK)
        out[:, to] = up[:, at] * up_mask[step, j].astype(jnp.bfloat16)
        to = pl.ds(2 * width + j * BLK, BLK)
        out[:, to] = down_t[:, j * BLK : (j + 1) * BLK] * down_mask[j, step].astype(jnp.bfloat16)


def mask_weights(gate, up, down, gate_mask, up_mask, down_mask):
    depth, width = gate.shape
    return pl.pallas_call(
        mask_kernel,
        grid=(depth // BLK,),
        in_specs=[
            pl.BlockSpec((BLK, width), lambda i: (i, 0)),
            pl.BlockSpec((BLK, width), lambda i: (i, 0)),
            pl.BlockSpec((width, BLK), lambda i: (0, i)),
            SMEM,
            SMEM,
            SMEM,
        ],
        out_specs=pl.BlockSpec((BLK, 3 * width), lambda i: (i, 0)),
        out_shape=jax.ShapeDtypeStruct((depth, 3 * width), jnp.bfloat16),
        compiler_params=params(),
        cost_estimate=pl.CostEstimate(
            flops=3 * depth * width, bytes_accessed=12 * depth * width, transcendentals=0
        ),
        name="mask_weights",
    )(gate, up, down, gate_mask, up_mask, down_mask)


def forward_kernel(offset, rows, *refs):
    gathered, weights, outs = refs[:4], refs[4], refs[5:]
    width = weights.shape[1] // 3
    every = slice(None)
    for at in range(3):
        columns = slice(at * width, (at + 1) * width)
        left = jnp.concatenate(tokens_of(at // 2, gathered, offset, rows, every))
        part = nn(left, weights[:, columns]).astype(jnp.bfloat16)
        for number, piece in enumerate(GATHERED):
            for out, group in zip(outs, GROUPS):
                if piece in group:
                    first = group.index(piece) * rows
                    out[first : first + rows, columns] = part[number * rows : (number + 1) * rows]


def forward(gathered, offset, rows, weights):
    total = weights.shape[1]
    return pl.pallas_call(
        functools.partial(forward_kernel, offset, rows),
        in_specs=[VMEM] * 5,
        out_specs=[VMEM] * len(GROUPS),
        out_shape=[
            jax.ShapeDtypeStruct((len(group) * rows, total), jnp.bfloat16) for group in GROUPS
        ],
        compiler_params=params(),
        cost_estimate=cheap(),
        name="forward",
    )(*gathered, weights)


def backward_kernel(*refs):
    arrays, weights, outs = refs[:5], refs[5], refs[6:]
    total = weights.shape[1]
    width = total // 3
    rows = arrays[3].shape[0]
    for which, columns in enumerate((slice(2 * width, total), slice(0, 2 * width))):
        left = jnp.concatenate(values_of(arrays, columns))
        part = nt(left, weights[:, columns]).astype(jnp.bfloat16)
        for at, (dz, half) in enumerate(GATHERED):
            outs[2 * half + which][owner(dz)] = part[at * rows : (at + 1) * rows]


def backward(arrays, weights):
    rows = arrays[3].shape[0]
    depth, total = weights.shape
    outs = pl.pallas_call(
        backward_kernel,
        in_specs=[VMEM] * 6,
        out_specs=[VMEM] * 4,
        out_shape=[jax.ShapeDtypeStruct((4, rows, depth), jnp.bfloat16)] * 4,
        compiler_params=params(),
        cost_estimate=pl.CostEstimate(
            flops=16 * rows * depth * total, bytes_accessed=8 * depth * total, transcendentals=0
        ),
        name="backward",
    )(*arrays, weights)
    outs = [out.reshape(4 * rows, depth) for out in outs]
    return outs[2:], outs[:2]


def weight_grad_kernel(offsets, *refs):
    number = 9 * len(offsets)
    gate_mask, up_mask, down_mask, gate_grad, up_grad, down_grad = refs[number:]
    width, depth = down_grad.shape
    every = slice(None)

    def tokens(kind, columns):
        parts = []
        for which, offset in enumerate(offsets):
            chunk = refs[9 * which : 9 * which + 9]
            parts += tokens_of(kind, chunk[:4], offset, chunk[7].shape[0], columns)
        return jnp.concatenate(parts)

    def values(columns):
        parts = []
        for which in range(len(offsets)):
            parts += values_of(refs[9 * which + 4 : 9 * which + 9], columns)
        return jnp.concatenate(parts)

    def store(part, mask, row, out):
        for j in range(part.shape[1] // BLK):
            for i in range(part.shape[0] // BLK):
                block = part[i * BLK : (i + 1) * BLK, j * BLK : (j + 1) * BLK]
                keep = mask[row // BLK + i, j].astype(jnp.bfloat16)
                out[row + i * BLK : row + (i + 1) * BLK, j * BLK : (j + 1) * BLK] = (
                    block.astype(jnp.bfloat16) * keep
                )

    for row in range(0, depth, 256):
        left = tokens(0, slice(row, row + 256))
        store(tn(left, values(slice(0, width))), gate_mask, row, gate_grad)
        store(tn(left, values(slice(width, 2 * width))), up_mask, row, up_grad)
    for row in range(0, width, 256):
        size = min(256, width - row)
        left = values(slice(2 * width + row, 2 * width + row + size))
        store(tn(left, tokens(1, every)), down_mask, row, down_grad)


def weight_grads(offsets, chunks, gate_mask, up_mask, down_mask):
    depth = chunks[0][0][0].shape[-1]
    total = chunks[0][1][0].shape[-1]
    width = total // 3
    count = sum(8 * arrays[3].shape[0] for _, arrays in chunks)
    inputs = [item for gathered, arrays in chunks for item in (*gathered, *arrays)]
    return pl.pallas_call(
        functools.partial(weight_grad_kernel, offsets),
        in_specs=[VMEM] * len(inputs) + [SMEM] * 3,
        out_specs=[VMEM] * 3,
        out_shape=[
            jax.ShapeDtypeStruct((depth, width), jnp.bfloat16),
            jax.ShapeDtypeStruct((depth, width), jnp.bfloat16),
            jax.ShapeDtypeStruct((width, depth), jnp.bfloat16),
        ],
        compiler_params=params(),
        cost_estimate=pl.CostEstimate(
            flops=2 * count * depth * total, bytes_accessed=16 * depth * total, transcendentals=0
        ),
        name="weight_grads",
    )(*inputs, gate_mask, up_mask, down_mask)


def wide(array):
    return array.astype(jnp.float32)


def elementwise(totals):
    width = totals.shape[-1] // 3
    gate = totals[..., :width]
    up_part = totals[..., width : 2 * width]
    hidden_grad = totals[..., 2 * width :]
    sigmoid_gate = jax.nn.sigmoid(gate)
    activated = gate * sigmoid_gate
    hidden = activated * up_part
    gate_delta = hidden_grad * up_part * sigmoid_gate * (1.0 + gate * (1.0 - sigmoid_gate))
    up_delta = hidden_grad * activated
    return jnp.concatenate([gate_delta, up_delta, hidden], axis=-1).astype(jnp.bfloat16)


def after(value, *others):
    return lax.optimization_barrier((value, others))[0]


def chip_sum(for_own, received):
    return (wide(for_own) + wide(received)).astype(jnp.bfloat16)


class Gather:
    def __init__(self, pair):
        self.pair = pair

    def far(self, *others):
        self.pair = after(self.pair, *others)
        self.pairs = [self.pair] + [move(self.pair, dy=-dy) for dy in range(1, 4)]

    def core(self, *others):
        pairs = after(self.pairs, *others)
        own = [jnp.stack([pair[kind] for pair in pairs]) for kind in range(2)]
        self.arrays = (*own, *[move(array, dcore=1) for array in own])
        return own


class Chunk:
    def __init__(self, gather, offset, rows, weights):
        self.source, self.offset, self.rows = gather, offset, 2 * rows
        self.weights = weights

    def forward(self, *others):
        self.gathered = self.source.arrays
        gathered = after(self.gathered, *others)
        outs = forward(gathered, self.offset, self.rows, self.weights)
        self.late_up, self.late_down, self.kept = outs[2:]
        self.from_down = move(outs[0], dz=1)
        self.from_up = move(outs[1], dz=-1)
        return outs[0]

    def relay(self, *others):
        rows = self.rows
        down = after(self.from_down, *others)
        send_up = self.late_up + down[:rows]
        self.last_down = move(send_up, dz=1)
        up = after(self.from_up, send_up)
        send_down = self.late_down + up[:rows]
        self.last_up = move(send_down, dz=-1)
        self.direct = (up[rows:], down[rows:])
        return send_up, send_down

    def swap(self, *others):
        last_down, last_up = after((self.last_down, self.last_up), *others)
        rows = self.rows
        self.sums = jnp.concatenate(
            [
                wide(self.kept[:rows]) + wide(last_down) + wide(self.direct[0]),
                wide(self.kept[rows:]) + wide(last_up) + wide(self.direct[1]),
            ]
        ).astype(jnp.bfloat16)
        self.partner = move(self.sums, dxl=1)
        return self.sums

    def spread(self, *others):
        partner = after(self.partner, *others)
        self.values = elementwise(wide(self.sums) + wide(partner))
        from_down = move(self.values, dz=1)
        self.near = (move(self.values, dz=-1), from_down)
        return self.values

    def far(self, *others):
        down = after(self.near[1], *others)
        sent_up = down[: self.rows]
        up = after(self.near[0], sent_up)
        sent_down = up[self.rows :]
        self.arrays = (self.values, up, down, move(sent_up, dz=1), move(sent_down, dz=-1))
        return sent_up, sent_down

    def backward(self, *others):
        self.arrays = after(self.arrays, *others)
        self.for_other, self.for_own = backward(self.arrays, self.weights)
        return self.for_other

    def send(self, *others):
        for_other = after(self.for_other, *others)
        self.received = [move(part, dcore=1) for part in for_other]
        return for_other

    def chip(self, *others):
        received = after(self.received, *others)
        chip = jnp.concatenate(
            [wide(mine) + wide(theirs) for mine, theirs in zip(self.for_own, received)], axis=1
        ).astype(jnp.bfloat16)
        rows = self.rows
        self.parts = [chip[:rows]] + [
            move(chip[dy * rows : (dy + 1) * rows], dy=dy) for dy in range(1, 4)
        ]
        return chip

    def last(self, *others):
        total = sum(wide(part) for part in after(self.parts, *others)).astype(jnp.bfloat16)
        half = self.rows // 2
        self.result = wide(total[:half]) + wide(move(total[half:], dxh=1))
        return total


def shards(tokens, out_grad, gate_weight, up_weight, down_weight, gate_mask, up_mask, down_mask):
    depth = tokens.shape[1]
    starts = [sum(CHUNKS[:i]) for i in range(len(CHUNKS))]
    weights = mask_weights(gate_weight, up_weight, down_weight, gate_mask, up_mask, down_mask)
    gathers, chunks = [], []
    for group in GATHERS:
        first, last = starts[group[0]], starts[group[-1]] + CHUNKS[group[-1]]
        part = jnp.stack([tokens[first:last], out_grad[first:last]])
        received = move(part, dxh=1)
        slices = [slice(starts[i] - first, starts[i] - first + CHUNKS[i]) for i in group]
        gather = Gather(
            jnp.concatenate([half[:, at] for at in slices for half in (part, received)], axis=1)
        )
        gathers.append(gather)
        for i in group:
            chunks.append(Chunk(gather, 2 * (starts[i] - first), CHUNKS[i], weights))
    gathers[0].far()
    before = gathers[0].core(weights, *[gather.pair for gather in gathers[1:]])
    gathers[1].far(before)
    for step in ORDER:
        name, _, which = step.partition(" ")
        if name == "core":
            before = gathers[int(which)].core(before)
        elif name == "grads":
            inputs = after([(chunk.gathered, chunk.arrays) for chunk in chunks], before)
            offsets = tuple(chunk.offset for chunk in chunks)
            grads = weight_grads(offsets, inputs, gate_mask, up_mask, down_mask)
            before = grads[0]
        else:
            before = getattr(chunks[int(which)], name)(before)
    result = jnp.concatenate([chunk.result for chunk in chunks]).astype(jnp.bfloat16)
    return (result[:, :depth], result[:, depth:], *grads)


def solution(mesh):
    in_specs = (
        P("col", "row"),
        P("col", "row"),
        P("row", "col"),
        P("row", "col"),
        P("col", "row"),
        P("row", "col"),
        P("row", "col"),
        P("col", "row"),
    )
    out_specs = (
        P("col", "row"),
        P("col", "row"),
        P("row", "col"),
        P("row", "col"),
        P("col", "row"),
    )
    return jax.shard_map(shards, mesh=mesh, in_specs=in_specs, out_specs=out_specs, check_vma=False)
```

```python
import functools

import jax
import jax.numpy as jnp
from jax import lax
from jax.experimental import pallas as pl
from jax.experimental.pallas import tpu as pltpu
from jax.sharding import PartitionSpec as P

BLK = 128
CHUNKS = (32, 32)
GATHERS = ((0,), (1,))
ORDER = (
    "forward 0",
    "relay_up 0",
    "core 1",
    "forward 1",
    "relay_down 0",
    "swap 0",
    "relay_up 1",
    "relay_down 1",
    "spread 0",
    "swap 1",
    "far 0",
    "spread 1",
    "backward 0",
    "send 0",
    "far 1",
    "chip 0",
    "backward 1",
    "send 1",
    "last 0",
    "chip 1",
    "grads",
    "last 1",
)
SEND_UP = ((2, 0), (1, 1))
SEND_DOWN = ((2, 1), (3, 0))
NEXT_UP = ((1, 0),)
NEXT_DOWN = ((3, 1),)
OWN = ((0, 0), (0, 1))
GROUPS = (SEND_UP, SEND_DOWN, NEXT_UP, NEXT_DOWN, OWN)
GATHERED = tuple((dz, half) for dz in (0, 1, 3, 2) for half in range(2))
VMEM_LIMIT = 24 * 1024 * 1024


def move(array, dy=0, dxh=0, dcore=0, dxl=0, dz=0):
    pairs = []
    for device in range(128):
        row, col = divmod(device, 16)
        x_lo, z = divmod(row, 4)
        y, x_hi, core = col // 4, col // 2 % 2, col % 2
        to_row = (x_lo + dxl) % 2 * 4 + (z + dz * (1 - 2 * core)) % 4
        to_col = ((y + dy) % 4 * 2 + (x_hi + dxh) % 2) * 2 + (core + dcore) % 2
        pairs.append((device, to_row * 16 + to_col))
    return lax.ppermute(array, ("row", "col"), pairs)


def nn(left, right):
    return lax.dot_general(
        left, right, (((1,), (0,)), ((), ())), preferred_element_type=jnp.float32
    )


def nt(left, right):
    return lax.dot_general(
        left, right, (((1,), (1,)), ((), ())), preferred_element_type=jnp.float32
    )


def tn(left, right):
    return lax.dot_general(
        left, right, (((0,), (0,)), ((), ())), preferred_element_type=jnp.float32
    )


def params():
    return pltpu.CompilerParams(vmem_limit_bytes=VMEM_LIMIT)


def cheap():
    return pl.CostEstimate(flops=1024, bytes_accessed=1024, transcendentals=0)


VMEM = pl.BlockSpec(memory_space=pltpu.VMEM)
SMEM = pl.BlockSpec(memory_space=pltpu.SMEM)


def owner(dz):
    z = lax.rem(lax.axis_index("row"), 4)
    odd = lax.rem(lax.axis_index("col"), 2)
    return lax.rem(z + dz + odd * ((4 - 2 * dz) % 4), 4)


def tokens_of(kind, gathered, offset, rows, columns):
    return [
        gathered[2 * half + kind][owner(dz), offset : offset + rows, columns]
        for dz, half in GATHERED
    ]


def values_of(arrays, columns):
    own, up, down, far_first, far_second = arrays
    return [array[:, columns] for array in (own, up, down, far_first, far_second)]


def mask_kernel(gate, up, down, gate_mask, up_mask, down_mask, out):
    step = pl.program_id(0)
    width = gate.shape[1]
    down_t = down[...].T
    for j in range(width // BLK):
        at = pl.ds(j * BLK, BLK)
        out[:, at] = gate[:, at] * gate_mask[step, j].astype(jnp.bfloat16)
        to = pl.ds(width + j * BLK, BLK)
        out[:, to] = up[:, at] * up_mask[step, j].astype(jnp.bfloat16)
        to = pl.ds(2 * width + j * BLK, BLK)
        out[:, to] = down_t[:, j * BLK : (j + 1) * BLK] * down_mask[j, step].astype(jnp.bfloat16)


def mask_weights(gate, up, down, gate_mask, up_mask, down_mask):
    depth, width = gate.shape
    return pl.pallas_call(
        mask_kernel,
        grid=(depth // BLK,),
        in_specs=[
            pl.BlockSpec((BLK, width), lambda i: (i, 0)),
            pl.BlockSpec((BLK, width), lambda i: (i, 0)),
            pl.BlockSpec((width, BLK), lambda i: (0, i)),
            SMEM,
            SMEM,
            SMEM,
        ],
        out_specs=pl.BlockSpec((BLK, 3 * width), lambda i: (i, 0)),
        out_shape=jax.ShapeDtypeStruct((depth, 3 * width), jnp.bfloat16),
        compiler_params=params(),
        cost_estimate=pl.CostEstimate(
            flops=3 * depth * width, bytes_accessed=12 * depth * width, transcendentals=0
        ),
        name="mask_weights",
    )(gate, up, down, gate_mask, up_mask, down_mask)


def forward_kernel(offset, rows, *refs):
    gathered, weights, outs = refs[:4], refs[4], refs[5:]
    width = weights.shape[1] // 3
    every = slice(None)
    for at in range(3):
        columns = slice(at * width, (at + 1) * width)
        left = jnp.concatenate(tokens_of(at // 2, gathered, offset, rows, every))
        part = nn(left, weights[:, columns]).astype(jnp.bfloat16)
        for number, piece in enumerate(GATHERED):
            for out, group in zip(outs, GROUPS):
                if piece in group:
                    first = group.index(piece) * rows
                    out[first : first + rows, columns] = part[number * rows : (number + 1) * rows]


def forward(gathered, offset, rows, weights):
    total = weights.shape[1]
    return pl.pallas_call(
        functools.partial(forward_kernel, offset, rows),
        in_specs=[VMEM] * 5,
        out_specs=[VMEM] * len(GROUPS),
        out_shape=[
            jax.ShapeDtypeStruct((len(group) * rows, total), jnp.bfloat16) for group in GROUPS
        ],
        compiler_params=params(),
        cost_estimate=cheap(),
        name="forward",
    )(*gathered, weights)


def backward_kernel(*refs):
    arrays, weights, outs = refs[:5], refs[5], refs[6:]
    total = weights.shape[1]
    width = total // 3
    rows = arrays[3].shape[0]
    for which, columns in enumerate((slice(2 * width, total), slice(0, 2 * width))):
        left = jnp.concatenate(values_of(arrays, columns))
        part = nt(left, weights[:, columns]).astype(jnp.bfloat16)
        for at, (dz, half) in enumerate(GATHERED):
            outs[2 * half + which][owner(dz)] = part[at * rows : (at + 1) * rows]


def backward(arrays, weights):
    rows = arrays[3].shape[0]
    depth, total = weights.shape
    outs = pl.pallas_call(
        backward_kernel,
        in_specs=[VMEM] * 6,
        out_specs=[VMEM] * 4,
        out_shape=[jax.ShapeDtypeStruct((4, rows, depth), jnp.bfloat16)] * 4,
        compiler_params=params(),
        cost_estimate=pl.CostEstimate(
            flops=16 * rows * depth * total, bytes_accessed=8 * depth * total, transcendentals=0
        ),
        name="backward",
    )(*arrays, weights)
    outs = [out.reshape(4 * rows, depth) for out in outs]
    return outs[2:], outs[:2]


def weight_grad_kernel(offsets, *refs):
    number = 9 * len(offsets)
    gate_mask, up_mask, down_mask, gate_grad, up_grad, down_grad = refs[number:]
    width, depth = down_grad.shape
    every = slice(None)

    def tokens(kind, columns):
        parts = []
        for which, offset in enumerate(offsets):
            chunk = refs[9 * which : 9 * which + 9]
            parts += tokens_of(kind, chunk[:4], offset, chunk[7].shape[0], columns)
        return jnp.concatenate(parts)

    def values(columns):
        parts = []
        for which in range(len(offsets)):
            parts += values_of(refs[9 * which + 4 : 9 * which + 9], columns)
        return jnp.concatenate(parts)

    def store(part, mask, row, out):
        for j in range(part.shape[1] // BLK):
            for i in range(part.shape[0] // BLK):
                block = part[i * BLK : (i + 1) * BLK, j * BLK : (j + 1) * BLK]
                keep = mask[row // BLK + i, j].astype(jnp.bfloat16)
                out[row + i * BLK : row + (i + 1) * BLK, j * BLK : (j + 1) * BLK] = (
                    block.astype(jnp.bfloat16) * keep
                )

    for row in range(0, depth, 256):
        left = tokens(0, slice(row, row + 256))
        store(tn(left, values(slice(0, width))), gate_mask, row, gate_grad)
        store(tn(left, values(slice(width, 2 * width))), up_mask, row, up_grad)
    for row in range(0, width, 256):
        size = min(256, width - row)
        left = values(slice(2 * width + row, 2 * width + row + size))
        store(tn(left, tokens(1, every)), down_mask, row, down_grad)


def weight_grads(offsets, chunks, gate_mask, up_mask, down_mask):
    depth = chunks[0][0][0].shape[-1]
    total = chunks[0][1][0].shape[-1]
    width = total // 3
    count = sum(8 * arrays[3].shape[0] for _, arrays in chunks)
    inputs = [item for gathered, arrays in chunks for item in (*gathered, *arrays)]
    return pl.pallas_call(
        functools.partial(weight_grad_kernel, offsets),
        in_specs=[VMEM] * len(inputs) + [SMEM] * 3,
        out_specs=[VMEM] * 3,
        out_shape=[
            jax.ShapeDtypeStruct((depth, width), jnp.bfloat16),
            jax.ShapeDtypeStruct((depth, width), jnp.bfloat16),
            jax.ShapeDtypeStruct((width, depth), jnp.bfloat16),
        ],
        compiler_params=params(),
        cost_estimate=pl.CostEstimate(
            flops=2 * count * depth * total, bytes_accessed=16 * depth * total, transcendentals=0
        ),
        name="weight_grads",
    )(*inputs, gate_mask, up_mask, down_mask)


def wide(array):
    return array.astype(jnp.float32)


def elementwise(totals):
    width = totals.shape[-1] // 3
    gate = totals[..., :width]
    up_part = totals[..., width : 2 * width]
    hidden_grad = totals[..., 2 * width :]
    sigmoid_gate = jax.nn.sigmoid(gate)
    activated = gate * sigmoid_gate
    hidden = activated * up_part
    gate_delta = hidden_grad * up_part * sigmoid_gate * (1.0 + gate * (1.0 - sigmoid_gate))
    up_delta = hidden_grad * activated
    return jnp.concatenate([gate_delta, up_delta, hidden], axis=-1).astype(jnp.bfloat16)


def after(value, *others):
    return lax.optimization_barrier((value, others))[0]


def chip_sum(for_own, received):
    return (wide(for_own) + wide(received)).astype(jnp.bfloat16)


class Gather:
    def __init__(self, pair):
        self.pair = pair

    def far(self, *others):
        self.pair = after(self.pair, *others)
        self.pairs = [self.pair] + [move(self.pair, dy=-dy) for dy in range(1, 4)]

    def core(self, *others):
        pairs = after(self.pairs, *others)
        own = [jnp.stack([pair[kind] for pair in pairs]) for kind in range(2)]
        self.arrays = (*own, *[move(array, dcore=1) for array in own])
        return own


class Chunk:
    def __init__(self, gather, offset, rows, weights):
        self.source, self.offset, self.rows = gather, offset, 2 * rows
        self.weights = weights

    def forward(self, *others):
        self.gathered = self.source.arrays
        gathered = after(self.gathered, *others)
        outs = forward(gathered, self.offset, self.rows, self.weights)
        self.late_up, self.late_down, self.kept = outs[2:]
        self.from_down = move(outs[0], dz=1)
        self.from_up = move(outs[1], dz=-1)
        return outs[0]

    def relay_up(self, *others):
        down = after(self.from_down, *others)
        send_up = self.late_up + down[: self.rows]
        self.last_down = move(send_up, dz=1)
        self.direct_down = down[self.rows :]
        return send_up

    def relay_down(self, *others):
        up = after(self.from_up, *others)
        send_down = self.late_down + up[: self.rows]
        self.last_up = move(send_down, dz=-1)
        self.direct = (up[self.rows :], self.direct_down)
        return send_down

    def swap(self, *others):
        last_down, last_up = after((self.last_down, self.last_up), *others)
        rows = self.rows
        self.sums = jnp.concatenate(
            [
                wide(self.kept[:rows]) + wide(last_down) + wide(self.direct[0]),
                wide(self.kept[rows:]) + wide(last_up) + wide(self.direct[1]),
            ]
        ).astype(jnp.bfloat16)
        self.partner = move(self.sums, dxl=1)
        return self.sums

    def spread(self, *others):
        partner = after(self.partner, *others)
        self.values = elementwise(wide(self.sums) + wide(partner))
        from_down = move(self.values, dz=1)
        self.near = (move(self.values, dz=-1), from_down)
        return self.values

    def far(self, *others):
        down = after(self.near[1], *others)
        sent_up = down[: self.rows]
        up = after(self.near[0], sent_up)
        sent_down = up[self.rows :]
        self.arrays = (self.values, up, down, move(sent_up, dz=1), move(sent_down, dz=-1))
        return sent_up, sent_down

    def backward(self, *others):
        self.arrays = after(self.arrays, *others)
        self.for_other, self.for_own = backward(self.arrays, self.weights)
        return self.for_other

    def send(self, *others):
        for_other = after(self.for_other, *others)
        self.received = [move(part, dcore=1) for part in for_other]
        return for_other

    def chip(self, *others):
        received = after(self.received, *others)
        chip = jnp.concatenate(
            [wide(mine) + wide(theirs) for mine, theirs in zip(self.for_own, received)], axis=1
        ).astype(jnp.bfloat16)
        rows = self.rows
        self.parts = [chip[:rows]] + [
            move(chip[dy * rows : (dy + 1) * rows], dy=dy) for dy in range(1, 4)
        ]
        return chip

    def last(self, *others):
        total = sum(wide(part) for part in after(self.parts, *others)).astype(jnp.bfloat16)
        half = self.rows // 2
        self.result = wide(total[:half]) + wide(move(total[half:], dxh=1))
        return total


def shards(tokens, out_grad, gate_weight, up_weight, down_weight, gate_mask, up_mask, down_mask):
    depth = tokens.shape[1]
    starts = [sum(CHUNKS[:i]) for i in range(len(CHUNKS))]
    weights = mask_weights(gate_weight, up_weight, down_weight, gate_mask, up_mask, down_mask)
    gathers, chunks = [], []
    for group in GATHERS:
        first, last = starts[group[0]], starts[group[-1]] + CHUNKS[group[-1]]
        part = jnp.stack([tokens[first:last], out_grad[first:last]])
        received = move(part, dxh=1)
        slices = [slice(starts[i] - first, starts[i] - first + CHUNKS[i]) for i in group]
        gather = Gather(
            jnp.concatenate([half[:, at] for at in slices for half in (part, received)], axis=1)
        )
        gathers.append(gather)
        for i in group:
            chunks.append(Chunk(gather, 2 * (starts[i] - first), CHUNKS[i], weights))
    gathers[0].far()
    before = gathers[0].core(weights, *[gather.pair for gather in gathers[1:]])
    gathers[1].far(before)
    for step in ORDER:
        name, _, which = step.partition(" ")
        if name == "core":
            before = gathers[int(which)].core(before)
        elif name == "grads":
            inputs = after([(chunk.gathered, chunk.arrays) for chunk in chunks], before)
            offsets = tuple(chunk.offset for chunk in chunks)
            grads = weight_grads(offsets, inputs, gate_mask, up_mask, down_mask)
            before = grads[0]
        else:
            before = getattr(chunks[int(which)], name)(before)
    result = jnp.concatenate([chunk.result for chunk in chunks]).astype(jnp.bfloat16)
    return (result[:, :depth], result[:, depth:], *grads)


def solution(mesh):
    in_specs = (
        P("col", "row"),
        P("col", "row"),
        P("row", "col"),
        P("row", "col"),
        P("col", "row"),
        P("row", "col"),
        P("row", "col"),
        P("col", "row"),
    )
    out_specs = (
        P("col", "row"),
        P("col", "row"),
        P("row", "col"),
        P("row", "col"),
        P("col", "row"),
    )
    return jax.shard_map(shards, mesh=mesh, in_specs=in_specs, out_specs=out_specs, check_vma=False)
```

```python
import functools

import jax
import jax.numpy as jnp
from jax import lax
from jax.experimental import pallas as pl
from jax.experimental.pallas import tpu as pltpu
from jax.sharding import PartitionSpec as P

BLK = 128
CHUNKS = (32, 32)
GATHERS = ((0,), (1,))
ORDER = (
    "forward 0",
    "relay 0",
    "core 1",
    "forward 1",
    "swap 0",
    "relay 1",
    "spread 0",
    "swap 1",
    "far 0",
    "spread 1",
    "backward 0",
    "send 0",
    "far 1",
    "chip 0",
    "backward 1",
    "send 1",
    "last 0",
    "chip 1",
    "grads",
    "last 1",
)
SEND_UP = ((2, 0), (1, 1))
SEND_DOWN = ((2, 1), (3, 0))
NEXT_UP = ((1, 0),)
NEXT_DOWN = ((3, 1),)
OWN = ((0, 0), (0, 1))
GROUPS = (SEND_UP, SEND_DOWN, NEXT_UP, NEXT_DOWN, OWN)
GATHERED = tuple((dz, half) for dz in (0, 1, 3, 2) for half in range(2))
VMEM_LIMIT = 24 * 1024 * 1024


def move(array, dy=0, dxh=0, dcore=0, dxl=0, dz=0):
    pairs = []
    for device in range(128):
        row, col = divmod(device, 16)
        x_lo, z = divmod(row, 4)
        y, x_hi, core = col // 4, col // 2 % 2, col % 2
        to_row = (x_lo + dxl) % 2 * 4 + (z + dz * (1 - 2 * core)) % 4
        to_col = ((y + dy) % 4 * 2 + (x_hi + dxh) % 2) * 2 + (core + dcore) % 2
        pairs.append((device, to_row * 16 + to_col))
    return lax.ppermute(array, ("row", "col"), pairs)


def nn(left, right):
    return lax.dot_general(
        left, right, (((1,), (0,)), ((), ())), preferred_element_type=jnp.float32
    )


def nt(left, right):
    return lax.dot_general(
        left, right, (((1,), (1,)), ((), ())), preferred_element_type=jnp.float32
    )


def tn(left, right):
    return lax.dot_general(
        left, right, (((0,), (0,)), ((), ())), preferred_element_type=jnp.float32
    )


def params():
    return pltpu.CompilerParams(vmem_limit_bytes=VMEM_LIMIT)


def cheap():
    return pl.CostEstimate(flops=1024, bytes_accessed=1024, transcendentals=0)


VMEM = pl.BlockSpec(memory_space=pltpu.VMEM)
SMEM = pl.BlockSpec(memory_space=pltpu.SMEM)


def owner(dz):
    z = lax.rem(lax.axis_index("row"), 4)
    odd = lax.rem(lax.axis_index("col"), 2)
    return lax.rem(z + dz + odd * ((4 - 2 * dz) % 4), 4)


def tokens_of(kind, gathered, offset, rows, columns):
    return [
        gathered[2 * half + kind][owner(dz), offset : offset + rows, columns]
        for dz, half in GATHERED
    ]


def values_of(arrays, columns):
    own, up, down, far_first, far_second = arrays
    return [array[:, columns] for array in (own, up, down, far_first, far_second)]


def mask_kernel(gate, up, down, gate_mask, up_mask, down_mask, out):
    step = pl.program_id(0)
    width = gate.shape[1]
    down_t = down[...].T
    for j in range(width // BLK):
        at = pl.ds(j * BLK, BLK)
        out[:, at] = gate[:, at] * gate_mask[step, j].astype(jnp.bfloat16)
        to = pl.ds(width + j * BLK, BLK)
        out[:, to] = up[:, at] * up_mask[step, j].astype(jnp.bfloat16)
        to = pl.ds(2 * width + j * BLK, BLK)
        out[:, to] = down_t[:, j * BLK : (j + 1) * BLK] * down_mask[j, step].astype(jnp.bfloat16)


def mask_weights(gate, up, down, gate_mask, up_mask, down_mask):
    depth, width = gate.shape
    return pl.pallas_call(
        mask_kernel,
        grid=(depth // BLK,),
        in_specs=[
            pl.BlockSpec((BLK, width), lambda i: (i, 0)),
            pl.BlockSpec((BLK, width), lambda i: (i, 0)),
            pl.BlockSpec((width, BLK), lambda i: (0, i)),
            SMEM,
            SMEM,
            SMEM,
        ],
        out_specs=pl.BlockSpec((BLK, 3 * width), lambda i: (i, 0)),
        out_shape=jax.ShapeDtypeStruct((depth, 3 * width), jnp.bfloat16),
        compiler_params=params(),
        cost_estimate=pl.CostEstimate(
            flops=3 * depth * width, bytes_accessed=12 * depth * width, transcendentals=0
        ),
        name="mask_weights",
    )(gate, up, down, gate_mask, up_mask, down_mask)


def forward_kernel(offset, rows, *refs):
    gathered, weights, outs = refs[:4], refs[4], refs[5:]
    width = weights.shape[1] // 3
    every = slice(None)
    for at in range(3):
        columns = slice(at * width, (at + 1) * width)
        left = jnp.concatenate(tokens_of(at // 2, gathered, offset, rows, every))
        part = nn(left, weights[:, columns]).astype(jnp.bfloat16)
        for number, piece in enumerate(GATHERED):
            for out, group in zip(outs, GROUPS):
                if piece in group:
                    first = group.index(piece) * rows
                    out[first : first + rows, columns] = part[number * rows : (number + 1) * rows]


def forward(gathered, offset, rows, weights):
    total = weights.shape[1]
    return pl.pallas_call(
        functools.partial(forward_kernel, offset, rows),
        in_specs=[VMEM] * 5,
        out_specs=[VMEM] * len(GROUPS),
        out_shape=[
            jax.ShapeDtypeStruct((len(group) * rows, total), jnp.bfloat16) for group in GROUPS
        ],
        compiler_params=params(),
        cost_estimate=cheap(),
        name="forward",
    )(*gathered, weights)


def backward_kernel(*refs):
    arrays, weights, outs = refs[:5], refs[5], refs[6:]
    total = weights.shape[1]
    width = total // 3
    rows = arrays[3].shape[0]
    for which, columns in enumerate((slice(2 * width, total), slice(0, 2 * width))):
        left = jnp.concatenate(values_of(arrays, columns))
        part = nt(left, weights[:, columns]).astype(jnp.bfloat16)
        for at, (dz, half) in enumerate(GATHERED):
            outs[2 * half + which][owner(dz)] = part[at * rows : (at + 1) * rows]


def backward(arrays, weights):
    rows = arrays[3].shape[0]
    depth, total = weights.shape
    outs = pl.pallas_call(
        backward_kernel,
        in_specs=[VMEM] * 6,
        out_specs=[VMEM] * 4,
        out_shape=[jax.ShapeDtypeStruct((4, rows, depth), jnp.bfloat16)] * 4,
        compiler_params=params(),
        cost_estimate=pl.CostEstimate(
            flops=16 * rows * depth * total, bytes_accessed=8 * depth * total, transcendentals=0
        ),
        name="backward",
    )(*arrays, weights)
    outs = [out.reshape(4 * rows, depth) for out in outs]
    return outs[2:], outs[:2]


def weight_grad_kernel(offsets, *refs):
    number = 9 * len(offsets)
    gate_mask, up_mask, down_mask, gate_grad, up_grad, down_grad = refs[number:]
    width, depth = down_grad.shape
    every = slice(None)

    def tokens(kind, columns):
        parts = []
        for which, offset in enumerate(offsets):
            chunk = refs[9 * which : 9 * which + 9]
            parts += tokens_of(kind, chunk[:4], offset, chunk[7].shape[0], columns)
        return jnp.concatenate(parts)

    def values(columns):
        parts = []
        for which in range(len(offsets)):
            parts += values_of(refs[9 * which + 4 : 9 * which + 9], columns)
        return jnp.concatenate(parts)

    def store(part, mask, row, out):
        for j in range(part.shape[1] // BLK):
            for i in range(part.shape[0] // BLK):
                block = part[i * BLK : (i + 1) * BLK, j * BLK : (j + 1) * BLK]
                keep = mask[row // BLK + i, j].astype(jnp.bfloat16)
                out[row + i * BLK : row + (i + 1) * BLK, j * BLK : (j + 1) * BLK] = (
                    block.astype(jnp.bfloat16) * keep
                )

    for row in range(0, depth, 256):
        left = tokens(0, slice(row, row + 256))
        store(tn(left, values(slice(0, width))), gate_mask, row, gate_grad)
        store(tn(left, values(slice(width, 2 * width))), up_mask, row, up_grad)
    for row in range(0, width, 256):
        size = min(256, width - row)
        left = values(slice(2 * width + row, 2 * width + row + size))
        store(tn(left, tokens(1, every)), down_mask, row, down_grad)


def weight_grads(offsets, chunks, gate_mask, up_mask, down_mask):
    depth = chunks[0][0][0].shape[-1]
    total = chunks[0][1][0].shape[-1]
    width = total // 3
    count = sum(8 * arrays[3].shape[0] for _, arrays in chunks)
    inputs = [item for gathered, arrays in chunks for item in (*gathered, *arrays)]
    return pl.pallas_call(
        functools.partial(weight_grad_kernel, offsets),
        in_specs=[VMEM] * len(inputs) + [SMEM] * 3,
        out_specs=[VMEM] * 3,
        out_shape=[
            jax.ShapeDtypeStruct((depth, width), jnp.bfloat16),
            jax.ShapeDtypeStruct((depth, width), jnp.bfloat16),
            jax.ShapeDtypeStruct((width, depth), jnp.bfloat16),
        ],
        compiler_params=params(),
        cost_estimate=pl.CostEstimate(
            flops=2 * count * depth * total, bytes_accessed=16 * depth * total, transcendentals=0
        ),
        name="weight_grads",
    )(*inputs, gate_mask, up_mask, down_mask)


def wide(array):
    return array.astype(jnp.float32)


def elementwise(totals):
    width = totals.shape[-1] // 3
    gate = totals[..., :width]
    up_part = totals[..., width : 2 * width]
    hidden_grad = totals[..., 2 * width :]
    sigmoid_gate = jax.nn.sigmoid(gate)
    activated = gate * sigmoid_gate
    hidden = activated * up_part
    gate_delta = hidden_grad * up_part * sigmoid_gate * (1.0 + gate * (1.0 - sigmoid_gate))
    up_delta = hidden_grad * activated
    return jnp.concatenate([gate_delta, up_delta, hidden], axis=-1).astype(jnp.bfloat16)


def after(value, *others):
    return lax.optimization_barrier((value, others))[0]


def chip_sum(for_own, received):
    return (wide(for_own) + wide(received)).astype(jnp.bfloat16)


class Gather:
    def __init__(self, pair):
        self.pair = pair

    def far(self, *others):
        self.pair = after(self.pair, *others)
        self.pairs = [self.pair] + [move(self.pair, dy=-dy) for dy in range(1, 4)]

    def core(self, *others):
        pairs = after(self.pairs, *others)
        own = [jnp.stack([pair[kind] for pair in pairs]) for kind in range(2)]
        self.arrays = (*own, *[move(array, dcore=1) for array in own])
        return own


class Chunk:
    def __init__(self, gather, offset, rows, weights):
        self.source, self.offset, self.rows = gather, offset, 2 * rows
        self.weights = weights

    def forward(self, *others):
        self.gathered = self.source.arrays
        gathered = after(self.gathered, *others)
        outs = forward(gathered, self.offset, self.rows, self.weights)
        self.late_up, self.late_down, self.kept = outs[2:]
        self.from_down = move(outs[0], dz=1)
        self.from_up = move(outs[1], dz=-1)
        return outs[0]

    def relay(self, *others):
        rows = self.rows
        down = after(self.from_down, *others)
        send_up = self.late_up + down[:rows]
        self.last_down = move(send_up, dz=1)
        up = after(self.from_up, send_up)
        send_down = self.late_down + up[:rows]
        self.last_up = move(send_down, dz=-1)
        self.direct = (up[rows:], down[rows:])
        return send_up, send_down

    def swap(self, *others):
        last_down, last_up = after((self.last_down, self.last_up), *others)
        rows = self.rows
        self.sums = jnp.concatenate(
            [
                wide(self.kept[:rows]) + wide(last_down) + wide(self.direct[0]),
                wide(self.kept[rows:]) + wide(last_up) + wide(self.direct[1]),
            ]
        ).astype(jnp.bfloat16)
        self.partner = move(self.sums, dxl=1)
        return self.sums

    def spread(self, *others):
        partner = after(self.partner, *others)
        self.values = elementwise(wide(self.sums) + wide(partner))
        from_down = move(self.values, dz=1)
        self.near = (move(self.values, dz=-1), from_down)
        return self.values

    def far(self, *others):
        down = after(self.near[1], *others)
        sent_up = down[: self.rows]
        up = after(self.near[0], sent_up)
        sent_down = up[self.rows :]
        self.arrays = (self.values, up, down, move(sent_up, dz=1), move(sent_down, dz=-1))
        return sent_up, sent_down

    def backward(self, *others):
        self.arrays = after(self.arrays, *others)
        self.for_other, self.for_own = backward(self.arrays, self.weights)
        return self.for_other

    def send(self, *others):
        for_other = after(self.for_other, *others)
        self.received = [move(part, dcore=1) for part in for_other]
        return for_other

    def chip(self, *others):
        received = after(self.received, *others)
        chip = jnp.concatenate(
            [wide(mine) + wide(theirs) for mine, theirs in zip(self.for_own, received)], axis=1
        ).astype(jnp.bfloat16)
        rows = self.rows
        self.parts = [chip[:rows]] + [
            move(chip[dy * rows : (dy + 1) * rows], dy=dy) for dy in range(1, 4)
        ]
        return chip

    def last(self, *others):
        total = sum(wide(part) for part in after(self.parts, *others)).astype(jnp.bfloat16)
        half = self.rows // 2
        self.result = wide(total[:half]) + wide(move(total[half:], dxh=1))
        return total


def shards(tokens, out_grad, gate_weight, up_weight, down_weight, gate_mask, up_mask, down_mask):
    depth = tokens.shape[1]
    starts = [sum(CHUNKS[:i]) for i in range(len(CHUNKS))]
    weights = mask_weights(gate_weight, up_weight, down_weight, gate_mask, up_mask, down_mask)
    gathers, chunks = [], []
    for group in GATHERS:
        first, last = starts[group[0]], starts[group[-1]] + CHUNKS[group[-1]]
        part = jnp.stack([tokens[first:last], out_grad[first:last]])
        received = move(part, dxh=1)
        slices = [slice(starts[i] - first, starts[i] - first + CHUNKS[i]) for i in group]
        gather = Gather(
            jnp.concatenate([half[:, at] for at in slices for half in (part, received)], axis=1)
        )
        gathers.append(gather)
        for i in group:
            chunks.append(Chunk(gather, 2 * (starts[i] - first), CHUNKS[i], weights))
    gathers[0].far()
    before = gathers[0].core(weights, *[gather.pair for gather in gathers[1:]])
    gathers[1].far(before)
    for step in ORDER:
        name, _, which = step.partition(" ")
        if name == "core":
            before = gathers[int(which)].core(before)
        elif name == "grads":
            inputs = after([(chunk.gathered, chunk.arrays) for chunk in chunks], before)
            offsets = tuple(chunk.offset for chunk in chunks)
            grads = weight_grads(offsets, inputs, gate_mask, up_mask, down_mask)
            before = grads[0]
        else:
            before = getattr(chunks[int(which)], name)(before)
    result = jnp.concatenate([chunk.result for chunk in chunks]).astype(jnp.bfloat16)
    return (result[:, :depth], result[:, depth:], *grads)


def solution(mesh):
    in_specs = (
        P("col", "row"),
        P("col", "row"),
        P("row", "col"),
        P("row", "col"),
        P("col", "row"),
        P("row", "col"),
        P("row", "col"),
        P("col", "row"),
    )
    out_specs = (
        P("col", "row"),
        P("col", "row"),
        P("row", "col"),
        P("row", "col"),
        P("col", "row"),
    )
    return jax.shard_map(shards, mesh=mesh, in_specs=in_specs, out_specs=out_specs, check_vma=False)
```

```python
import functools

import jax
import jax.numpy as jnp
from jax import lax
from jax.experimental import pallas as pl
from jax.experimental.pallas import tpu as pltpu
from jax.sharding import PartitionSpec as P

BLK = 128
CHUNKS = (32, 32)
GATHERS = ((0,), (1,))
ORDER = (
    "forward 0",
    "relay 0",
    "core 1",
    "forward 1",
    "swap 0",
    "relay 1",
    "spread 0",
    "swap 1",
    "far 0",
    "spread 1",
    "backward 0",
    "send 0",
    "far 1",
    "chip 0",
    "backward 1",
    "send 1",
    "last 0",
    "chip 1",
    "grads",
    "last 1",
)
SEND_UP = ((2, 0), (1, 1))
SEND_DOWN = ((2, 1), (3, 0))
NEXT_UP = ((1, 0),)
NEXT_DOWN = ((3, 1),)
OWN = ((0, 0), (0, 1))
TOGETHER = ((SEND_UP, SEND_DOWN, NEXT_UP, NEXT_DOWN, OWN),)
APART = ((SEND_UP, SEND_DOWN), (NEXT_UP, NEXT_DOWN, OWN))
GATHERED = tuple((dz, half) for dz in (0, 1, 3, 2) for half in range(2))
VMEM_LIMIT = 24 * 1024 * 1024


def move(array, dy=0, dxh=0, dcore=0, dxl=0, dz=0):
    pairs = []
    for device in range(128):
        row, col = divmod(device, 16)
        x_lo, z = divmod(row, 4)
        y, x_hi, core = col // 4, col // 2 % 2, col % 2
        to_row = (x_lo + dxl) % 2 * 4 + (z + dz * (1 - 2 * core)) % 4
        to_col = ((y + dy) % 4 * 2 + (x_hi + dxh) % 2) * 2 + (core + dcore) % 2
        pairs.append((device, to_row * 16 + to_col))
    return lax.ppermute(array, ("row", "col"), pairs)


def nn(left, right):
    return lax.dot_general(
        left, right, (((1,), (0,)), ((), ())), preferred_element_type=jnp.float32
    )


def nt(left, right):
    return lax.dot_general(
        left, right, (((1,), (1,)), ((), ())), preferred_element_type=jnp.float32
    )


def tn(left, right):
    return lax.dot_general(
        left, right, (((0,), (0,)), ((), ())), preferred_element_type=jnp.float32
    )


def params():
    return pltpu.CompilerParams(vmem_limit_bytes=VMEM_LIMIT)


def cheap():
    return pl.CostEstimate(flops=1024, bytes_accessed=1024, transcendentals=0)


VMEM = pl.BlockSpec(memory_space=pltpu.VMEM)
SMEM = pl.BlockSpec(memory_space=pltpu.SMEM)


def owner(dz):
    z = lax.rem(lax.axis_index("row"), 4)
    odd = lax.rem(lax.axis_index("col"), 2)
    return lax.rem(z + dz + odd * ((4 - 2 * dz) % 4), 4)


def tokens_of(kind, gathered, offset, rows, columns, pieces):
    return [
        gathered[2 * half + kind][owner(dz), offset : offset + rows, columns]
        for dz, half in pieces
    ]


def values_of(arrays, columns):
    own, up, down, far_first, far_second = arrays
    return [array[:, columns] for array in (own, up, down, far_first, far_second)]


def mask_kernel(gate, up, down, gate_mask, up_mask, down_mask, out):
    step = pl.program_id(0)
    width = gate.shape[1]
    down_t = down[...].T
    for j in range(width // BLK):
        at = pl.ds(j * BLK, BLK)
        out[:, at] = gate[:, at] * gate_mask[step, j].astype(jnp.bfloat16)
        to = pl.ds(width + j * BLK, BLK)
        out[:, to] = up[:, at] * up_mask[step, j].astype(jnp.bfloat16)
        to = pl.ds(2 * width + j * BLK, BLK)
        out[:, to] = down_t[:, j * BLK : (j + 1) * BLK] * down_mask[j, step].astype(jnp.bfloat16)


def mask_weights(gate, up, down, gate_mask, up_mask, down_mask):
    depth, width = gate.shape
    return pl.pallas_call(
        mask_kernel,
        grid=(depth // BLK,),
        in_specs=[
            pl.BlockSpec((BLK, width), lambda i: (i, 0)),
            pl.BlockSpec((BLK, width), lambda i: (i, 0)),
            pl.BlockSpec((width, BLK), lambda i: (0, i)),
            SMEM,
            SMEM,
            SMEM,
        ],
        out_specs=pl.BlockSpec((BLK, 3 * width), lambda i: (i, 0)),
        out_shape=jax.ShapeDtypeStruct((depth, 3 * width), jnp.bfloat16),
        compiler_params=params(),
        cost_estimate=pl.CostEstimate(
            flops=3 * depth * width, bytes_accessed=12 * depth * width, transcendentals=0
        ),
        name="mask_weights",
    )(gate, up, down, gate_mask, up_mask, down_mask)


def forward_kernel(groups, offset, rows, *refs):
    gathered, weights, outs = refs[:4], refs[4], refs[5:]
    width = weights.shape[1] // 3
    pieces = [piece for group in groups for piece in group]
    for at in range(3):
        columns = slice(at * width, (at + 1) * width)
        left = jnp.concatenate(
            tokens_of(at // 2, gathered, offset, rows, slice(None), pieces)
        )
        part = nn(left, weights[:, columns]).astype(jnp.bfloat16)
        first = 0
        for out, group in zip(outs, groups):
            size = len(group) * rows
            out[:, columns] = part[first : first + size]
            first += size


def forward(groups, gathered, offset, rows, weights):
    total = weights.shape[1]
    return pl.pallas_call(
        functools.partial(forward_kernel, groups, offset, rows),
        in_specs=[VMEM] * 5,
        out_specs=[VMEM] * len(groups),
        out_shape=[
            jax.ShapeDtypeStruct((len(group) * rows, total), jnp.bfloat16) for group in groups
        ],
        compiler_params=params(),
        cost_estimate=cheap(),
        name="forward",
    )(*gathered, weights)


def backward_kernel(halves, *refs):
    arrays, weights, outs = refs[:5], refs[5], refs[6:]
    own, up, down, far_first, far_second = arrays
    total = weights.shape[1]
    width = total // 3
    rows = far_first.shape[0]
    for which, columns in enumerate((slice(2 * width, total), slice(0, 2 * width))):
        left = []
        for half in halves:
            at = slice(half * rows, (half + 1) * rows)
            left += [array[at, columns] for array in (own, up, down)]
            left.append((far_first, far_second)[half][:, columns])
        part = nt(jnp.concatenate(left), weights[:, columns]).astype(jnp.bfloat16)
        for at in range(len(halves)):
            for number, dz in enumerate((0, 1, 3, 2)):
                first = (4 * at + number) * rows
                outs[2 * at + which][owner(dz)] = part[first : first + rows]


def backward(halves, arrays, weights):
    rows = arrays[3].shape[0]
    depth, total = weights.shape
    count = 2 * len(halves)
    outs = pl.pallas_call(
        functools.partial(backward_kernel, halves),
        in_specs=[VMEM] * 6,
        out_specs=[VMEM] * count,
        out_shape=[jax.ShapeDtypeStruct((4, rows, depth), jnp.bfloat16)] * count,
        compiler_params=params(),
        cost_estimate=pl.CostEstimate(
            flops=4 * count * rows * depth * total,
            bytes_accessed=8 * depth * total,
            transcendentals=0,
        ),
        name="backward",
    )(*arrays, weights)
    return [out.reshape(4 * rows, depth) for out in outs]


def weight_grad_kernel(offsets, *refs):
    number = 9 * len(offsets)
    gate_mask, up_mask, down_mask, gate_grad, up_grad, down_grad = refs[number:]
    width, depth = down_grad.shape
    every = slice(None)

    def tokens(kind, columns):
        parts = []
        for which, offset in enumerate(offsets):
            chunk = refs[9 * which : 9 * which + 9]
            parts += tokens_of(kind, chunk[:4], offset, chunk[7].shape[0], columns, GATHERED)
        return jnp.concatenate(parts)

    def values(columns):
        parts = []
        for which in range(len(offsets)):
            parts += values_of(refs[9 * which + 4 : 9 * which + 9], columns)
        return jnp.concatenate(parts)

    def store(part, mask, row, out):
        for j in range(part.shape[1] // BLK):
            for i in range(part.shape[0] // BLK):
                block = part[i * BLK : (i + 1) * BLK, j * BLK : (j + 1) * BLK]
                keep = mask[row // BLK + i, j].astype(jnp.bfloat16)
                out[row + i * BLK : row + (i + 1) * BLK, j * BLK : (j + 1) * BLK] = (
                    block.astype(jnp.bfloat16) * keep
                )

    for row in range(0, depth, 256):
        left = tokens(0, slice(row, row + 256))
        store(tn(left, values(slice(0, width))), gate_mask, row, gate_grad)
        store(tn(left, values(slice(width, 2 * width))), up_mask, row, up_grad)
    for row in range(0, width, 256):
        size = min(256, width - row)
        left = values(slice(2 * width + row, 2 * width + row + size))
        store(tn(left, tokens(1, every)), down_mask, row, down_grad)


def weight_grads(offsets, chunks, gate_mask, up_mask, down_mask):
    depth = chunks[0][0][0].shape[-1]
    total = chunks[0][1][0].shape[-1]
    width = total // 3
    count = sum(8 * arrays[3].shape[0] for _, arrays in chunks)
    inputs = [item for gathered, arrays in chunks for item in (*gathered, *arrays)]
    return pl.pallas_call(
        functools.partial(weight_grad_kernel, offsets),
        in_specs=[VMEM] * len(inputs) + [SMEM] * 3,
        out_specs=[VMEM] * 3,
        out_shape=[
            jax.ShapeDtypeStruct((depth, width), jnp.bfloat16),
            jax.ShapeDtypeStruct((depth, width), jnp.bfloat16),
            jax.ShapeDtypeStruct((width, depth), jnp.bfloat16),
        ],
        compiler_params=params(),
        cost_estimate=pl.CostEstimate(
            flops=2 * count * depth * total, bytes_accessed=16 * depth * total, transcendentals=0
        ),
        name="weight_grads",
    )(*inputs, gate_mask, up_mask, down_mask)


def wide(array):
    return array.astype(jnp.float32)


def elementwise(totals):
    width = totals.shape[-1] // 3
    gate = totals[..., :width]
    up_part = totals[..., width : 2 * width]
    hidden_grad = totals[..., 2 * width :]
    sigmoid_gate = jax.nn.sigmoid(gate)
    activated = gate * sigmoid_gate
    hidden = activated * up_part
    gate_delta = hidden_grad * up_part * sigmoid_gate * (1.0 + gate * (1.0 - sigmoid_gate))
    up_delta = hidden_grad * activated
    return jnp.concatenate([gate_delta, up_delta, hidden], axis=-1).astype(jnp.bfloat16)


def after(value, *others):
    return lax.optimization_barrier((value, others))[0]


def chip_sum(for_own, received):
    return (wide(for_own) + wide(received)).astype(jnp.bfloat16)


class Gather:
    def __init__(self, pair):
        self.pair = pair

    def far(self, *others):
        self.pair = after(self.pair, *others)
        self.pairs = [self.pair] + [move(self.pair, dy=-dy) for dy in range(1, 4)]

    def core(self, *others):
        pairs = after(self.pairs, *others)
        own = [jnp.stack([pair[kind] for pair in pairs]) for kind in range(2)]
        self.arrays = (*own, *[move(array, dcore=1) for array in own])
        return own


class Chunk:
    def __init__(self, gather, offset, rows, weights, last):
        self.source, self.offset, self.rows = gather, offset, 2 * rows
        self.weights = weights
        self.groups = TOGETHER if last else APART
        self.halves = ((1,), (0,)) if last else ((1, 0),)

    def forward(self, *others):
        self.gathered = self.source.arrays
        gathered = after(self.gathered, *others)
        outs = []
        for groups in self.groups:
            outs += forward(groups, gathered, self.offset, self.rows, self.weights)
        self.late_up, self.late_down, self.kept = outs[2:]
        self.from_down = move(outs[0], dz=1)
        self.from_up = move(outs[1], dz=-1)
        return outs[0]

    def relay(self, *others):
        rows = self.rows
        down = after(self.from_down, *others)
        send_up = self.late_up + down[:rows]
        self.last_down = move(send_up, dz=1)
        up = after(self.from_up, send_up)
        send_down = self.late_down + up[:rows]
        self.last_up = move(send_down, dz=-1)
        self.direct = (up[rows:], down[rows:])
        return send_up, send_down

    def swap(self, *others):
        last_down, last_up = after((self.last_down, self.last_up), *others)
        rows = self.rows
        self.sums = jnp.concatenate(
            [
                wide(self.kept[:rows]) + wide(last_down) + wide(self.direct[0]),
                wide(self.kept[rows:]) + wide(last_up) + wide(self.direct[1]),
            ]
        ).astype(jnp.bfloat16)
        self.partner = move(self.sums, dxl=1)
        return self.sums

    def spread(self, *others):
        partner = after(self.partner, *others)
        self.values = elementwise(wide(self.sums) + wide(partner))
        from_down = move(self.values, dz=1)
        self.near = (move(self.values, dz=-1), from_down)
        return self.values

    def far(self, *others):
        down = after(self.near[1], *others)
        sent_up = down[: self.rows]
        up = after(self.near[0], sent_up)
        sent_down = up[self.rows :]
        self.arrays = (self.values, up, down, move(sent_up, dz=1), move(sent_down, dz=-1))
        return sent_up, sent_down

    def backward(self, *others):
        self.arrays = after(self.arrays, *others)
        outs = []
        for halves in self.halves:
            outs += backward(halves, self.arrays, self.weights)
        self.for_other, self.for_own = outs[:2], outs[2:]
        return self.for_other

    def send(self, *others):
        for_other = after(self.for_other, *others)
        self.received = [move(part, dcore=1) for part in for_other]
        return for_other

    def chip(self, *others):
        received = after(self.received, *others)
        chip = jnp.concatenate(
            [wide(mine) + wide(theirs) for mine, theirs in zip(self.for_own, received)], axis=1
        ).astype(jnp.bfloat16)
        rows = self.rows
        self.parts = [chip[:rows]] + [
            move(chip[dy * rows : (dy + 1) * rows], dy=dy) for dy in range(1, 4)
        ]
        return chip

    def last(self, *others):
        total = sum(wide(part) for part in after(self.parts, *others)).astype(jnp.bfloat16)
        half = self.rows // 2
        self.result = wide(total[:half]) + wide(move(total[half:], dxh=1))
        return total


def shards(tokens, out_grad, gate_weight, up_weight, down_weight, gate_mask, up_mask, down_mask):
    depth = tokens.shape[1]
    starts = [sum(CHUNKS[:i]) for i in range(len(CHUNKS))]
    weights = mask_weights(gate_weight, up_weight, down_weight, gate_mask, up_mask, down_mask)
    gathers, chunks = [], []
    for group in GATHERS:
        first, last = starts[group[0]], starts[group[-1]] + CHUNKS[group[-1]]
        part = jnp.stack([tokens[first:last], out_grad[first:last]])
        received = move(part, dxh=1)
        slices = [slice(starts[i] - first, starts[i] - first + CHUNKS[i]) for i in group]
        gather = Gather(
            jnp.concatenate([half[:, at] for at in slices for half in (part, received)], axis=1)
        )
        gathers.append(gather)
        for i in group:
            chunks.append(Chunk(gather, 2 * (starts[i] - first), CHUNKS[i], weights, i == len(CHUNKS) - 1))
    gathers[0].far()
    before = gathers[0].core(weights, *[gather.pair for gather in gathers[1:]])
    gathers[1].far(before)
    for step in ORDER:
        name, _, which = step.partition(" ")
        if name == "core":
            before = gathers[int(which)].core(before)
        elif name == "grads":
            inputs = after([(chunk.gathered, chunk.arrays) for chunk in chunks], before)
            offsets = tuple(chunk.offset for chunk in chunks)
            grads = weight_grads(offsets, inputs, gate_mask, up_mask, down_mask)
            before = grads[0]
        else:
            before = getattr(chunks[int(which)], name)(before)
    result = jnp.concatenate([chunk.result for chunk in chunks]).astype(jnp.bfloat16)
    return (result[:, :depth], result[:, depth:], *grads)


def solution(mesh):
    in_specs = (
        P("col", "row"),
        P("col", "row"),
        P("row", "col"),
        P("row", "col"),
        P("col", "row"),
        P("row", "col"),
        P("row", "col"),
        P("col", "row"),
    )
    out_specs = (
        P("col", "row"),
        P("col", "row"),
        P("row", "col"),
        P("row", "col"),
        P("col", "row"),
    )
    return jax.shard_map(shards, mesh=mesh, in_specs=in_specs, out_specs=out_specs, check_vma=False)
```

```python
import functools

import jax
import jax.numpy as jnp
from jax import lax
from jax.experimental import pallas as pl
from jax.experimental.pallas import tpu as pltpu
from jax.sharding import PartitionSpec as P

BLK = 128
CHUNKS = (32, 32)
GATHERS = ((0,), (1,))
ORDER = (
    "forward 0",
    "relay 0",
    "core 1",
    "forward 1",
    "swap 0",
    "relay 1",
    "spread 0",
    "swap 1",
    "far 0",
    "spread 1",
    "backward 0",
    "send 0",
    "far 1",
    "chip 0",
    "backward 1",
    "send 1",
    "last 0",
    "chip 1",
    "grads",
    "last 1",
)
SEND_UP = ((2, 0), (1, 1))
SEND_DOWN = ((2, 1), (3, 0))
NEXT_UP = ((1, 0),)
NEXT_DOWN = ((3, 1),)
OWN = ((0, 0), (0, 1))
TOGETHER = ((SEND_UP, SEND_DOWN, NEXT_UP, NEXT_DOWN, OWN),)
APART = ((SEND_UP, SEND_DOWN), (NEXT_UP, NEXT_DOWN, OWN))
GATHERED = tuple((dz, half) for dz in (0, 1, 3, 2) for half in range(2))
VMEM_LIMIT = 24 * 1024 * 1024


def move(array, dy=0, dxh=0, dcore=0, dxl=0, dz=0):
    pairs = []
    for device in range(128):
        row, col = divmod(device, 16)
        x_lo, z = divmod(row, 4)
        y, x_hi, core = col // 4, col // 2 % 2, col % 2
        to_row = (x_lo + dxl) % 2 * 4 + (z + dz * (1 - 2 * core)) % 4
        to_col = ((y + dy) % 4 * 2 + (x_hi + dxh) % 2) * 2 + (core + dcore) % 2
        pairs.append((device, to_row * 16 + to_col))
    return lax.ppermute(array, ("row", "col"), pairs)


def nn(left, right):
    return lax.dot_general(
        left, right, (((1,), (0,)), ((), ())), preferred_element_type=jnp.float32
    )


def nt(left, right):
    return lax.dot_general(
        left, right, (((1,), (1,)), ((), ())), preferred_element_type=jnp.float32
    )


def tn(left, right):
    return lax.dot_general(
        left, right, (((0,), (0,)), ((), ())), preferred_element_type=jnp.float32
    )


def params():
    return pltpu.CompilerParams(vmem_limit_bytes=VMEM_LIMIT)


def cheap():
    return pl.CostEstimate(flops=1024, bytes_accessed=1024, transcendentals=0)


VMEM = pl.BlockSpec(memory_space=pltpu.VMEM)
SMEM = pl.BlockSpec(memory_space=pltpu.SMEM)


def owner(dz):
    z = lax.rem(lax.axis_index("row"), 4)
    odd = lax.rem(lax.axis_index("col"), 2)
    return lax.rem(z + dz + odd * ((4 - 2 * dz) % 4), 4)


def tokens_of(kind, gathered, offset, rows, columns, pieces):
    return [
        gathered[2 * half + kind][owner(dz), offset : offset + rows, columns]
        for dz, half in pieces
    ]


def values_of(arrays, columns):
    own, up, down, far_first, far_second = arrays
    return [array[:, columns] for array in (own, up, down, far_first, far_second)]


def mask_kernel(gate, up, down, gate_mask, up_mask, down_mask, out):
    step = pl.program_id(0)
    width = gate.shape[1]
    down_t = down[...].T
    for j in range(width // BLK):
        at = pl.ds(j * BLK, BLK)
        out[:, at] = gate[:, at] * gate_mask[step, j].astype(jnp.bfloat16)
        to = pl.ds(width + j * BLK, BLK)
        out[:, to] = up[:, at] * up_mask[step, j].astype(jnp.bfloat16)
        to = pl.ds(2 * width + j * BLK, BLK)
        out[:, to] = down_t[:, j * BLK : (j + 1) * BLK] * down_mask[j, step].astype(jnp.bfloat16)


def mask_weights(gate, up, down, gate_mask, up_mask, down_mask):
    depth, width = gate.shape
    return pl.pallas_call(
        mask_kernel,
        grid=(depth // BLK,),
        in_specs=[
            pl.BlockSpec((BLK, width), lambda i: (i, 0)),
            pl.BlockSpec((BLK, width), lambda i: (i, 0)),
            pl.BlockSpec((width, BLK), lambda i: (0, i)),
            SMEM,
            SMEM,
            SMEM,
        ],
        out_specs=pl.BlockSpec((BLK, 3 * width), lambda i: (i, 0)),
        out_shape=jax.ShapeDtypeStruct((depth, 3 * width), jnp.bfloat16),
        compiler_params=params(),
        cost_estimate=pl.CostEstimate(
            flops=3 * depth * width, bytes_accessed=12 * depth * width, transcendentals=0
        ),
        name="mask_weights",
    )(gate, up, down, gate_mask, up_mask, down_mask)


def forward_kernel(groups, offset, rows, *refs):
    gathered, weights, outs = refs[:4], refs[4], refs[5:]
    width = weights.shape[1] // 3
    pieces = [piece for group in groups for piece in group]
    for at in range(3):
        columns = slice(at * width, (at + 1) * width)
        left = jnp.concatenate(
            tokens_of(at // 2, gathered, offset, rows, slice(None), pieces)
        )
        part = nn(left, weights[:, columns]).astype(jnp.bfloat16)
        first = 0
        for out, group in zip(outs, groups):
            size = len(group) * rows
            out[:, columns] = part[first : first + size]
            first += size


def forward(groups, gathered, offset, rows, weights):
    total = weights.shape[1]
    return pl.pallas_call(
        functools.partial(forward_kernel, groups, offset, rows),
        in_specs=[VMEM] * 5,
        out_specs=[VMEM] * len(groups),
        out_shape=[
            jax.ShapeDtypeStruct((len(group) * rows, total), jnp.bfloat16) for group in groups
        ],
        compiler_params=params(),
        cost_estimate=cheap(),
        name="forward",
    )(*gathered, weights)


def backward_kernel(*refs):
    arrays, weights, outs = refs[:5], refs[5], refs[6:]
    total = weights.shape[1]
    width = total // 3
    rows = arrays[3].shape[0]
    for which, columns in enumerate((slice(2 * width, total), slice(0, 2 * width))):
        left = jnp.concatenate(values_of(arrays, columns))
        part = nt(left, weights[:, columns]).astype(jnp.bfloat16)
        for at, (dz, half) in enumerate(GATHERED):
            outs[2 * half + which][owner(dz)] = part[at * rows : (at + 1) * rows]


def backward(arrays, weights):
    rows = arrays[3].shape[0]
    depth, total = weights.shape
    outs = pl.pallas_call(
        backward_kernel,
        in_specs=[VMEM] * 6,
        out_specs=[VMEM] * 4,
        out_shape=[jax.ShapeDtypeStruct((4, rows, depth), jnp.bfloat16)] * 4,
        compiler_params=params(),
        cost_estimate=pl.CostEstimate(
            flops=16 * rows * depth * total, bytes_accessed=8 * depth * total, transcendentals=0
        ),
        name="backward",
    )(*arrays, weights)
    outs = [out.reshape(4 * rows, depth) for out in outs]
    return outs[2:], outs[:2]


def weight_grad_kernel(offsets, *refs):
    number = 9 * len(offsets)
    gate_mask, up_mask, down_mask, gate_grad, up_grad, down_grad = refs[number:]
    width, depth = down_grad.shape
    every = slice(None)

    def tokens(kind, columns):
        parts = []
        for which, offset in enumerate(offsets):
            chunk = refs[9 * which : 9 * which + 9]
            parts += tokens_of(kind, chunk[:4], offset, chunk[7].shape[0], columns, GATHERED)
        return jnp.concatenate(parts)

    def values(columns):
        parts = []
        for which in range(len(offsets)):
            parts += values_of(refs[9 * which + 4 : 9 * which + 9], columns)
        return jnp.concatenate(parts)

    def store(part, mask, row, out):
        for j in range(part.shape[1] // BLK):
            for i in range(part.shape[0] // BLK):
                block = part[i * BLK : (i + 1) * BLK, j * BLK : (j + 1) * BLK]
                keep = mask[row // BLK + i, j].astype(jnp.bfloat16)
                out[row + i * BLK : row + (i + 1) * BLK, j * BLK : (j + 1) * BLK] = (
                    block.astype(jnp.bfloat16) * keep
                )

    for row in range(0, depth, 256):
        left = tokens(0, slice(row, row + 256))
        store(tn(left, values(slice(0, width))), gate_mask, row, gate_grad)
        store(tn(left, values(slice(width, 2 * width))), up_mask, row, up_grad)
    for row in range(0, width, 256):
        size = min(256, width - row)
        left = values(slice(2 * width + row, 2 * width + row + size))
        store(tn(left, tokens(1, every)), down_mask, row, down_grad)


def weight_grads(offsets, chunks, gate_mask, up_mask, down_mask):
    depth = chunks[0][0][0].shape[-1]
    total = chunks[0][1][0].shape[-1]
    width = total // 3
    count = sum(8 * arrays[3].shape[0] for _, arrays in chunks)
    inputs = [item for gathered, arrays in chunks for item in (*gathered, *arrays)]
    return pl.pallas_call(
        functools.partial(weight_grad_kernel, offsets),
        in_specs=[VMEM] * len(inputs) + [SMEM] * 3,
        out_specs=[VMEM] * 3,
        out_shape=[
            jax.ShapeDtypeStruct((depth, width), jnp.bfloat16),
            jax.ShapeDtypeStruct((depth, width), jnp.bfloat16),
            jax.ShapeDtypeStruct((width, depth), jnp.bfloat16),
        ],
        compiler_params=params(),
        cost_estimate=pl.CostEstimate(
            flops=2 * count * depth * total, bytes_accessed=16 * depth * total, transcendentals=0
        ),
        name="weight_grads",
    )(*inputs, gate_mask, up_mask, down_mask)


def wide(array):
    return array.astype(jnp.float32)


def elementwise(totals):
    width = totals.shape[-1] // 3
    gate = totals[..., :width]
    up_part = totals[..., width : 2 * width]
    hidden_grad = totals[..., 2 * width :]
    sigmoid_gate = jax.nn.sigmoid(gate)
    activated = gate * sigmoid_gate
    hidden = activated * up_part
    gate_delta = hidden_grad * up_part * sigmoid_gate * (1.0 + gate * (1.0 - sigmoid_gate))
    up_delta = hidden_grad * activated
    return jnp.concatenate([gate_delta, up_delta, hidden], axis=-1).astype(jnp.bfloat16)


def after(value, *others):
    return lax.optimization_barrier((value, others))[0]


def chip_sum(for_own, received):
    return (wide(for_own) + wide(received)).astype(jnp.bfloat16)


class Gather:
    def __init__(self, pair):
        self.pair = pair

    def far(self, *others):
        self.pair = after(self.pair, *others)
        self.pairs = [self.pair] + [move(self.pair, dy=-dy) for dy in range(1, 4)]

    def core(self, *others):
        pairs = after(self.pairs, *others)
        own = [jnp.stack([pair[kind] for pair in pairs]) for kind in range(2)]
        self.arrays = (*own, *[move(array, dcore=1) for array in own])
        return own


class Chunk:
    def __init__(self, gather, offset, rows, weights, last):
        self.source, self.offset, self.rows = gather, offset, 2 * rows
        self.weights = weights
        self.groups = TOGETHER if last else APART

    def forward(self, *others):
        self.gathered = self.source.arrays
        gathered = after(self.gathered, *others)
        outs = []
        for groups in self.groups:
            outs += forward(groups, gathered, self.offset, self.rows, self.weights)
        self.late_up, self.late_down, self.kept = outs[2:]
        self.from_down = move(outs[0], dz=1)
        self.from_up = move(outs[1], dz=-1)
        return outs[0]

    def relay(self, *others):
        rows = self.rows
        down = after(self.from_down, *others)
        send_up = self.late_up + down[:rows]
        self.last_down = move(send_up, dz=1)
        up = after(self.from_up, send_up)
        send_down = self.late_down + up[:rows]
        self.last_up = move(send_down, dz=-1)
        self.direct = (up[rows:], down[rows:])
        return send_up, send_down

    def swap(self, *others):
        last_down, last_up = after((self.last_down, self.last_up), *others)
        rows = self.rows
        self.sums = jnp.concatenate(
            [
                wide(self.kept[:rows]) + wide(last_down) + wide(self.direct[0]),
                wide(self.kept[rows:]) + wide(last_up) + wide(self.direct[1]),
            ]
        ).astype(jnp.bfloat16)
        self.partner = move(self.sums, dxl=1)
        return self.sums

    def spread(self, *others):
        partner = after(self.partner, *others)
        self.values = elementwise(wide(self.sums) + wide(partner))
        from_down = move(self.values, dz=1)
        self.near = (move(self.values, dz=-1), from_down)
        return self.values

    def far(self, *others):
        down = after(self.near[1], *others)
        sent_up = down[: self.rows]
        up = after(self.near[0], sent_up)
        sent_down = up[self.rows :]
        self.arrays = (self.values, up, down, move(sent_up, dz=1), move(sent_down, dz=-1))
        return sent_up, sent_down

    def backward(self, *others):
        self.arrays = after(self.arrays, *others)
        self.for_other, self.for_own = backward(self.arrays, self.weights)
        return self.for_other

    def send(self, *others):
        for_other = after(self.for_other, *others)
        self.received = [move(part, dcore=1) for part in for_other]
        return for_other

    def chip(self, *others):
        received = after(self.received, *others)
        chip = jnp.concatenate(
            [wide(mine) + wide(theirs) for mine, theirs in zip(self.for_own, received)], axis=1
        ).astype(jnp.bfloat16)
        rows = self.rows
        self.parts = [chip[:rows]] + [
            move(chip[dy * rows : (dy + 1) * rows], dy=dy) for dy in range(1, 4)
        ]
        return chip

    def last(self, *others):
        total = sum(wide(part) for part in after(self.parts, *others)).astype(jnp.bfloat16)
        half = self.rows // 2
        self.result = wide(total[:half]) + wide(move(total[half:], dxh=1))
        return total


def shards(tokens, out_grad, gate_weight, up_weight, down_weight, gate_mask, up_mask, down_mask):
    depth = tokens.shape[1]
    starts = [sum(CHUNKS[:i]) for i in range(len(CHUNKS))]
    weights = mask_weights(gate_weight, up_weight, down_weight, gate_mask, up_mask, down_mask)
    gathers, chunks = [], []
    for group in GATHERS:
        first, last = starts[group[0]], starts[group[-1]] + CHUNKS[group[-1]]
        part = jnp.stack([tokens[first:last], out_grad[first:last]])
        received = move(part, dxh=1)
        slices = [slice(starts[i] - first, starts[i] - first + CHUNKS[i]) for i in group]
        gather = Gather(
            jnp.concatenate([half[:, at] for at in slices for half in (part, received)], axis=1)
        )
        gathers.append(gather)
        for i in group:
            chunks.append(Chunk(gather, 2 * (starts[i] - first), CHUNKS[i], weights, i == len(CHUNKS) - 1))
    gathers[0].far()
    before = gathers[0].core(weights, *[gather.pair for gather in gathers[1:]])
    gathers[1].far(before)
    for step in ORDER:
        name, _, which = step.partition(" ")
        if name == "core":
            before = gathers[int(which)].core(before)
        elif name == "grads":
            inputs = after([(chunk.gathered, chunk.arrays) for chunk in chunks], before)
            offsets = tuple(chunk.offset for chunk in chunks)
            grads = weight_grads(offsets, inputs, gate_mask, up_mask, down_mask)
            before = grads[0]
        else:
            before = getattr(chunks[int(which)], name)(before)
    result = jnp.concatenate([chunk.result for chunk in chunks]).astype(jnp.bfloat16)
    return (result[:, :depth], result[:, depth:], *grads)


def solution(mesh):
    in_specs = (
        P("col", "row"),
        P("col", "row"),
        P("row", "col"),
        P("row", "col"),
        P("col", "row"),
        P("row", "col"),
        P("row", "col"),
        P("col", "row"),
    )
    out_specs = (
        P("col", "row"),
        P("col", "row"),
        P("row", "col"),
        P("row", "col"),
        P("col", "row"),
    )
    return jax.shard_map(shards, mesh=mesh, in_specs=in_specs, out_specs=out_specs, check_vma=False)
```

```python
import functools

import jax
import jax.numpy as jnp
from jax import lax
from jax.experimental import pallas as pl
from jax.experimental.pallas import tpu as pltpu
from jax.sharding import PartitionSpec as P

BLK = 128
CHUNKS = (32, 32)
GATHERS = ((0,), (1,))
ORDER = (
    "forward 0",
    "relay 0",
    "core 1",
    "forward 1",
    "swap 0",
    "relay 1",
    "spread 0",
    "swap 1",
    "far 0",
    "spread 1",
    "backward 0",
    "send 0",
    "far 1",
    "chip 0",
    "backward 1",
    "send 1",
    "last 0",
    "chip 1",
    "grads",
    "last 1",
)
SEND_UP = ((2, 0), (1, 1))
SEND_DOWN = ((2, 1), (3, 0))
NEXT_UP = ((1, 0),)
NEXT_DOWN = ((3, 1),)
OWN = ((0, 0), (0, 1))
GROUPS = (SEND_UP, SEND_DOWN, NEXT_UP, NEXT_DOWN, OWN)
GATHERED = tuple((dz, half) for dz in (0, 1, 3, 2) for half in range(2))
VMEM_LIMIT = 24 * 1024 * 1024


def move(array, dy=0, dxh=0, dcore=0, dxl=0, dz=0):
    pairs = []
    for device in range(128):
        row, col = divmod(device, 16)
        x_lo, z = divmod(row, 4)
        y, x_hi, core = col // 4, col // 2 % 2, col % 2
        to_row = (x_lo + dxl) % 2 * 4 + (z + dz * (1 - 2 * core)) % 4
        to_col = ((y + dy) % 4 * 2 + (x_hi + dxh) % 2) * 2 + (core + dcore) % 2
        pairs.append((device, to_row * 16 + to_col))
    return lax.ppermute(array, ("row", "col"), pairs)


def nn(left, right):
    return lax.dot_general(
        left, right, (((1,), (0,)), ((), ())), preferred_element_type=jnp.float32
    )


def nt(left, right):
    return lax.dot_general(
        left, right, (((1,), (1,)), ((), ())), preferred_element_type=jnp.float32
    )


def tn(left, right):
    return lax.dot_general(
        left, right, (((0,), (0,)), ((), ())), preferred_element_type=jnp.float32
    )


def params():
    return pltpu.CompilerParams(vmem_limit_bytes=VMEM_LIMIT)


def cheap():
    return pl.CostEstimate(flops=1024, bytes_accessed=1024, transcendentals=0)


VMEM = pl.BlockSpec(memory_space=pltpu.VMEM)
SMEM = pl.BlockSpec(memory_space=pltpu.SMEM)


def owner(dz):
    z = lax.rem(lax.axis_index("row"), 4)
    odd = lax.rem(lax.axis_index("col"), 2)
    return lax.rem(z + dz + odd * ((4 - 2 * dz) % 4), 4)


def tokens_of(kind, gathered, offset, rows, columns):
    return [
        gathered[2 * half + kind][owner(dz), offset : offset + rows, columns]
        for dz, half in GATHERED
    ]


def values_of(arrays, columns):
    own, up, down, far_first, far_second = arrays
    return [array[:, columns] for array in (own, up, down, far_first, far_second)]


def mask_kernel(gate, up, down, gate_mask, up_mask, down_mask, out):
    step = pl.program_id(0)
    width = gate.shape[1]
    down_t = down[...].T
    for j in range(width // BLK):
        at = pl.ds(j * BLK, BLK)
        out[:, at] = gate[:, at] * gate_mask[step, j].astype(jnp.bfloat16)
        to = pl.ds(width + j * BLK, BLK)
        out[:, to] = up[:, at] * up_mask[step, j].astype(jnp.bfloat16)
        to = pl.ds(2 * width + j * BLK, BLK)
        out[:, to] = down_t[:, j * BLK : (j + 1) * BLK] * down_mask[j, step].astype(jnp.bfloat16)


def mask_weights(gate, up, down, gate_mask, up_mask, down_mask):
    depth, width = gate.shape
    return pl.pallas_call(
        mask_kernel,
        grid=(depth // BLK,),
        in_specs=[
            pl.BlockSpec((BLK, width), lambda i: (i, 0)),
            pl.BlockSpec((BLK, width), lambda i: (i, 0)),
            pl.BlockSpec((width, BLK), lambda i: (0, i)),
            SMEM,
            SMEM,
            SMEM,
        ],
        out_specs=pl.BlockSpec((BLK, 3 * width), lambda i: (i, 0)),
        out_shape=jax.ShapeDtypeStruct((depth, 3 * width), jnp.bfloat16),
        compiler_params=params(),
        cost_estimate=pl.CostEstimate(
            flops=3 * depth * width, bytes_accessed=12 * depth * width, transcendentals=0
        ),
        name="mask_weights",
    )(gate, up, down, gate_mask, up_mask, down_mask)


def forward_kernel(offset, rows, *refs):
    gathered, weights, outs = refs[:4], refs[4], refs[5:]
    width = weights.shape[1] // 3
    every = slice(None)
    for at in range(3):
        columns = slice(at * width, (at + 1) * width)
        left = jnp.concatenate(tokens_of(at // 2, gathered, offset, rows, every))
        part = nn(left, weights[:, columns]).astype(jnp.bfloat16)
        for number, piece in enumerate(GATHERED):
            for out, group in zip(outs, GROUPS):
                if piece in group:
                    first = group.index(piece) * rows
                    out[first : first + rows, columns] = part[number * rows : (number + 1) * rows]


def forward(gathered, offset, rows, weights):
    total = weights.shape[1]
    return pl.pallas_call(
        functools.partial(forward_kernel, offset, rows),
        in_specs=[VMEM] * 5,
        out_specs=[VMEM] * len(GROUPS),
        out_shape=[
            jax.ShapeDtypeStruct((len(group) * rows, total), jnp.bfloat16) for group in GROUPS
        ],
        compiler_params=params(),
        cost_estimate=cheap(),
        name="forward",
    )(*gathered, weights)


def backward_kernel(*refs):
    arrays, weights, outs = refs[:5], refs[5], refs[6:]
    total = weights.shape[1]
    width = total // 3
    rows = arrays[3].shape[0]
    for which, columns in enumerate((slice(2 * width, total), slice(0, 2 * width))):
        left = jnp.concatenate(values_of(arrays, columns))
        part = nt(left, weights[:, columns]).astype(jnp.bfloat16)
        for at, (dz, half) in enumerate(GATHERED):
            outs[2 * half + which][owner(dz)] = part[at * rows : (at + 1) * rows]


def backward(arrays, weights):
    rows = arrays[3].shape[0]
    depth, total = weights.shape
    outs = pl.pallas_call(
        backward_kernel,
        in_specs=[VMEM] * 6,
        out_specs=[VMEM] * 4,
        out_shape=[jax.ShapeDtypeStruct((4, rows, depth), jnp.bfloat16)] * 4,
        compiler_params=params(),
        cost_estimate=pl.CostEstimate(
            flops=16 * rows * depth * total, bytes_accessed=8 * depth * total, transcendentals=0
        ),
        name="backward",
    )(*arrays, weights)
    outs = [out.reshape(4 * rows, depth) for out in outs]
    return outs[2:], outs[:2]


def weight_grad_kernel(offsets, *refs):
    number = 9 * len(offsets)
    gate_mask, up_mask, down_mask, gate_grad, up_grad, down_grad = refs[number:]
    width, depth = down_grad.shape
    every = slice(None)

    def tokens(kind, columns):
        parts = []
        for which, offset in enumerate(offsets):
            chunk = refs[9 * which : 9 * which + 9]
            parts += tokens_of(kind, chunk[:4], offset, chunk[7].shape[0], columns)
        return jnp.concatenate(parts)

    def values(columns):
        parts = []
        for which in range(len(offsets)):
            parts += values_of(refs[9 * which + 4 : 9 * which + 9], columns)
        return jnp.concatenate(parts)

    def store(part, mask, row, out):
        for j in range(part.shape[1] // BLK):
            for i in range(part.shape[0] // BLK):
                block = part[i * BLK : (i + 1) * BLK, j * BLK : (j + 1) * BLK]
                keep = mask[row // BLK + i, j].astype(jnp.bfloat16)
                out[row + i * BLK : row + (i + 1) * BLK, j * BLK : (j + 1) * BLK] = (
                    block.astype(jnp.bfloat16) * keep
                )

    for row in range(0, depth, 256):
        left = tokens(0, slice(row, row + 256))
        store(tn(left, values(slice(0, width))), gate_mask, row, gate_grad)
        store(tn(left, values(slice(width, 2 * width))), up_mask, row, up_grad)
    for row in range(0, width, 256):
        size = min(256, width - row)
        left = values(slice(2 * width + row, 2 * width + row + size))
        store(tn(left, tokens(1, every)), down_mask, row, down_grad)


def weight_grads(offsets, chunks, gate_mask, up_mask, down_mask):
    depth = chunks[0][0][0].shape[-1]
    total = chunks[0][1][0].shape[-1]
    width = total // 3
    count = sum(8 * arrays[3].shape[0] for _, arrays in chunks)
    inputs = [item for gathered, arrays in chunks for item in (*gathered, *arrays)]
    return pl.pallas_call(
        functools.partial(weight_grad_kernel, offsets),
        in_specs=[VMEM] * len(inputs) + [SMEM] * 3,
        out_specs=[VMEM] * 3,
        out_shape=[
            jax.ShapeDtypeStruct((depth, width), jnp.bfloat16),
            jax.ShapeDtypeStruct((depth, width), jnp.bfloat16),
            jax.ShapeDtypeStruct((width, depth), jnp.bfloat16),
        ],
        compiler_params=params(),
        cost_estimate=pl.CostEstimate(
            flops=2 * count * depth * total, bytes_accessed=16 * depth * total, transcendentals=0
        ),
        name="weight_grads",
    )(*inputs, gate_mask, up_mask, down_mask)


def wide(array):
    return array.astype(jnp.float32)


def elementwise(totals):
    width = totals.shape[-1] // 3
    gate = totals[..., :width]
    up_part = totals[..., width : 2 * width]
    hidden_grad = totals[..., 2 * width :]
    sigmoid_gate = jax.nn.sigmoid(gate)
    activated = gate * sigmoid_gate
    hidden = activated * up_part
    gate_delta = hidden_grad * up_part * sigmoid_gate * (1.0 + gate * (1.0 - sigmoid_gate))
    up_delta = hidden_grad * activated
    return jnp.concatenate([gate_delta, up_delta, hidden], axis=-1).astype(jnp.bfloat16)


def after(value, *others):
    return lax.optimization_barrier((value, others))[0]


def chip_sum(for_own, received):
    return (wide(for_own) + wide(received)).astype(jnp.bfloat16)


class Gather:
    def __init__(self, part, slices, direct):
        self.part, self.slices, self.direct = part, slices, direct
        if not direct:
            self.near = self.join(part, move(part, dxh=1))

    def join(self, *halves):
        return jnp.concatenate([half[:, at] for at in self.slices for half in halves], axis=1)

    def far(self, *others):
        if self.direct:
            part = after(self.part, *others)
            self.parts = [
                [move(part, dy=-dy, dxh=dx) if dy or dx else part for dx in range(2)]
                for dy in range(4)
            ]
        else:
            near = after(self.near, *others)
            self.parts = [[near]] + [[move(near, dy=-dy)] for dy in range(1, 4)]

    def core(self, *others):
        parts = after(self.parts, *others)
        pairs = [self.join(*part) if self.direct else part[0] for part in parts]
        own = [jnp.stack([pair[kind] for pair in pairs]) for kind in range(2)]
        self.arrays = (*own, *[move(array, dcore=1) for array in own])
        return own


class Chunk:
    def __init__(self, gather, offset, rows, weights):
        self.source, self.offset, self.rows = gather, offset, 2 * rows
        self.weights = weights

    def forward(self, *others):
        self.gathered = self.source.arrays
        gathered = after(self.gathered, *others)
        outs = forward(gathered, self.offset, self.rows, self.weights)
        self.late_up, self.late_down, self.kept = outs[2:]
        self.from_down = move(outs[0], dz=1)
        self.from_up = move(outs[1], dz=-1)
        return outs[0]

    def relay(self, *others):
        rows = self.rows
        down = after(self.from_down, *others)
        send_up = self.late_up + down[:rows]
        self.last_down = move(send_up, dz=1)
        up = after(self.from_up, send_up)
        send_down = self.late_down + up[:rows]
        self.last_up = move(send_down, dz=-1)
        self.direct = (up[rows:], down[rows:])
        return send_up, send_down

    def swap(self, *others):
        last_down, last_up = after((self.last_down, self.last_up), *others)
        rows = self.rows
        self.sums = jnp.concatenate(
            [
                wide(self.kept[:rows]) + wide(last_down) + wide(self.direct[0]),
                wide(self.kept[rows:]) + wide(last_up) + wide(self.direct[1]),
            ]
        ).astype(jnp.bfloat16)
        self.partner = move(self.sums, dxl=1)
        return self.sums

    def spread(self, *others):
        partner = after(self.partner, *others)
        self.values = elementwise(wide(self.sums) + wide(partner))
        from_down = move(self.values, dz=1)
        self.near = (move(self.values, dz=-1), from_down)
        return self.values

    def far(self, *others):
        down = after(self.near[1], *others)
        sent_up = down[: self.rows]
        up = after(self.near[0], sent_up)
        sent_down = up[self.rows :]
        self.arrays = (self.values, up, down, move(sent_up, dz=1), move(sent_down, dz=-1))
        return sent_up, sent_down

    def backward(self, *others):
        self.arrays = after(self.arrays, *others)
        self.for_other, self.for_own = backward(self.arrays, self.weights)
        return self.for_other

    def send(self, *others):
        for_other = after(self.for_other, *others)
        self.received = [move(part, dcore=1) for part in for_other]
        return for_other

    def chip(self, *others):
        received = after(self.received, *others)
        chip = jnp.concatenate(
            [wide(mine) + wide(theirs) for mine, theirs in zip(self.for_own, received)], axis=1
        ).astype(jnp.bfloat16)
        rows = self.rows
        self.parts = [chip[:rows]] + [
            move(chip[dy * rows : (dy + 1) * rows], dy=dy) for dy in range(1, 4)
        ]
        return chip

    def last(self, *others):
        total = sum(wide(part) for part in after(self.parts, *others)).astype(jnp.bfloat16)
        half = self.rows // 2
        self.result = wide(total[:half]) + wide(move(total[half:], dxh=1))
        return total


def shards(tokens, out_grad, gate_weight, up_weight, down_weight, gate_mask, up_mask, down_mask):
    depth = tokens.shape[1]
    starts = [sum(CHUNKS[:i]) for i in range(len(CHUNKS))]
    weights = mask_weights(gate_weight, up_weight, down_weight, gate_mask, up_mask, down_mask)
    gathers, chunks = [], []
    for group in GATHERS:
        first, last = starts[group[0]], starts[group[-1]] + CHUNKS[group[-1]]
        part = jnp.stack([tokens[first:last], out_grad[first:last]])
        slices = [slice(starts[i] - first, starts[i] - first + CHUNKS[i]) for i in group]
        gather = Gather(part, slices, not gathers)
        gathers.append(gather)
        for i in group:
            chunks.append(Chunk(gather, 2 * (starts[i] - first), CHUNKS[i], weights))
    gathers[0].far()
    before = gathers[0].core(weights, *[gather.near for gather in gathers[1:]])
    gathers[1].far(before)
    for step in ORDER:
        name, _, which = step.partition(" ")
        if name == "core":
            before = gathers[int(which)].core(before)
        elif name == "grads":
            inputs = after([(chunk.gathered, chunk.arrays) for chunk in chunks], before)
            offsets = tuple(chunk.offset for chunk in chunks)
            grads = weight_grads(offsets, inputs, gate_mask, up_mask, down_mask)
            before = grads[0]
        else:
            before = getattr(chunks[int(which)], name)(before)
    result = jnp.concatenate([chunk.result for chunk in chunks]).astype(jnp.bfloat16)
    return (result[:, :depth], result[:, depth:], *grads)


def solution(mesh):
    in_specs = (
        P("col", "row"),
        P("col", "row"),
        P("row", "col"),
        P("row", "col"),
        P("col", "row"),
        P("row", "col"),
        P("row", "col"),
        P("col", "row"),
    )
    out_specs = (
        P("col", "row"),
        P("col", "row"),
        P("row", "col"),
        P("row", "col"),
        P("col", "row"),
    )
    return jax.shard_map(shards, mesh=mesh, in_specs=in_specs, out_specs=out_specs, check_vma=False)
```
